32 devices in a mesh: seq: 4 (over x, core), dp: 8 (over z, y).
Axes of the slice: x: 2, y: 2, z: 4, core: 2. Of those that a mesh axis runs over, the one named last changes fastest.
Arguments:
- tokens: bfloat16 [8, 512, 768], P('dp', 'seq'), may hold values from -6 to 6
- memory: bfloat16 [8, 1024, 768], P('dp', 'seq'), may hold values from -6 to 6
- target_segments: int32 [8, 512], P('dp'), may hold values from 0 to 254, as said below
- memory_segments: int32 [8, 1024], P('dp'), may hold values from 0 to 254, as said below
- pad_counts: int32 [8, 2], P('dp'), may hold values from 0 to 252, as said below
- out_grad: bfloat16 [8, 512, 768], P('dp', 'seq'), may hold values from -6 to 6
- self_query: bfloat16 [768, 768], replicated, may hold values from -0.21875 to 0.21875
- self_key: bfloat16 [768, 768], replicated, may hold values from -0.21875 to 0.21875
- self_value: bfloat16 [768, 768], replicated, may hold values from -0.21875 to 0.21875
- self_out: bfloat16 [768, 768], replicated, may hold values from -0.875 to 0.875
- cross_query: bfloat16 [768, 768], replicated, may hold values from -0.21875 to 0.21875
- cross_key: bfloat16 [768, 768], replicated, may hold values from -0.21875 to 0.21875
- cross_value: bfloat16 [768, 768], replicated, may hold values from -0.21875 to 0.21875
- cross_out: bfloat16 [768, 768], replicated, may hold values from -0.875 to 0.875
- feed_in: bfloat16 [768, 3072], replicated, may hold values from -0.21875 to 0.21875
- feed_out: bfloat16 [3072, 768], replicated, may hold values from -0.109375 to 0.109375
- gain_attend: bfloat16 [768], replicated, may hold values from 0.099609375 to 1.8984375
- shift_attend: bfloat16 [768], replicated, may hold values from -3 to 3
- gain_cross: bfloat16 [768], replicated, may hold values from 0.099609375 to 1.8984375
- shift_cross: bfloat16 [768], replicated, may hold values from -3 to 3
- gain_feed: bfloat16 [768], replicated, may hold values from 0.099609375 to 1.8984375
- shift_feed: bfloat16 [768], replicated, may hold values from -3 to 3
Outputs:
- layer_out: float32 [8, 512, 768], P('dp', 'seq')
- tokens_grad: float32 [8, 512, 768], P('dp', 'seq')
- memory_grad: float32 [8, 1024, 768], P('dp', 'seq')
- grad_self_query: float32 [768, 768], P('dp')
- grad_self_key: float32 [768, 768], P('dp')
- grad_self_value: float32 [768, 768], P('dp')
- grad_self_out: float32 [768, 768], P('dp')
- grad_cross_query: float32 [768, 768], P('dp')
- grad_cross_key: float32 [768, 768], P('dp')
- grad_cross_value: float32 [768, 768], P('dp')
- grad_cross_out: float32 [768, 768], P('dp')
- grad_feed_in: float32 [768, 3072], P('dp')
- grad_feed_out: float32 [3072, 768], P('dp')
- grad_gain_attend: float32 [768], P('dp')
- grad_shift_attend: float32 [768], P('dp')
- grad_gain_cross: float32 [768], P('dp')
- grad_shift_cross: float32 [768], P('dp')
- grad_gain_feed: float32 [768], P('dp')
- grad_shift_feed: float32 [768], P('dp')
The draws below stay inside these ranges and needn't reach their ends.
Inputs may be any that keep to these rules, and one draw needn't show every extreme that they name: `target_segments`: in each row ids start at 0, never fall, and rise by at most one from one position to the next; the padded tail of a row continues its last document. `memory_segments`: in each row ids start at 0, never fall and rise by at most one from one position to the next; the unpadded memory of a row holds each id of the row's targets, every one of them, and no other. `pad_counts`: column 0 counts padded target positions, column 1 padded memory positions; the memory of a row's last document is never wholly padded; some row has no padding.
All inputs are finite; a program needn't handle non-finite values.
Results may differ from the reference program's by a relative error of at most 0.018.
Values may be sent and summed in bfloat16 or wider, within the bound.
A program may use at most 192 MiB of HBM per device.

```python
import jax
import jax.numpy as jnp
from jax import lax

D = 768
HEADS = 12
HEAD_DIM = 64
FF = 3072
TGT_LEN = 512
SPAN = 128
SRC_LEN = 1024
ROWS = 8


def draw_row(key, complete, padded):
    row_keys = jax.random.split(key, 6)
    first_cut = jax.random.randint(row_keys[0], (), 1, SPAN)
    first_cut = jnp.where(complete, SPAN - 1, first_cut)
    second_cut = jax.random.randint(row_keys[1], (), TGT_LEN - SPAN + 1, TGT_LEN - SPAN // 2 + 1)
    second_cut = jnp.where(complete | padded, TGT_LEN - SPAN + 1, second_cut)
    target_valid = jax.random.randint(row_keys[2], (), second_cut + 1, TGT_LEN + 1)
    target_valid = jnp.where(complete, TGT_LEN, jnp.where(padded, second_cut + 1, target_valid))
    places = jnp.arange(TGT_LEN)
    sparse = (jax.random.randint(row_keys[3], (TGT_LEN,), 0, 12) == 0) | complete
    inside = (places > 0) & (places < first_cut) | (places > second_cut) & (places < target_valid)
    cuts = ((places == first_cut) | (places == second_cut) | sparse & inside).astype(jnp.int32)
    target_ids = jnp.cumsum(cuts).astype(jnp.int32)
    jitter = jax.random.randint(row_keys[4], (TGT_LEN,), 0, 2)
    memory_cuts = jnp.zeros((SRC_LEN,), jnp.int32).at[2 * places + jitter].add(cuts)
    memory_ids = jnp.cumsum(memory_cuts).astype(jnp.int32)
    last_cut = jnp.max(places * cuts)
    trimmed = jnp.where(complete, 0, jnp.where(padded, 3, jax.random.randint(row_keys[5], (), 0, 4)))
    memory_valid = jnp.maximum(2 * target_valid - trimmed, 2 * last_cut + 2)
    padding = jnp.stack([TGT_LEN - target_valid, SRC_LEN - memory_valid]).astype(jnp.int32)
    return (target_ids, memory_ids, padding)


def layout(key):
    row_keys = jax.random.split(key, ROWS)
    complete_row = jax.random.randint(jax.random.fold_in(key, 7), (), 0, ROWS)
    padded_row = (complete_row + 1) % ROWS
    rows_index = jnp.arange(ROWS)
    return jax.vmap(draw_row)(row_keys, rows_index == complete_row, rows_index == padded_row)


def draw_target_segments(key, part):
    shared = layout(key)
    return shared[0]


def draw_memory_segments(key, part):
    shared = layout(key)
    return shared[1]


def draw_pad_counts(key, part):
    shared = layout(key)
    return shared[2]


def steps_of(own_key, shape, cuts, smallest, largest):
    level, own = 1.0, jax.random.fold_in(own_key, 6)
    for axis_at, blocks in cuts:
        heights = jnp.exp(jax.random.uniform(jax.random.fold_in(own, axis_at), (blocks,), jnp.float32, smallest / len(cuts), largest / len(cuts)))
        level = level * jnp.repeat(heights, shape[axis_at] // blocks).reshape([-1 if axis == axis_at else 1 for axis in range(len(shape))])
    return level


def noise(key, shape, deviation, bound, cuts=(), dtype=jnp.bfloat16):
    drawn = deviation * jax.random.normal(key, shape, jnp.float32)
    if cuts:
        drawn = drawn * steps_of(key, shape, cuts, -0.22, 0.18)
    return jnp.clip(drawn, -bound, bound).astype(dtype)


def setup_inputs(seed: int = 0) -> dict:
    seeds = jax.random.split(jax.random.key(seed), 23)
    return {
        "tokens": noise(seeds[0], (ROWS, TGT_LEN, D), 1.0, 6.0, ((0, 8), (1, 4))),
        "memory": noise(seeds[1], (ROWS, SRC_LEN, D), 1.0, 6.0, ((0, 8), (1, 4))),
        "target_segments": draw_target_segments(jax.random.fold_in(seeds[22], 71), 0),
        "memory_segments": draw_memory_segments(jax.random.fold_in(seeds[22], 71), 0),
        "pad_counts": draw_pad_counts(jax.random.fold_in(seeds[22], 71), 0),
        "out_grad": noise(seeds[5], (ROWS, TGT_LEN, D), 1.0, 6.0, ((0, 8), (1, 4))),
        "self_query": noise(seeds[6], (D, D), D ** -0.5, 0.21875),
        "self_key": noise(seeds[7], (D, D), D ** -0.5, 0.21875),
        "self_value": noise(seeds[8], (D, D), D ** -0.5, 0.21875),
        "self_out": noise(seeds[9], (D, D), (D // 16) ** -0.5, 0.875),
        "cross_query": noise(seeds[10], (D, D), D ** -0.5, 0.21875),
        "cross_key": noise(seeds[11], (D, D), D ** -0.5, 0.21875),
        "cross_value": noise(seeds[12], (D, D), D ** -0.5, 0.21875),
        "cross_out": noise(seeds[13], (D, D), (D // 16) ** -0.5, 0.875),
        "feed_in": noise(seeds[14], (D, FF), D ** -0.5, 0.21875),
        "feed_out": noise(seeds[15], (FF, D), FF ** -0.5, 0.109375),
        "gain_attend": jnp.clip(1.0 + 0.18 * jax.random.normal(seeds[16], (D,), jnp.float32), 0.099609375, 1.8984375).astype(jnp.bfloat16),
        "shift_attend": noise(seeds[17], (D,), 0.5, 3.0),
        "gain_cross": jnp.clip(1.0 + 0.18 * jax.random.normal(seeds[18], (D,), jnp.float32), 0.099609375, 1.8984375).astype(jnp.bfloat16),
        "shift_cross": noise(seeds[19], (D,), 0.5, 3.0),
        "gain_feed": jnp.clip(1.0 + 0.18 * jax.random.normal(seeds[20], (D,), jnp.float32), 0.099609375, 1.8984375).astype(jnp.bfloat16),
        "shift_feed": noise(seeds[21], (D,), 0.5, 3.0),
    }


@jax.custom_vjp
def low(v):
    return lax.optimization_barrier(v.astype(jnp.bfloat16)).astype(jnp.float32)

@jax.custom_vjp
def low_back(v):
    return v

def low_keep(v):
    return (low(v), None)

def low_pass(kept, grad):
    return (grad,)

def back_keep(v):
    return (v, None)

def back_low(kept, grad):
    return (low(grad),)
low.defvjp(low_keep, low_pass)
low_back.defvjp(back_keep, back_low)
EPSILON = 1e-05
NEGATIVE = -1e+30
HIGHEST = lax.Precision.HIGHEST

def matmul(left_side, right_side):
    return jnp.dot(left_side, right_side, precision=HIGHEST)

def layer_norm(values, gain_vec, shift_vec):
    row_mean = lax.optimization_barrier(jnp.mean(values, axis=-1, keepdims=True))
    centered = values - row_mean
    spread = lax.optimization_barrier(jnp.mean(centered * centered, axis=-1, keepdims=True))
    return centered * lax.rsqrt(spread + EPSILON) * gain_vec + shift_vec

def attend(queries, keys_in, values_in, allowed):
    head_query = queries.reshape(queries.shape[0], HEADS, HEAD_DIM)
    head_key = keys_in.reshape(keys_in.shape[0], HEADS, HEAD_DIM)
    head_value = values_in.reshape(values_in.shape[0], HEADS, HEAD_DIM)
    scores = jnp.einsum('qhd,khd->hqk', head_query, head_key, precision=HIGHEST) * HEAD_DIM ** (-0.5)
    scores = jnp.where(allowed[None], low_back(scores), NEGATIVE)
    weights = low(jax.nn.softmax(scores, axis=-1))
    mixture = jnp.einsum('hqk,khd->qhd', weights, head_value, precision=HIGHEST)
    return low_back(low(mixture.reshape(queries.shape[0], HEADS * HEAD_DIM)))

def row_forward(params, row_tokens, row_memory, target_ids, memory_ids, row_pads):
    self_query, self_key, self_value, self_out, cross_query, cross_key, cross_value, cross_out, feed_in, feed_out, gain_attend, shift_attend, gain_cross, shift_cross, gain_feed, shift_feed = params
    places = jnp.arange(TGT_LEN)
    sources = jnp.arange(SRC_LEN)
    target_valid = TGT_LEN - row_pads[0]
    memory_valid = SRC_LEN - row_pads[1]
    diagonal = places[None, :] == places[:, None]
    self_allowed = (places[None, :] <= places[:, None]) & (target_ids[None, :] == target_ids[:, None]) & ((places[None, :] < target_valid) | diagonal)
    cross_allowed = (memory_ids[None, :] == target_ids[:, None]) & (sources[None, :] < memory_valid)
    hidden_attend = low(layer_norm(row_tokens, gain_attend, shift_attend))
    queries = low_back(low(matmul(hidden_attend, self_query)))
    keys_all = low_back(low(matmul(hidden_attend, self_key)))
    values_all = low_back(low(matmul(hidden_attend, self_value)))
    after_self = row_tokens + low_back(matmul(attend(queries, keys_all, values_all, self_allowed), self_out))
    hidden_cross = low(layer_norm(after_self, gain_cross, shift_cross))
    cross_rows = low_back(low(matmul(hidden_cross, cross_query)))
    memory_keys = low_back(low(matmul(row_memory, cross_key)))
    memory_values = low_back(low(matmul(row_memory, cross_value)))
    after_cross = after_self + low_back(matmul(attend(cross_rows, memory_keys, memory_values, cross_allowed), cross_out))
    hidden_feed = low(layer_norm(after_cross, gain_feed, shift_feed))
    upward = low_back(matmul(hidden_feed, feed_in))
    activated = low(jax.nn.gelu(upward, approximate=False))
    return after_cross + low_back(matmul(activated, feed_out))

def add_grads(first_tree, second_tree):
    return jax.tree.map(jnp.add, first_tree, second_tree)

def reference(tokens, memory, target_segments, memory_segments, pad_counts, out_grad, self_query, self_key, self_value, self_out, cross_query, cross_key, cross_value, cross_out, feed_in, feed_out, gain_attend, shift_attend, gain_cross, shift_cross, gain_feed, shift_feed):
    params = tuple((weight.astype(jnp.float32) for weight in (self_query, self_key, self_value, self_out, cross_query, cross_key, cross_value, cross_out, feed_in, feed_out, gain_attend, shift_attend, gain_cross, shift_cross, gain_feed, shift_feed)))

    def row_step(totals, row_data):
        row_tokens, row_memory, target_ids, memory_ids, row_pads, row_cotangent = row_data

        def forward(param_list, tokens_in, memory_in):
            return row_forward(param_list, tokens_in, memory_in, target_ids, memory_ids, row_pads)
        result, pullback = jax.vjp(forward, params, row_tokens.astype(jnp.float32), row_memory.astype(jnp.float32))
        param_grads, tokens_back, memory_back = pullback(row_cotangent.astype(jnp.float32))
        return (add_grads(totals, param_grads), (result, tokens_back, memory_back))
    zero_grads = tuple((jnp.zeros_like(weight) for weight in params))
    totals, (layer_out, tokens_grad, memory_grad) = lax.scan(row_step, zero_grads, (tokens, memory, target_segments, memory_segments, pad_counts, out_grad))
    return (layer_out, tokens_grad, memory_grad, totals[0], totals[1], totals[2], totals[3], totals[4], totals[5], totals[6], totals[7], totals[8], totals[9], totals[10], totals[11], totals[12], totals[13], totals[14], totals[15])
```

```python
import jax
import jax.numpy as jnp
from jax import lax
from jax.sharding import PartitionSpec as P

HEAD_DIM = 64
EPSILON = 1e-05
NEGATIVE = -1e30
F32 = jnp.float32
BF16 = jnp.bfloat16


def normalize(values):
    centered = values - jnp.mean(values, axis=-1, keepdims=True)
    rate = lax.rsqrt(jnp.mean(centered * centered, axis=-1, keepdims=True) + EPSILON)
    return centered * rate, rate


def norm_back(grad, gain, normed, rate):
    scaled = grad * gain
    inner = jnp.mean(scaled * normed, axis=-1, keepdims=True)
    return rate * (scaled - jnp.mean(scaled, axis=-1, keepdims=True) - normed * inner)


def mm(left, right):
    return jnp.dot(left, right, preferred_element_type=F32)


def mm_t(left, right):
    return lax.dot_general(left, right, (((1,), (1,)), ((), ())), preferred_element_type=F32)


def t_mm(left, right):
    return lax.dot_general(left, right, (((0,), (0,)), ((), ())), preferred_element_type=F32)


def heads(values):
    return values.reshape(values.shape[0], -1, HEAD_DIM)


def scores_of(query, key, allowed):
    scores = jnp.einsum("qhd,khd->hqk", query, key, preferred_element_type=F32) * HEAD_DIM**-0.5
    return jnp.where(allowed[None], scores, NEGATIVE)


def attend(query, key, value, allowed):
    scores = scores_of(heads(query), heads(key), allowed)
    highest = jnp.max(scores, axis=-1, keepdims=True)
    exponent = jnp.exp(scores - highest)
    totals = jnp.sum(exponent, axis=-1, keepdims=True)
    weights = (exponent / totals).astype(BF16)
    mixed = jnp.einsum("hqk,khd->qhd", weights, heads(value), preferred_element_type=F32)
    return mixed.reshape(query.shape).astype(BF16), highest + jnp.log(totals)


def attend_back(query, key, value, allowed, log_total, grad):
    query, key, value, grad = heads(query), heads(key), heads(value), heads(grad)
    weights = jnp.exp(scores_of(query, key, allowed) - log_total)
    grad_weights = jnp.einsum("qhd,khd->hqk", grad, value, preferred_element_type=F32)
    inner = jnp.sum(weights * grad_weights, axis=-1, keepdims=True)
    grad_scores = (weights * (grad_weights - inner)).astype(BF16)
    factor = HEAD_DIM**-0.5
    grad_query = jnp.einsum("hqk,khd->qhd", grad_scores, key, preferred_element_type=F32) * factor
    grad_key = jnp.einsum("hqk,qhd->khd", grad_scores, query, preferred_element_type=F32) * factor
    grad_value = jnp.einsum("hqk,qhd->khd", weights.astype(BF16), grad, preferred_element_type=F32)
    flat = lambda v: v.reshape(v.shape[0], -1).astype(BF16)
    return flat(grad_query), flat(grad_key), flat(grad_value)


def swap(value, axis, bit):
    size = lax.axis_size(axis)
    return lax.ppermute(value, axis, [(i, i ^ bit) for i in range(size)])


def scatter_sum(value, bits):
    index = lax.axis_index("dp")
    size = lax.axis_size("dp")
    levels = size.bit_length() - 1
    blocks = value.reshape((2,) * levels + value.shape[1:])
    left = list(range(levels))[::-1]
    for bit in bits:
        place = left.index(bit)
        mine = (index >> bit) & 1
        keep = lax.dynamic_index_in_dim(blocks, mine, place, keepdims=False)
        send = lax.dynamic_index_in_dim(blocks, 1 - mine, place, keepdims=False)
        left.pop(place)
        got = swap(send.astype(BF16), "dp", 1 << bit)
        blocks = keep.astype(F32) + got.astype(F32)
    return blocks


def shards(
    tokens,
    memory,
    target_segments,
    memory_segments,
    pad_counts,
    out_grad,
    self_query,
    self_key,
    self_value,
    self_out,
    cross_query,
    cross_key,
    cross_value,
    cross_out,
    feed_in,
    feed_out,
    gain_attend,
    shift_attend,
    gain_cross,
    shift_cross,
    gain_feed,
    shift_feed,
):
    seq, dp = lax.axis_size("seq"), lax.axis_size("dp")
    me = lax.axis_index("seq")
    span, width = tokens.shape[1:]
    full, src_full = span * seq, memory.shape[1] * seq
    part = width // seq
    feed = feed_in.shape[1]
    unit = feed // dp // seq

    def columns(weight):
        return lax.dynamic_slice_in_dim(weight, me * part, part, 1)

    def rows(weight):
        return lax.dynamic_slice_in_dim(weight, me * part, part, 0)

    def own(values):
        return lax.dynamic_slice_in_dim(values, me * span, span, 0)

    fi = lax.dynamic_index_in_dim(
        feed_in.reshape(width, dp, seq, unit), me, 2, keepdims=False
    ).reshape(width, dp * unit)
    fo = lax.dynamic_index_in_dim(
        feed_out.reshape(dp, seq, unit, width), me, 1, keepdims=False
    ).reshape(dp * unit, width)

    gather = lambda v, axis: lax.all_gather(v, "seq", axis=axis, tiled=True)
    scatter = lambda v: lax.psum_scatter(
        v.astype(BF16), "seq", scatter_dimension=0, tiled=True
    ).astype(F32)

    target_ids, memory_ids = target_segments[0], memory_segments[0]
    places = jnp.arange(full)
    same = target_ids[None, :] == target_ids[:, None]
    alive = (places < full - pad_counts[0, 0])[None, :] | (places[None, :] == places[:, None])
    self_mask = same & (places[None, :] <= places[:, None]) & alive
    cross_mask = (memory_ids[None, :] == target_ids[:, None]) & (
        jnp.arange(src_full) < src_full - pad_counts[0, 1]
    )[None, :]

    row = gather(tokens[0], 0).astype(F32)
    source = gather(memory[0], 0)
    grad_out = gather(out_grad[0], 0)

    gains = [g.astype(F32) for g in (gain_attend, gain_cross, gain_feed)]
    shifts = [g.astype(F32) for g in (shift_attend, shift_cross, shift_feed)]

    n_attend, r_attend = normalize(row)
    h_attend = (n_attend * gains[0] + shifts[0]).astype(BF16)
    query = mm(h_attend, columns(self_query)).astype(BF16)
    key = mm(h_attend, columns(self_key)).astype(BF16)
    value = mm(h_attend, columns(self_value)).astype(BF16)
    mixed_own, self_total = attend(query, key, value, self_mask)
    self_mixed = gather(mixed_own, 1)
    after_self = row + mm(self_mixed, self_out)
    n_cross, r_cross = normalize(after_self)
    h_cross = (n_cross * gains[1] + shifts[1]).astype(BF16)
    cross_rows = mm(h_cross, columns(cross_query)).astype(BF16)
    mem_keys = mm(source, columns(cross_key)).astype(BF16)
    mem_values = mm(source, columns(cross_value)).astype(BF16)
    cross_own, cross_total = attend(cross_rows, mem_keys, mem_values, cross_mask)
    cross_mixed = gather(cross_own, 1)
    after_cross = after_self + mm(cross_mixed, cross_out)
    n_feed, r_feed = normalize(after_cross)
    h_feed = (n_feed * gains[2] + shifts[2]).astype(BF16)
    upward = mm(h_feed, fi)
    activated, pull_gelu = jax.vjp(lambda v: jax.nn.gelu(v, approximate=False), upward)
    activated = activated.astype(BF16)
    layer_out = own(after_cross) + scatter(mm(activated, fo))

    grad_upward = pull_gelu(mm_t(grad_out, fo))[0].astype(BF16)
    grad_fo = t_mm(activated, grad_out)
    grad_fi = t_mm(h_feed, grad_upward)
    grad_h = gather(scatter(mm_t(grad_upward, fi)).astype(BF16), 0).astype(F32)
    stats = [None] * 6
    stats[4], stats[5] = jnp.sum(grad_h * n_feed, 0), jnp.sum(grad_h, 0)
    grad_after_cross = grad_out.astype(F32) + norm_back(grad_h, gains[2], n_feed, r_feed)
    gac = grad_after_cross.astype(BF16)
    grad_co = t_mm(cross_mixed, columns(gac))
    grad_cm = mm_t(gac, rows(cross_out)).astype(BF16)
    grad_cr, grad_mk, grad_mv = attend_back(
        cross_rows, mem_keys, mem_values, cross_mask, cross_total, grad_cm
    )
    grad_ck, grad_cv = t_mm(source, grad_mk), t_mm(source, grad_mv)
    memory_grad = scatter(mm_t(grad_mk, columns(cross_key)) + mm_t(grad_mv, columns(cross_value)))
    grad_cq = t_mm(h_cross, grad_cr)
    grad_h = mm_t(gather(grad_cr, 1), cross_query)
    stats[2], stats[3] = jnp.sum(grad_h * n_cross, 0), jnp.sum(grad_h, 0)
    grad_after_self = grad_after_cross + norm_back(grad_h, gains[1], n_cross, r_cross)
    gas = grad_after_self.astype(BF16)
    grad_so = t_mm(self_mixed, columns(gas))
    grad_sm = mm_t(gas, rows(self_out)).astype(BF16)
    grad_q, grad_k, grad_v = attend_back(query, key, value, self_mask, self_total, grad_sm)
    grad_h = scatter(
        mm_t(grad_q, columns(self_query))
        + mm_t(grad_k, columns(self_key))
        + mm_t(grad_v, columns(self_value))
    )
    grad_sq, grad_sk, grad_sv = (t_mm(h_attend, g) for g in (grad_q, grad_k, grad_v))
    n_own = own(n_attend)
    stats[0], stats[1] = jnp.sum(grad_h * n_own, 0), jnp.sum(grad_h, 0)
    tokens_grad = own(grad_after_self) + norm_back(grad_h, gains[0], n_own, own(r_attend))

    levels = dp.bit_length() - 1
    up = list(range(levels))
    first, second = up, up[1:] + up[:1]
    share = width // dp
    split = lambda v: v.reshape(dp, share, -1)
    groups = (
        (split(grad_fo), first),
        (split(grad_fi), second),
        (split(jnp.concatenate([grad_co, grad_ck, grad_cv, grad_cq], 1)), first),
        (split(jnp.concatenate([grad_so, grad_sq, grad_sk, grad_sv], 1)), second),
    )
    summed = [gather(scatter_sum(v, bits).astype(BF16)[None], 0) for v, bits in groups]
    whole_fo = summed[0].reshape(seq * share, width).astype(F32)
    whole_fi = (
        summed[1].reshape(seq, share, dp, unit).transpose(1, 2, 0, 3).reshape(share, feed)
    ).astype(F32)

    def whole(group, at):
        block = group[:, :, at * part : (at + 1) * part]
        return block.transpose(1, 0, 2).reshape(share, width).astype(F32)

    co, ck, cv, cq = (whole(summed[2], at) for at in range(4))
    so, sq, sk, sv = (whole(summed[3], at) for at in range(4))

    shared = (me == 0).astype(F32)
    stats = jnp.stack(stats[:2] + [v * shared for v in stats[2:]])
    stats = lax.psum(stats, ("seq", "dp"))
    norm_part = lax.dynamic_slice_in_dim(stats, lax.axis_index("dp") * share, share, 1)
    return (
        layer_out[None],
        tokens_grad[None],
        memory_grad[None],
        sq,
        sk,
        sv,
        so,
        cq,
        ck,
        cv,
        co,
        whole_fi,
        whole_fo,
    ) + tuple(norm_part[i] for i in range(6))


def solution(mesh):
    rows = P("dp", "seq", None)
    in_specs = (rows, rows, P("dp", None), P("dp", None), P("dp", None), rows) + (P(),) * 16
    out_specs = (rows,) * 3 + (P("dp", None),) * 10 + (P("dp"),) * 6
    return jax.shard_map(shards, mesh=mesh, in_specs=in_specs, out_specs=out_specs, check_vma=False)
```

```python
import functools

import jax
import jax.numpy as jnp
from jax import lax
from jax.experimental import pallas as pl
from jax.experimental.pallas import tpu as pltpu
from jax.sharding import PartitionSpec as P

HEAD_DIM = 64
EPSILON = 1e-05
NEGATIVE = -1e30
F32 = jnp.float32
BF16 = jnp.bfloat16
MESH = pl.DeviceIdType.MESH
WINDOW = 256
CHUNKS = 2


def mm(left, right):
    return jnp.dot(left, right, preferred_element_type=F32)


def mm_t(left, right):
    return lax.dot_general(left, right, (((1,), (1,)), ((), ())), preferred_element_type=F32)


def t_mm(left, right):
    return lax.dot_general(left, right, (((0,), (0,)), ((), ())), preferred_element_type=F32)


def normalize(values):
    centered = values - jnp.mean(values, axis=-1, keepdims=True)
    rate = lax.rsqrt(jnp.mean(centered * centered, axis=-1, keepdims=True) + EPSILON)
    return centered * rate, rate


def norm_back(grad, gain, normed, rate):
    scaled = grad * gain
    inner = jnp.mean(scaled * normed, axis=-1, keepdims=True)
    return rate * (scaled - jnp.mean(scaled, axis=-1, keepdims=True) - normed * inner)


class Names:
    def __init__(self, names, refs):
        self.__dict__.update(zip(names, refs))


INPUTS = ["tokens", "memory", "out_grad", "target_ids", "memory_ids", "pads"]
INPUTS += ["w_sq", "w_sk", "w_sv", "w_so", "w_cq", "w_ck", "w_cv", "w_co", "w_fi", "w_fo"]
INPUTS += ["gain_a", "shift_a", "gain_c", "shift_c", "gain_f", "shift_f"]
OUTPUTS = ["o_layer", "o_tokens", "o_memory", "o_stats"]
GROUPS = ["g_fo", "g_fi", "g_cross", "g_self"]
ORDERS = ((1, 2, 0), (0, 1, 2))


def row_kernel(scratch_names, seq, direct, *refs):
    r = Names(INPUTS + OUTPUTS + (["o_sums"] if direct else GROUPS) + scratch_names, refs)
    me = lax.axis_index("seq")
    core = lax.rem(me, 2)
    chip = me // 2
    peer_c = me + 1 - 2 * core
    peer_x = lax.rem(me + 2, 4)
    span = r.tokens.shape[0]
    full, width = r.row.shape
    src_span = r.memory.shape[0]
    src_full = src_span * seq
    part = width // seq
    count = part // HEAD_DIM
    size = full // CHUNKS
    odd = core
    window = pl.ds(pl.multiple_of((me * part) // 128 * 128, 128), WINDOW)
    own_rows = pl.ds(pl.multiple_of(me * part, 64), part)
    own_span = pl.ds(pl.multiple_of(me * span, span), span)

    def pick(value):
        return jnp.where(odd == 1, value[:, 64 : 64 + part], value[:, :part])

    def place(value):
        empty = jnp.zeros((value.shape[0], WINDOW - part), value.dtype)
        return jnp.where(
            odd == 1,
            jnp.concatenate([empty, value], 1),
            jnp.concatenate([value, empty], 1),
        )

    loads = []

    def load(src, dst):
        copy = pltpu.make_async_copy(src, dst, r.load_sem.at[len(loads)])
        copy.start()
        loads.append(copy)
        return copy

    get_sq = load(r.w_sq.at[:, window], r.win_sq)
    get_sk = load(r.w_sk.at[:, window], r.win_sk)
    get_sv = load(r.w_sv.at[:, window], r.win_sv)
    get_tok = load(r.tokens, r.row.at[own_span])
    get_ck = load(r.w_ck.at[:, window], r.win_ck)
    get_cv = load(r.w_cv.at[:, window], r.win_cv)
    get_mem = load(r.memory, r.mem.at[pl.ds(pl.multiple_of(me * src_span, src_span), src_span)])
    get_so = load(r.w_so, r.all_so)
    get_cq = load(r.w_cq, r.all_cq)
    get_co = load(r.w_co, r.all_co)
    get_og = load(r.out_grad, r.grad_out.at[own_span])
    if direct:
        place_dp = lax.axis_index("dp")
        blocks, share = r.g_fo.shape[0] * 4, r.g_fo.shape[3]
        unit = share
        get_fi, get_fo = [], []
        for b in range(blocks):
            start = pl.multiple_of(b * (seq * unit) + chip * 128, 128)
            get_fi.append(load(r.w_fi.at[:, pl.ds(start, WINDOW)], r.wide_fi.at[b]))
            start = pl.multiple_of((b * seq + me) * unit, 16)
            get_fo.append(load(r.w_fo.at[pl.ds(start, unit)], r.own_fo.at[pl.ds(b * unit, unit)]))
    else:
        get_fi = [load(r.w_fi, r.own_fi)]
        get_fo = [load(r.w_fo, r.own_fo)]

    barrier = pltpu.get_barrier_semaphore()
    peers = [{"seq": peer_c}, {"seq": peer_x}]
    bits, peers_dp = [], []
    if direct:
        for level in range(3):
            bit = lax.rem(place_dp // 2**level, 2)
            bits.append(bit)
            peers_dp.append({"dp": place_dp + 2**level * (1 - 2 * bit)})
    for peer in peers + peers_dp:
        pl.semaphore_signal(barrier, inc=1, device_id=peer, device_id_type=MESH)
    pl.semaphore_wait(barrier, len(peers + peers_dp))
    peer_c_id, peer_x_id = peers

    sent, busy = [], []

    def send(src, dst, peer):
        at = len(sent)
        copy = pltpu.make_async_remote_copy(
            src_ref=src,
            dst_ref=dst,
            send_sem=r.send_sem.at[at],
            recv_sem=r.recv_sem.at[at],
            device_id=peer,
            device_id_type=MESH,
        )
        copy.start()
        sent.append(copy)
        busy.append(copy)
        return copy

    def finish(copies):
        for copy in copies:
            copy.wait_send()
            busy[:] = [other for other in busy if other is not copy]

    class Gather:
        def __init__(self, src, spot):
            self.spot = spot
            self.x = send(src, spot(me), peer_x_id)
            self.c = send(src, spot(me), peer_c_id)

        def relay(self):
            self.x.wait_recv()
            self.second = send(self.spot(peer_x), self.spot(peer_x), peer_c_id)

        def wait(self):
            self.c.wait_recv()
            self.second.wait_recv()

    def rows_at(ref, length):
        return lambda who: ref.at[pl.ds(pl.multiple_of(who * length, length), length)]

    tok = Gather(r.tokens, rows_at(r.row, span))
    mem = Gather(r.memory, rows_at(r.mem, src_span))

    def column(ids):
        return jnp.broadcast_to(ids.astype(F32), (128, ids.shape[1])).T[:, :1]

    target_ids = r.target_ids[...]
    memory_ids = r.memory_ids[...]
    self_code = jnp.where(
        lax.broadcasted_iota(jnp.int32, (1, full), 1) < full - r.pads[0, 0], target_ids, -1
    ).astype(F32)
    cross_code = jnp.where(
        lax.broadcasted_iota(jnp.int32, (1, src_full), 1) < src_full - r.pads[0, 1], memory_ids, -1
    ).astype(F32)
    target_col = column(target_ids)
    i_pos = lax.broadcasted_iota(jnp.int32, (full, full), 0)
    j_pos = lax.broadcasted_iota(jnp.int32, (full, full), 1)
    self_mask = ((target_col == self_code) & (j_pos <= i_pos)) | (i_pos == j_pos)
    r.self_bias[...] = jnp.where(self_mask, 0.0, NEGATIVE)
    r.target_col[...] = target_col
    r.cross_code[...] = cross_code

    def self_masked(scores, rows, reach):
        return scores + r.self_bias[rows, :reach]

    def cross_masked(scores, rows, reach):
        return jnp.where(r.target_col[rows, :] == r.cross_code[:, :reach], scores, NEGATIVE)

    gain_a, shift_a, gain_c, shift_c, gain_f, shift_f = (
        getattr(r, name)[...].astype(F32).reshape(1, width) for name in INPUTS[-6:]
    )
    if direct:
        from_row = lax.broadcasted_iota(jnp.int32, (WINDOW, WINDOW), 0)
        to_col = lax.broadcasted_iota(jnp.int32, (WINDOW, WINDOW), 1)
        skip = me * unit - chip * 128
        for copy in get_fi:
            copy.wait()
        for t in range(0, blocks * unit, WINDOW):
            total = None
            for b in range(t // unit, min(blocks, (t + WINDOW - 1) // unit + 1)):
                at = to_col + (t - b * unit)
                chosen = (from_row == at + skip) & (at >= 0) & (at < unit)
                term = mm(r.wide_fi[b], jnp.where(chosen, 1.0, 0.0).astype(BF16))
                total = term if total is None else total + term
            r.own_fi[:, t : t + WINDOW] = total.astype(BF16)

    get_tok.wait()
    tok.relay()
    for copy in (get_sq, get_sk, get_sv):
        copy.wait()
    tok.wait()
    row = r.row[...].astype(F32)
    normed, _ = normalize(row)
    r.n_attend[...] = normed.astype(BF16)
    h_attend = (normed * gain_a + shift_a).astype(BF16)
    r.h_attend[...] = h_attend
    r.after[...] = row

    def to_heads(value, ref, rows):
        for h in range(count):
            ref[h, rows, :] = value[:, h * HEAD_DIM : (h + 1) * HEAD_DIM].astype(ref.dtype)

    everything = slice(0, full)
    to_heads(pick(mm(h_attend, r.win_sq[...])) * HEAD_DIM**-0.5, r.q, everything)
    to_heads(pick(mm(h_attend, r.win_sk[...])), r.k, everything)
    to_heads(pick(mm(h_attend, r.win_sv[...])), r.v, everything)

    def attend(q, k, v, masked, weights, mixed, rows, reach):
        def one(h, carry):
            scores = masked(mm_t(q[h, rows, :], k[h, :reach, :]), rows, reach)
            highest = jnp.max(scores, axis=-1, keepdims=True)
            exponent = jnp.exp(scores - highest)
            total = jnp.sum(exponent, axis=-1, keepdims=True)
            low = exponent.astype(BF16)
            weights[h, rows, :reach] = low
            over = 1.0 / total
            mixed[h, rows, HEAD_DIM : HEAD_DIM + 1] = over
            mixed[h, rows, :HEAD_DIM] = mm(low, v[h, :reach, :]) * over
            return carry

        lax.fori_loop(0, count, one, 0)
        return jnp.concatenate([mixed[h, rows, :HEAD_DIM] for h in range(count)], axis=1).astype(BF16)

    def attend_back(q, k, v, grad, weights, mixed, grad_q, dk, dv, rows, reach, first):
        def one(h, carry):
            scaled = grad[h, rows, :].astype(F32) * mixed[h, rows, HEAD_DIM : HEAD_DIM + 1]
            inner = jnp.sum(scaled * mixed[h, rows, :HEAD_DIM], axis=-1, keepdims=True)
            low = scaled.astype(BF16)
            exponent = weights[h, rows, :reach]
            grad_weights = mm_t(low, v[h, :reach, :])
            grad_scores = (exponent.astype(F32) * (grad_weights - inner)).astype(BF16)
            grad_q[h, rows, :] = mm(grad_scores, k[h, :reach, :]) * HEAD_DIM**-0.5
            more_k = mm(q[h, rows, :].T, grad_scores)
            more_v = mm(low.T, exponent)
            if first:
                dk[h, :, :reach] = more_k
                dv[h, :, :reach] = more_v
            else:
                dk[h, :, :reach] += more_k
                dv[h, :, :reach] += more_v
            return carry

        lax.fori_loop(0, count, one, 0)
        return jnp.concatenate([grad_q[h, rows, :] for h in range(count)], axis=1).astype(BF16)

    chunks = [slice(c * size, (c + 1) * size) for c in range(CHUNKS)]

    def gather_columns(buffer, value, rows):
        buffer[me, rows, :] = value
        return Gather(buffer.at[me, rows], lambda who: buffer.at[who, rows])

    def joined(buffer, rows):
        return jnp.concatenate([buffer[s, rows, :] for s in range(seq)], axis=1)

    to_self = []
    for c, rows in enumerate(chunks):
        mixed = attend(
            r.q, r.k, r.v, self_masked, r.self_weights, r.self_mix, rows, rows.stop
        )
        to_self.append(gather_columns(r.self_parts, mixed, rows))
    mem.relay()
    for copy in (get_ck, get_cv, get_mem):
        copy.wait()
    mem.wait()
    out = Gather(r.out_grad, rows_at(r.grad_out, span))
    source = r.mem[...]
    every = slice(0, src_full)
    to_heads(pick(mm(source, r.win_ck[...])), r.mk, every)
    to_heads(pick(mm(source, r.win_cv[...])), r.mv, every)

    for copy in (get_so, get_cq):
        copy.wait()
    to_cross = []
    for c, rows in enumerate(chunks):
        to_self[c].relay()
        to_self[c].wait()
        mixed = joined(r.self_parts, rows)
        r.self_mixed[rows, :] = mixed
        after = r.after[rows, :] + mm(mixed, r.all_so[...])
        r.after[rows, :] = after
        normed, rate = normalize(after)
        r.n_cross[rows, :] = normed.astype(BF16)
        r.r_cross[rows, :] = rate
        hidden = (normed * gain_c + shift_c).astype(BF16)
        r.h_cross[rows, :] = hidden
        to_heads(pick(mm(hidden, r.all_cq[:, window])) * HEAD_DIM**-0.5, r.cq, rows)
        mixed = attend(
            r.cq, r.mk, r.mv, cross_masked, r.cross_weights, r.cross_mix, rows, src_full
        )
        to_cross.append(gather_columns(r.cross_parts, mixed, rows))

    for copy in [get_co, get_og] + get_fo + ([] if direct else get_fi):
        copy.wait()
    out.relay()
    out.wait()
    half = size // 2
    stats = {}

    def add(name, value):
        value = jnp.sum(value, axis=0, keepdims=True)
        stats[name] = stats[name] + value if name in stats else value

    class Total:
        def __init__(self, c, value):
            self.c = c
            self.keep = pl.ds(pl.multiple_of(core * half, half), half)
            other = pl.ds(pl.multiple_of((1 - core) * half, half), half)
            r.sum_send[c] = value.astype(BF16)
            self.step = send(r.sum_send.at[c, other], r.sum_core.at[c], peer_c_id)

        def second(self):
            self.step.wait_recv()
            value = r.sum_send[self.c, self.keep, :].astype(F32) + r.sum_core[self.c].astype(F32)
            r.sum_mid[self.c] = value.astype(BF16)
            self.step = send(r.sum_mid.at[self.c], r.sum_chip.at[self.c], peer_x_id)

        def third(self):
            self.step.wait_recv()
            value = r.sum_mid[self.c].astype(F32) + r.sum_chip[self.c].astype(F32)
            r.sum_full[self.c, self.keep, :] = value.astype(BF16)
            self.step = send(
                r.sum_full.at[self.c, self.keep], r.sum_full.at[self.c, self.keep], peer_c_id
            )

        def wait(self):
            self.step.wait_recv()
            return r.sum_full[self.c].astype(F32)

    lanes = 2 * part

    class Reduce:
        def __init__(self, group, half_at):
            self.group = getattr(r, GROUPS[group])
            self.at = 2 * group + half_at
            self.cols = pl.ds(half_at * lanes, lanes)
            self.order = ORDERS[half_at]
            self.step = 0

        def index(self, last):
            spots = [slice(None)] * 3
            for bit in self.order[: self.step]:
                spots[2 - bit] = bits[bit]
            bit = self.order[self.step]
            spots[2 - bit] = last(bits[bit])
            return tuple(spots) + (slice(None), self.cols)

        def start(self):
            inbox = (r.in_half, r.in_quarter, r.in_eighth)[self.step].at[self.at]
            away = self.index(lambda bit: 1 - bit)
            self.copy = send(self.group.at[away], inbox, peers_dp[self.order[self.step]])
            self.inbox = inbox

        def next(self):
            self.copy.wait_recv()
            keep = self.index(lambda bit: bit)
            value = self.group[keep].astype(F32) + self.inbox[...].astype(F32)
            if self.step < 2:
                self.group[keep] = value.astype(BF16)
                self.step += 1
                self.start()
            else:
                r.done[self.at] = value.astype(BF16)
                self.local = load(r.done.at[self.at], r.o_sums.at[self.at, me])
                spot = lambda who: r.o_sums.at[self.at, who]
                self.gather = Gather(r.done.at[self.at], spot)

    class Group:
        def __init__(self, group):
            self.halves = [Reduce(group, at) for at in range(2)]
            for part_of in self.halves:
                part_of.start()

        def next(self):
            for part_of in self.halves:
                part_of.next()

        def relay(self):
            for part_of in self.halves:
                part_of.gather.relay()

        def wait(self):
            for part_of in self.halves:
                part_of.local.wait()
                part_of.gather.wait()

    class Nothing:
        next = relay = wait = lambda self: None

    def reduced(group):
        return Group(group) if direct else Nothing()

    def put(group, at, value):
        ref = getattr(r, GROUPS[group])
        value = value.astype(BF16)
        if direct:
            value = value.reshape(2, 2, 2, share, value.shape[-1])
            ref[:, :, :, :, at : at + value.shape[-1]] = value
        else:
            ref[:, at : at + value.shape[-1]] = value

    totals = []
    for c, rows in enumerate(chunks):
        to_cross[c].relay()
        to_cross[c].wait()
        mixed = joined(r.cross_parts, rows)
        r.cross_mixed[rows, :] = mixed
        after = r.after[rows, :] + mm(mixed, r.all_co[...])
        r.after[rows, :] = after
        normed, rate = normalize(after)
        r.n_feed[rows, :] = normed.astype(BF16)
        r.r_feed[rows, :] = rate
        hidden = (normed * gain_f + shift_f).astype(BF16)
        r.h_feed[rows, :] = hidden
        upward = mm(hidden, r.own_fi[...])
        if c > 0:
            totals[c - 1].second()
        bell = 0.5 + 0.5 * lax.erf(upward * 2.0**-0.5)
        r.active[rows, :] = (upward * bell).astype(BF16)
        slope = bell + upward * jnp.exp(-0.5 * upward * upward) * 0.3989422804014327
        grad_up = (mm_t(r.grad_out[rows, :], r.own_fo[...]) * slope).astype(BF16)
        r.grad_up[rows, :] = grad_up
        back = mm_t(grad_up, r.own_fi[...])
        add("gf", back * normed)
        add("sf", back)
        totals.append(Total(c, back))
    scatter_rows = []

    class Scatter:
        def __init__(self, mail, core_in, chip_in, value):
            self.mail, self.core_in, self.chip_in = mail, core_in, chip_in
            mail[...] = value.reshape(mail.shape).astype(BF16)
            for spot in range(2):
                send(mail.at[2 * spot + 1 - core], core_in.at[spot], peer_c_id)
            self.steps = sent[-2:]

        def second(self):
            for step in self.steps:
                step.wait_recv()
            away = 1 - chip
            value = self.mail[2 * away + core].astype(F32) + self.core_in[away].astype(F32)
            self.mail[2 * away + core] = value.astype(BF16)
            self.step = send(self.mail.at[2 * away + core], self.chip_in, peer_x_id)

        def wait(self):
            self.step.wait_recv()
            value = self.mail[me].astype(F32) + self.core_in[chip].astype(F32)
            return value + self.chip_in[...].astype(F32)

    layer = Scatter(r.layer_mail, r.layer_core, r.layer_chip, mm(r.active[...], r.own_fo[...]))
    totals[0].third()
    totals[1].second()
    put(0, 0, t_mm(r.active[...], r.grad_out[...]))
    sum_fo = reduced(0)
    put(1, 0, t_mm(r.h_feed[...], r.grad_up[...]))
    sum_fi = reduced(1)
    layer.second()

    to_rows = []
    for c, rows in enumerate(chunks):
        grad = totals[c].wait()
        normed = r.n_feed[rows, :].astype(F32)
        grad = r.grad_out[rows, :].astype(F32) + norm_back(grad, gain_f, normed, r.r_feed[rows, :])
        r.grad_row[rows, :] = grad
        low = grad.astype(BF16)
        r.grad_cross[rows, :] = low
        to_heads(mm_t(low, r.all_co[own_rows, :]).astype(BF16), r.grad_mix, rows)
        if c == 0:
            totals[1].third()
        grad_rows = attend_back(
            r.cq, r.mk, r.mv, r.grad_mix, r.cross_weights, r.cross_mix, r.grad_q,
            r.grad_mk, r.grad_mv, rows, src_full, c == 0,
        )
        to_rows.append(gather_columns(r.row_parts, grad_rows, rows))
        if c == 0:
            r.o_layer[...] = r.after[own_span, :] + layer.wait()
    sum_fo.next()
    mk_t = r.grad_mk[...].reshape(part, src_full)
    mv_t = r.grad_mv[...].reshape(part, src_full)
    mk_low, mv_low = mk_t.astype(BF16), mv_t.astype(BF16)
    terms = mm_t(place(mk_t.T.astype(BF16)), r.win_ck[...]) + mm_t(
        place(mv_t.T.astype(BF16)), r.win_cv[...]
    )
    memory_sum = Scatter(r.mem_mail, r.mem_core, r.mem_chip, terms)
    to_rows[0].relay()
    put(2, part, mm(mk_low, r.mem[...]).T)
    put(2, 2 * part, mm(mv_low, r.mem[...]).T)
    put(2, 0, pick(t_mm(r.cross_mixed[...], r.grad_cross[:, window])))
    put(2, 3 * part, t_mm(r.h_cross[...], r.row_parts[me]))
    sum_cross = reduced(2)
    sum_fi.next()
    memory_sum.second()

    for c, rows in enumerate(chunks):
        if c > 0:
            to_rows[c].relay()
        to_rows[c].wait()
        grad = mm_t(joined(r.row_parts, rows), r.all_cq[...])
        normed = r.n_cross[rows, :].astype(F32)
        add("gc", grad * normed)
        add("sc", grad)
        grad = r.grad_row[rows, :] + norm_back(grad, gain_c, normed, r.r_cross[rows, :])
        r.grad_row[rows, :] = grad
        low = grad.astype(BF16)
        r.grad_self[rows, :] = low
        to_heads(mm_t(low, r.all_so[own_rows, :]).astype(BF16), r.grad_mix, rows)
    sum_fo.next()
    for c, rows in reversed(list(enumerate(chunks))):
        r.grad_rows[rows, :] = attend_back(
            r.q, r.k, r.v, r.grad_mix, r.self_weights, r.self_mix, r.grad_q,
            r.grad_k, r.grad_v, rows, rows.stop, c == CHUNKS - 1,
        )
    sum_fo.next()
    sum_fi.next()
    sum_cross.next()
    k_t = r.grad_k[...].reshape(part, full)
    v_t = r.grad_v[...].reshape(part, full)
    grad_q = r.grad_rows[...]
    back = (
        mm_t(place(grad_q), r.win_sq[...])
        + mm_t(place(k_t.T.astype(BF16)), r.win_sk[...])
        + mm_t(place(v_t.T.astype(BF16)), r.win_sv[...])
    )
    add("ga", back * r.n_attend[...].astype(F32))
    add("sa", back)
    finish(layer.steps + [layer.step])
    tokens_sum = Scatter(r.layer_mail, r.layer_core, r.layer_chip, back)
    put(3, part, t_mm(r.h_attend[...], grad_q))
    put(3, 2 * part, mm(k_t.astype(BF16), r.h_attend[...]).T)
    put(3, 3 * part, mm(v_t.astype(BF16), r.h_attend[...]).T)
    put(3, 0, pick(t_mm(r.self_mixed[...], r.grad_self[:, window])))
    sum_self = reduced(3)
    shared = jnp.where(me == 0, 1.0, 0.0)
    stats = jnp.concatenate(
        [stats["ga"], stats["sa"], stats["gc"] * shared, stats["sc"] * shared, stats["gf"], stats["sf"]]
        + [jnp.zeros((2, width), F32)],
        axis=0,
    )

    class Stats:
        def __init__(self):
            self.value, self.step = stats, 0

        def start(self):
            r.stat_out[self.step] = self.value
            peer = (peers + peers_dp)[self.step]
            self.copy = send(r.stat_out.at[self.step], r.stat_in.at[self.step], peer)

        def next(self):
            self.copy.wait_recv()
            self.value = self.value + r.stat_in[self.step]
            self.step += 1
            if self.step < 5:
                self.start()

    if direct:
        norm_sum = Stats()
        norm_sum.start()
    tokens_sum.second()
    sum_fi.next()
    sum_fo.relay()
    sum_cross.next()
    if direct:
        norm_sum.next()
    r.o_memory[...] = memory_sum.wait()
    own_row = r.row[own_span, :].astype(F32)
    normed, rate = normalize(own_row)
    grad = tokens_sum.wait()
    r.o_tokens[...] = r.grad_row[own_span, :] + norm_back(grad, gain_a, normed, rate)
    sum_fi.relay()
    if direct:
        norm_sum.next()
    sum_cross.next()
    sum_self.next()
    if direct:
        norm_sum.next()
    sum_cross.relay()
    sum_self.next()
    if direct:
        norm_sum.next()
    sum_self.next()
    if direct:
        norm_sum.next()
        stats = norm_sum.value
    r.o_stats[...] = stats
    sum_self.relay()
    for group in (sum_fo, sum_fi, sum_cross, sum_self):
        group.wait()
    finish(list(busy))


def row_call(seq, span, src_span, width, part, units, direct, operands):
    full, src_full = span * seq, src_span * seq
    count, size = part // HEAD_DIM, full // CHUNKS
    half = size // 2
    shapes = dict(
        row=((full, width), BF16),
        mem=((src_full, width), BF16),
        grad_out=((full, width), BF16),
        win_sq=((width, WINDOW), BF16),
        win_sk=((width, WINDOW), BF16),
        win_sv=((width, WINDOW), BF16),
        win_ck=((width, WINDOW), BF16),
        win_cv=((width, WINDOW), BF16),
        all_so=((width, width), BF16),
        all_cq=((width, width), BF16),
        all_co=((width, width), BF16),
        own_fi=((width, units), BF16),
        own_fo=((units, width), BF16),
        self_bias=((full, full), F32),
        target_col=((full, 1), F32),
        cross_code=((1, src_full), F32),
        n_attend=((full, width), BF16),
        n_cross=((full, width), BF16),
        n_feed=((full, width), BF16),
        r_cross=((full, 1), F32),
        r_feed=((full, 1), F32),
        h_attend=((full, width), BF16),
        h_cross=((full, width), BF16),
        h_feed=((full, width), BF16),
        after=((full, width), F32),
        grad_row=((full, width), F32),
        q=((count, full, HEAD_DIM), BF16),
        k=((count, full, HEAD_DIM), BF16),
        v=((count, full, HEAD_DIM), BF16),
        cq=((count, full, HEAD_DIM), BF16),
        mk=((count, src_full, HEAD_DIM), BF16),
        mv=((count, src_full, HEAD_DIM), BF16),
        grad_mix=((count, full, HEAD_DIM), BF16),
        grad_q=((count, full, HEAD_DIM), F32),
        self_weights=((count, full, full), BF16),
        cross_weights=((count, full, src_full), BF16),
        self_mix=((count, full, 2 * HEAD_DIM), F32),
        cross_mix=((count, full, 2 * HEAD_DIM), F32),
        grad_k=((count, HEAD_DIM, full), F32),
        grad_v=((count, HEAD_DIM, full), F32),
        grad_mk=((count, HEAD_DIM, src_full), F32),
        grad_mv=((count, HEAD_DIM, src_full), F32),
        self_parts=((seq, full, part), BF16),
        cross_parts=((seq, full, part), BF16),
        row_parts=((seq, full, part), BF16),
        self_mixed=((full, width), BF16),
        cross_mixed=((full, width), BF16),
        active=((full, units), BF16),
        grad_up=((full, units), BF16),
        grad_cross=((full, width), BF16),
        grad_self=((full, width), BF16),
        grad_rows=((full, part), BF16),
        sum_send=((CHUNKS, size, width), BF16),
        sum_core=((CHUNKS, half, width), BF16),
        sum_mid=((CHUNKS, half, width), BF16),
        sum_chip=((CHUNKS, half, width), BF16),
        sum_full=((CHUNKS, size, width), BF16),
        layer_mail=((seq, span, width), BF16),
        layer_core=((2, span, width), BF16),
        layer_chip=((span, width), BF16),
        mem_mail=((seq, src_span, width), BF16),
        mem_core=((2, src_span, width), BF16),
        mem_chip=((src_span, width), BF16),
    )
    group = (width, 4 * part)
    if direct:
        blocks, share = 8, width // 8
        lanes = 2 * part
        group = (2, 2, 2, share, 4 * part)
        shapes.update({name: (group, BF16) for name in GROUPS})
        shapes.update(
            wide_fi=((blocks, width, WINDOW), BF16),
            in_half=((8, 2, 2, share, lanes), BF16),
            in_quarter=((8, 2, share, lanes), BF16),
            in_eighth=((8, share, lanes), BF16),
            done=((8, share, lanes), BF16),
            stat_out=((5, 8, width), F32),
            stat_in=((5, 8, width), F32),
        )
    names = list(shapes) + ["load_sem", "send_sem", "recv_sem"]
    scratch = [pltpu.VMEM(shape, dtype) for shape, dtype in shapes.values()]
    scratch += [pltpu.SemaphoreType.DMA((40,)), pltpu.SemaphoreType.DMA((104,)), pltpu.SemaphoreType.DMA((104,))]
    hbm = pl.BlockSpec(memory_space=pl.ANY)
    vmem = pl.BlockSpec(memory_space=pltpu.VMEM)
    smem = pl.BlockSpec(memory_space=pltpu.SMEM)
    outs = [((span, width), F32), ((span, width), F32), ((src_span, width), F32), ((8, width), F32)]
    out_specs = [vmem] * 4
    if direct:
        outs += [((8, seq, share, lanes), BF16)]
        out_specs += [hbm]
    else:
        outs += [(group, BF16)] * 4
        out_specs += [vmem] * 4
    return pl.pallas_call(
        functools.partial(row_kernel, names, seq, direct),
        out_shape=[jax.ShapeDtypeStruct(s, t) for s, t in outs],
        in_specs=[hbm] * 3 + [vmem] * 2 + [smem] + [hbm] * 10 + [vmem] * 6,
        out_specs=out_specs,
        scratch_shapes=scratch,
        compiler_params=pltpu.CompilerParams(
            collective_id=0, has_side_effects=True, vmem_limit_bytes=64 * 2**20 - 2**17
        ),
    )(*operands)


def final_kernel(seq, dp, layer, tokens, memory, stats, sums, *refs):
    outs, sems = refs[:-1], refs[-1]
    copies = [
        pltpu.make_async_copy(src, dst, sems.at[i])
        for i, (src, dst) in enumerate(zip((layer, tokens, memory), outs[:3]))
    ]
    for copy in copies:
        copy.start()
    sq, sk, sv, so, cq, ck, cv, co, fi, fo = outs[3:13]
    share, lanes = sums.shape[2:]
    part = lanes // 2
    unit = fo.shape[0] // seq
    for s in range(seq):
        for at in range(2):
            fo[s * unit : (s + 1) * unit, at * lanes : (at + 1) * lanes] = sums[at, s].astype(F32)
    for at in range(2):
        wide = [sums[2 + at, s].astype(F32) for s in range(seq)]
        for b in range(dp // 2):
            block = [w[:, b * unit : (b + 1) * unit] for w in wide]
            start = (at * (dp // 2) + b) * seq * unit
            fi[:, start : start + seq * unit] = jnp.concatenate(block, 1)
    for i, out in enumerate((co, ck, cv, cq, so, sq, sk, sv)):
        start = i % 2 * part
        block = [sums[4 + i // 2, s].astype(F32)[:, start : start + part] for s in range(seq)]
        out[...] = jnp.concatenate(block, 1)
    width = stats.shape[1]
    back = lax.rem(width - lax.axis_index("dp") * share, width)
    own = pltpu.roll(stats[...], back, 1)[:, :share]
    for i, out in enumerate(outs[13:]):
        out[...] = own[i]
    for copy in copies:
        copy.wait()


def final_call(seq, dp, layer, tokens, memory, stats, sums):
    share, width = sums.shape[2], stats.shape[1]
    feed = sums.shape[3] * 2 * seq
    hbm = pl.BlockSpec(memory_space=pl.ANY)
    vmem = pl.BlockSpec(memory_space=pltpu.VMEM)
    shapes = [layer.shape, tokens.shape, memory.shape] + [(share, width)] * 8
    shapes += [(share, feed), (feed // dp, width)] + [(share,)] * 6
    return pl.pallas_call(
        functools.partial(final_kernel, seq, dp),
        out_shape=[jax.ShapeDtypeStruct(shape, F32) for shape in shapes],
        in_specs=[hbm] * 3 + [vmem] * 2,
        out_specs=[hbm] * 3 + [vmem] * 16,
        scratch_shapes=[pltpu.SemaphoreType.DMA((3,))],
        compiler_params=pltpu.CompilerParams(vmem_limit_bytes=32 * 2**20),
    )(layer, tokens, memory, stats, sums)


def swap(value, axis, bit):
    size = lax.axis_size(axis)
    return lax.ppermute(value, axis, [(i, i ^ bit) for i in range(size)])


def scatter_sum(value, bits):
    index = lax.axis_index("dp")
    size = lax.axis_size("dp")
    levels = size.bit_length() - 1
    blocks = value.reshape((2,) * levels + value.shape[1:])
    left = list(range(levels))[::-1]
    for bit in bits:
        at = left.index(bit)
        mine = (index >> bit) & 1
        keep = lax.dynamic_index_in_dim(blocks, mine, at, keepdims=False)
        away = lax.dynamic_index_in_dim(blocks, 1 - mine, at, keepdims=False)
        left.pop(at)
        got = swap(away.astype(BF16), "dp", 1 << bit)
        blocks = keep.astype(F32) + got.astype(F32)
    return blocks


def shards(
    tokens,
    memory,
    target_segments,
    memory_segments,
    pad_counts,
    out_grad,
    self_query,
    self_key,
    self_value,
    self_out,
    cross_query,
    cross_key,
    cross_value,
    cross_out,
    feed_in,
    feed_out,
    gain_attend,
    shift_attend,
    gain_cross,
    shift_cross,
    gain_feed,
    shift_feed,
):
    seq, dp = lax.axis_size("seq"), lax.axis_size("dp")
    me = lax.axis_index("seq")
    span, width = tokens.shape[1:]
    part = width // seq
    feed = feed_in.shape[1]
    unit = feed // dp // seq
    direct = dp == 8 and unit == width // dp and unit % 16 == 0
    fi, fo = feed_in, feed_out
    if not direct:
        fi = lax.dynamic_index_in_dim(fi.reshape(width, dp, seq, unit), me, 2, keepdims=False)
        fi = fi.reshape(width, dp * unit)
        fo = lax.dynamic_index_in_dim(fo.reshape(dp, seq, unit, width), me, 1, keepdims=False)
        fo = fo.reshape(dp * unit, width)
    operands = (
        tokens[0], memory[0], out_grad[0], target_segments, memory_segments, pad_counts,
        self_query, self_key, self_value, self_out, cross_query, cross_key, cross_value, cross_out,
        fi, fo, gain_attend, shift_attend, gain_cross, shift_cross, gain_feed, shift_feed,
    )
    results = row_call(seq, span, memory.shape[1], width, part, dp * unit, direct, operands)
    if direct:
        results = final_call(seq, dp, *results)
        return tuple(value[None] for value in results[:3]) + tuple(results[3:])
    layer_out, tokens_grad, memory_grad, stats, g_fo, g_fi, g_cross, g_self = results
    gather = lambda v, axis: lax.all_gather(v, "seq", axis=axis, tiled=True)

    levels = dp.bit_length() - 1
    up = list(range(levels))
    first, second = up, up[1:] + up[:1]
    share = width // dp
    split = lambda v: v.reshape(dp, share, -1)
    groups = ((split(g_fo), first), (split(g_fi), second), (split(g_cross), first), (split(g_self), second))
    summed = [gather(scatter_sum(v, bits).astype(BF16)[None], 0) for v, bits in groups]
    whole_fo = summed[0].reshape(seq * share, width).astype(F32)
    whole_fi = (
        summed[1].reshape(seq, share, dp, unit).transpose(1, 2, 0, 3).reshape(share, feed)
    ).astype(F32)

    def whole(group, at):
        block = group[:, :, at * part : (at + 1) * part]
        return block.transpose(1, 0, 2).reshape(share, width).astype(F32)

    co, ck, cv, cq = (whole(summed[2], at) for at in range(4))
    so, sq, sk, sv = (whole(summed[3], at) for at in range(4))
    stats = lax.psum(stats, ("seq", "dp"))
    norm_part = lax.dynamic_slice_in_dim(stats, lax.axis_index("dp") * share, share, 1)
    return (
        layer_out[None],
        tokens_grad[None],
        memory_grad[None],
        sq,
        sk,
        sv,
        so,
        cq,
        ck,
        cv,
        co,
        whole_fi,
        whole_fo,
    ) + tuple(norm_part[i] for i in range(6))


def solution(mesh):
    rows = P("dp", "seq", None)
    in_specs = (rows, rows, P("dp", None), P("dp", None), P("dp", None), rows) + (P(),) * 16
    out_specs = (rows,) * 3 + (P("dp", None),) * 10 + (P("dp"),) * 6
    return jax.shard_map(shards, mesh=mesh, in_specs=in_specs, out_specs=out_specs, check_vma=False)
```

```python
import functools

import jax
import jax.numpy as jnp
from jax import lax
from jax.experimental import pallas as pl
from jax.experimental.pallas import tpu as pltpu
from jax.sharding import PartitionSpec as P

HEAD_DIM = 64
EPSILON = 1e-05
NEGATIVE = -1e30
F32 = jnp.float32
BF16 = jnp.bfloat16
MESH = pl.DeviceIdType.MESH
WINDOW = 256
CHUNKS = 2


def mm(left, right):
    return jnp.dot(left, right, preferred_element_type=F32)


def mm_t(left, right):
    return lax.dot_general(left, right, (((1,), (1,)), ((), ())), preferred_element_type=F32)


def t_mm(left, right):
    return lax.dot_general(left, right, (((0,), (0,)), ((), ())), preferred_element_type=F32)


def normalize(values):
    centered = values - jnp.mean(values, axis=-1, keepdims=True)
    rate = lax.rsqrt(jnp.mean(centered * centered, axis=-1, keepdims=True) + EPSILON)
    return centered * rate, rate


def norm_back(grad, gain, normed, rate):
    scaled = grad * gain
    inner = jnp.mean(scaled * normed, axis=-1, keepdims=True)
    return rate * (scaled - jnp.mean(scaled, axis=-1, keepdims=True) - normed * inner)


class Names:
    def __init__(self, names, refs):
        self.__dict__.update(zip(names, refs))


INPUTS = ["tokens", "memory", "out_grad", "target_ids", "memory_ids", "pads"]
INPUTS += ["w_sq", "w_sk", "w_sv", "w_so", "w_cq", "w_ck", "w_cv", "w_co", "w_fi", "w_fo"]
INPUTS += ["gain_a", "shift_a", "gain_c", "shift_c", "gain_f", "shift_f"]
OUTPUTS = ["o_layer", "o_tokens", "o_memory", "o_stats"]
SEMAPHORES = ["load_sem", "send_sem", "recv_sem"]
GROUPS = ["g_fo", "g_fi", "g_cross", "g_self"]
ALONG, ACROSS, MIXED, TURNED = (1, 2, 0), (0, 1, 2), (1, 0, 2), (0, 2, 1)
ORDERS = (ACROSS, ALONG, ALONG, ACROSS, ACROSS, ACROSS, ACROSS, ACROSS)
STRAIGHT = 6
CUTS = (2, 1, 1, 6)
(
    OWN_FI, TOKENS_NEAR, TOKENS_MIDDLE, TOKENS_FAR, MEMORY_NEAR, MEMORY_MIDDLE, MEMORY_FAR, TOKENS_RELAY, MEMORY_RELAY,
    COTANGENT_SEND, COTANGENT_RELAY, LAYER_SEND, LAYER_SECOND, LAYER_OUT, MEMORY_TERMS,
    MEMORY_SECOND, MEMORY_OUT, TOKEN_TERMS, TOKEN_SECOND, TOKEN_OUT, GRAD_FO, GRAD_FI, GRAD_CK,
    GRAD_CV, GRAD_CO, GRAD_CQ, GRAD_SO, GRAD_SQ, GRAD_SK, GRAD_SV, NORMS_SEND,
) = range(31)
(
    SELF, ROWS, CROSS, FEED_UP, FEED_BACK, LAYER, CROSS_GRAD, CROSS_BACK, SELF_GRAD, SELF_BACK,
    CROSS_RELAY, ROWS_RELAY, TOTAL_SECOND, TOTAL_THIRD, NORMS_STEP,
) = range(100, 115)
OUT, W_SO, W_CO, W_FO = range(4)
SCHEDULE = [
    OWN_FI, TOKENS_NEAR, MEMORY_NEAR, TOKENS_RELAY, TOKENS_MIDDLE, TOKENS_FAR, (SELF, 1), (SELF, 0),
    (ROWS, 1), COTANGENT_SEND, (ROWS, 0), MEMORY_RELAY, MEMORY_MIDDLE, MEMORY_FAR, (CROSS, 0),
    (CROSS, 1), COTANGENT_RELAY, (CROSS_RELAY, 0), (FEED_UP, 0), (CROSS_RELAY, 1), (FEED_BACK, 0),
    (FEED_UP, 1), (TOTAL_SECOND, 0), GRAD_FO, (LAYER, 1), (1, 0, 0), (0, 0, 0), (FEED_BACK, 1),
    GRAD_FI, (3, 0, 0), (2, 0, 0), (TOTAL_SECOND, 1), (LAYER, 0), LAYER_SEND, (0, 1, 0), (1, 1, 0),
    (TOTAL_THIRD, 0), LAYER_SECOND, (1, 0, 1), (0, 0, 1), (CROSS_GRAD, 0), (CROSS_BACK, 0),
    (TOTAL_THIRD, 1), (CROSS_GRAD, 1), GRAD_CO, (CROSS_BACK, 1), GRAD_CK, (4, 0, 0), (ROWS_RELAY, 0),
    (1, 1, 1), GRAD_CQ, LAYER_OUT, (1, 0, 2), (3, 0, 1), (0, 1, 1), GRAD_CV, (0, 0, 2), (5, 0, 0),
    MEMORY_TERMS, (ROWS_RELAY, 1), (2, 0, 1), (SELF_GRAD, 0), (1, 1, 2), MEMORY_SECOND, (SELF_GRAD, 1),
    GRAD_SO, (7, 0, 0), (3, 0, 2), (4, 0, 1), (SELF_BACK, 1), (SELF_BACK, 0), GRAD_SK, GRAD_SV,
    (7, 4, 0), (7, 1, 0), (7, 2, 0), TOKEN_TERMS, (7, 3, 0), (0, 1, 2), (5, 0, 1), (1, 0, 3),
    NORMS_SEND, GRAD_SQ, TOKEN_SECOND, (NORMS_STEP, 0), (6, 0, 0), (7, 0, 1), (2, 0, 2), (4, 0, 2),
    MEMORY_OUT, (7, 5, 0), (7, 4, 1), (0, 0, 3), (6, 1, 0), (6, 2, 0), (6, 3, 0), (6, 4, 0), (6, 5, 0),
    (3, 0, 3), (1, 0, 4), (7, 1, 1), (1, 1, 3), (7, 2, 1), (1, 0, 5), (0, 1, 3), (7, 3, 1), (5, 0, 2),
    (7, 0, 2), (6, 0, 1), TOKEN_OUT, (NORMS_STEP, 1), (2, 0, 3), (4, 0, 3), (7, 4, 2), (0, 0, 4),
    (7, 1, 2), (7, 5, 1), (7, 2, 2), (0, 0, 5), (7, 3, 2), (6, 1, 1), (3, 0, 4), (1, 1, 4), (6, 2, 1),
    (3, 0, 5), (0, 1, 4), (5, 0, 3), (6, 0, 2), (6, 3, 1), (1, 1, 5), (7, 0, 3), (0, 1, 5), (7, 4, 3),
    (6, 4, 1), (7, 5, 2), (7, 1, 3), (2, 0, 4), (7, 2, 3), (6, 5, 1), (6, 1, 2), (7, 3, 3),
    (NORMS_STEP, 2), (2, 0, 5), (6, 2, 2), (4, 0, 4), (6, 3, 2), (6, 0, 3), (6, 4, 2), (4, 0, 5),
    (5, 0, 4), (7, 5, 3), (7, 0, 5), (6, 5, 2), (7, 4, 5), (5, 0, 5), (6, 1, 3), (NORMS_STEP, 3),
    (7, 1, 5), (7, 2, 5), (6, 2, 3), (7, 3, 5), (6, 3, 3), (6, 0, 5), (6, 4, 3), (7, 5, 5), (6, 5, 3),
    (6, 1, 5), (6, 2, 5), (NORMS_STEP, 4), (6, 3, 5), (6, 4, 5), (6, 5, 5),
]


def row_kernel(scratch_names, seq, direct, *refs):
    r = Names(INPUTS + OUTPUTS + (["o_sums"] if direct else GROUPS) + scratch_names, refs)
    me = lax.axis_index("seq")
    core = lax.rem(me, 2)
    chip = me // 2
    peer_c = me + 1 - 2 * core
    peer_x = lax.rem(me + 2, 4)
    span = r.tokens.shape[0]
    full, width = r.row.shape
    src_span = r.memory.shape[0]
    src_full = src_span * seq
    part = width // seq
    count = part // HEAD_DIM
    size = full // CHUNKS
    odd = chip
    half_width = 2 * part
    core_window = pl.ds(pl.multiple_of(core * half_width, 128), half_width)
    window = pl.ds(pl.multiple_of(core * half_width + chip * 128, 128), WINDOW)
    own_window = pl.ds(pl.multiple_of(chip * 128, 128), WINDOW)
    own_rows = pl.ds(pl.multiple_of((2 * core + chip) * part, 64), part)
    own_head, other_head = chip * count, (1 - chip) * count
    own_span = pl.ds(pl.multiple_of(me * span, span), span)

    def pick(value):
        return jnp.where(odd == 1, value[:, 64 : 64 + part], value[:, :part])

    def place(value):
        empty = jnp.zeros((value.shape[0], WINDOW - part), value.dtype)
        return jnp.where(
            odd == 1,
            jnp.concatenate([empty, value], 1),
            jnp.concatenate([value, empty], 1),
        )

    loads = []

    def load(src, dst):
        copy = pltpu.make_async_copy(src, dst, r.load_sem.at[len(loads)])
        copy.start()
        loads.append(copy)
        return copy

    stores = []

    def store(src, dst):
        stores.append(load(src, dst))

    def ready(*copies):
        for copy in copies:
            copy.wait()

    place_dp = lax.axis_index("dp")
    peers = [{"seq": peer_c}, {"seq": peer_x}]
    to_core, to_chip = peers
    to_far = {"seq": lax.rem(peer_c + 2, 4)}
    bits, peers_dp = [], []
    if direct:
        for level in range(3):
            bit = lax.rem(place_dp // 2**level, 2)
            bits.append(bit)
            peers_dp.append({"dp": place_dp + 2**level * (1 - 2 * bit)})
    barrier = pltpu.get_barrier_semaphore()
    others = peers + peers_dp + ([to_far] if direct else [])
    for peer in others:
        pl.semaphore_signal(barrier, inc=1, device_id=peer, device_id_type=MESH)

    own_source = pl.ds(pl.multiple_of(me * src_span, src_span), src_span)
    get_tok = load(r.tokens, r.row.at[own_span])
    get_sq = load(r.w_sq.at[:, core_window], r.win_sq)
    get_sk = load(r.w_sk.at[:, core_window], r.win_sk)
    get_sv = load(r.w_sv.at[:, core_window], r.win_sv)
    get_mem = load(r.memory, r.mem.at[own_source])
    get_ck = load(r.w_ck.at[:, window], r.win_ck)
    get_cv = load(r.w_cv.at[:, window], r.win_cv)
    get_fi, get_fo = [], []
    if direct:
        blocks, share = r.g_fo.shape[0] * 4, r.g_fo.shape[3]
        unit = share

        def wide_fi(b):
            spot = pl.ds(b % 4 * WINDOW, WINDOW)
            return r.cross_weights.at[pl.ds(b // 4 * width, width), spot]

        for b in range(blocks):
            start = pl.multiple_of(b * (seq * unit) + chip * 128, 128)
            get_fi.append(load(r.w_fi.at[:, pl.ds(start, WINDOW)], wide_fi(b)))
        for b in range(blocks):
            start = pl.multiple_of((b * seq + me) * unit, 16)
            get_fo.append(load(r.w_fo.at[pl.ds(start, unit)], r.own_fo.at[pl.ds(b * unit, unit)]))
    else:
        get_fi = [load(r.w_fi, r.own_fi)]
        get_fo = [load(r.w_fo, r.own_fo)]
    get_so = load(r.w_so, r.all_so)
    get_cq = load(r.w_cq, r.all_cq)
    get_co = load(r.w_co, r.all_co)
    get_og = load(r.out_grad, r.grad_out.at[own_span])

    def column(ids):
        return jnp.broadcast_to(ids.astype(F32), (128, ids.shape[1])).T[:, :1]

    target_ids = r.target_ids[...]
    memory_ids = r.memory_ids[...]
    self_code = jnp.where(
        lax.broadcasted_iota(jnp.int32, (1, full), 1) < full - r.pads[0, 0], target_ids, -1
    ).astype(F32)
    cross_code = jnp.where(
        lax.broadcasted_iota(jnp.int32, (1, src_full), 1) < src_full - r.pads[0, 1], memory_ids, -1
    ).astype(F32)
    target_col = column(target_ids)
    i_pos = lax.broadcasted_iota(jnp.int32, (full, full), 0)
    j_pos = lax.broadcasted_iota(jnp.int32, (full, full), 1)
    self_mask = ((target_col == self_code) & (j_pos <= i_pos)) | (i_pos == j_pos)
    r.self_bias[...] = jnp.where(self_mask, 0.0, NEGATIVE)
    r.target_col[...] = target_col
    r.cross_code[...] = cross_code

    def self_masked(scores, rows, reach):
        return scores + r.self_bias[rows, :reach]

    def cross_masked(scores, rows, reach):
        return jnp.where(r.target_col[rows, :] == r.cross_code[:, :reach], scores, NEGATIVE)

    gain_a, shift_a, gain_c, shift_c, gain_f, shift_f = (
        getattr(r, name)[...].astype(F32).reshape(1, width) for name in INPUTS[-6:]
    )
    pl.semaphore_wait(barrier, len(others))

    sent, busy = [], []

    def send(src, dst, peer):
        at = len(sent)
        copy = pltpu.make_async_remote_copy(
            src_ref=src,
            dst_ref=dst,
            send_sem=r.send_sem.at[at],
            recv_sem=r.recv_sem.at[at],
            device_id=peer,
            device_id_type=MESH,
        )
        copy.start()
        sent.append(copy)
        busy.append(copy)
        return copy

    def finish(copies):
        for copy in copies:
            copy.wait_send()
            busy[:] = [other for other in busy if other is not copy]

    class Gather:
        def __init__(self, src, spot):
            self.spot = spot
            self.x = send(src, spot(me), to_chip)
            self.c = send(src, spot(me), to_core)

        def near(self):
            self.c.wait_recv()

        def relay(self):
            self.x.wait_recv()
            self.second = send(self.spot(peer_x), self.spot(peer_x), to_core)

        def far(self):
            self.second.wait_recv()

        def wait(self):
            self.near()
            self.far()

    def rows_at(ref, length):
        return lambda who: ref.at[pl.ds(pl.multiple_of(who * length, length), length)]

    tok = Gather(r.tokens, rows_at(r.row, span))
    mem = Gather(r.memory, rows_at(r.mem, src_span))
    tasks = {}

    class kept:
        to_self, to_cross, to_rows, total, slope, ended = {}, {}, {}, {}, {}, {}
        seen = set()

    def once(what):
        first = what not in kept.seen
        kept.seen.add(what)
        return first

    def task(name):
        def keep(function):
            tasks[name] = function

        return keep

    @task(OWN_FI)
    def _():
        if not direct:
            return
        from_row = lax.broadcasted_iota(jnp.int32, (WINDOW, WINDOW), 0)
        to_col = lax.broadcasted_iota(jnp.int32, (WINDOW, WINDOW), 1)
        skip = me * unit - chip * 128
        ready(*get_fi)
        for t in range(0, blocks * unit, WINDOW):
            total = None
            for b in range(t // unit, min(blocks, (t + WINDOW - 1) // unit + 1)):
                at = to_col + (t - b * unit)
                chosen = (from_row == at + skip) & (at >= 0) & (at < unit)
                term = mm(wide_fi(b)[...], jnp.where(chosen, 1.0, 0.0).astype(BF16))
                total = term if total is None else total + term
            r.own_fi[:, t : t + WINDOW] = total.astype(BF16)

    def to_heads(value, ref, rows):
        ones = jnp.ones((value.shape[0], HEAD_DIM), ref.dtype)
        for h in range(value.shape[1] // HEAD_DIM):
            head = value[:, h * HEAD_DIM : (h + 1) * HEAD_DIM].astype(ref.dtype)
            ref[h, rows, :] = head if ref.shape[2] == HEAD_DIM else jnp.concatenate([head, ones], 1)

    def part_of(who, length):
        return pl.ds(pl.multiple_of(who * length, length), length)

    def project_tokens(rows):
        row = r.row[rows, :].astype(F32)
        normed, _ = normalize(row)
        r.n_attend[rows, :] = normed.astype(BF16)
        hidden = (normed * gain_a + shift_a).astype(BF16)
        r.h_attend[rows, :] = hidden
        r.after[rows, :] = row
        to_heads(mm(hidden, r.win_sq[...]) * HEAD_DIM**-0.5, r.q, rows)
        to_heads(mm(hidden, r.win_sk[...]), r.k, rows)
        to_heads(mm(hidden, r.win_sv[...]), r.v, rows)

    def project_memory(rows):
        source = r.mem[rows, :]
        to_heads(pick(mm(source, r.win_ck[...])), r.mk, rows)
        to_heads(pick(mm(source, r.win_cv[...])), r.mv, rows)

    @task(TOKENS_NEAR)
    def _():
        ready(get_tok, get_sq, get_sk, get_sv)
        tok.near()
        project_tokens(part_of(chip, full // 2))

    @task(MEMORY_NEAR)
    def _():
        ready(get_mem, get_ck, get_cv)
        mem.near()
        project_memory(part_of(chip, src_full // 2))

    tasks[TOKENS_RELAY] = tok.relay

    @task(TOKENS_MIDDLE)
    def _():
        project_tokens(part_of(peer_x, span))

    @task(TOKENS_FAR)
    def _():
        tok.far()
        project_tokens(part_of(3 - me, span))

    tasks[MEMORY_RELAY] = mem.relay

    @task(MEMORY_MIDDLE)
    def _():
        project_memory(part_of(peer_x, src_span))

    @task(MEMORY_FAR)
    def _():
        mem.far()
        project_memory(part_of(3 - me, src_span))

    def attend(q, k, v, masked, weights, mixed, rows, reach, base=0):
        def one(h):
            scores = masked(mm_t(q[base + h, rows, :], k[base + h, :reach, :]), rows, reach)
            highest = jnp.max(scores, axis=-1, keepdims=True)
            low = jnp.exp(scores - highest).astype(BF16)
            product = mm(low, v[base + h, :reach, :])
            over = 1.0 / product[:, HEAD_DIM : HEAD_DIM + 1]
            head = product[:, :HEAD_DIM] * over
            if weights is not None:
                weights[h * full + rows.start : h * full + rows.stop, :reach] = low
                mixed[h, rows, HEAD_DIM : HEAD_DIM + 1] = over
                mixed[h, rows, :HEAD_DIM] = head
            return head.astype(BF16)

        return [one(h) for h in range(count)]

    def attend_back(q, k, v, grad, weights, mixed, dk, dv, rows, reach, first, base=0):
        def one(h):
            scaled = grad[h, rows, :].astype(F32) * mixed[h, rows, HEAD_DIM : HEAD_DIM + 1]
            inner = jnp.sum(scaled * mixed[h, rows, :HEAD_DIM], axis=-1, keepdims=True)
            low = scaled.astype(BF16)
            exponent = weights[h * full + rows.start : h * full + rows.stop, :reach]
            grad_weights = mm_t(low, v[base + h, :reach, :HEAD_DIM])
            grad_scores = (exponent.astype(F32) * (grad_weights - inner)).astype(BF16)
            grad_q = mm(grad_scores, k[base + h, :reach, :]) * HEAD_DIM**-0.5
            more_k = mm(q[base + h, rows, :].T, grad_scores)
            more_v = mm(low.T, exponent)
            if first:
                dk[h, :, :reach] = more_k
                dv[h, :, :reach] = more_v
            else:
                dk[h, :, :reach] += more_k
                dv[h, :, :reach] += more_v
            return grad_q.astype(BF16)

        return [one(h) for h in range(count)]

    chunks = [slice(c * size, (c + 1) * size) for c in range(CHUNKS)]
    half = size // 2

    def gather_columns(buffer, c, heads):
        buffer[c, me, :size, :] = jnp.concatenate(heads[:2], axis=1)
        buffer[c, me, size:, :] = jnp.concatenate([heads[2][:half], heads[2][half:]], axis=1)
        return Gather(buffer.at[c, me], lambda who: buffer.at[c, who])

    def joined(buffer, c):
        pieces = []
        for s in (0, 2, 1, 3):
            last = buffer[c, s, size:, :]
            pieces.append(buffer[c, s, :size, :])
            pieces.append(jnp.concatenate([last[:, :HEAD_DIM], last[:, HEAD_DIM:]], axis=0))
        return jnp.concatenate(pieces, axis=1)

    def self_chunk(c, rows):
        ours, theirs = (
            jnp.concatenate(attend(r.q, r.k, r.v, self_masked, weights, mix, rows, rows.stop, base), 1)
            for weights, mix, base in (
                (r.self_weights, r.self_mix, own_head),
                (None, None, other_head),
            )
        )
        first, second = jnp.where(chip == 0, ours, theirs), jnp.where(chip == 0, theirs, ours)
        spot = r.self_mixed.at[rows, core_window]
        spot[...] = jnp.concatenate([first, second], axis=1)
        kept.to_self[c] = send(spot, spot, to_core)

    @task(COTANGENT_SEND)
    def _():
        kept.out = Gather(r.out_grad, rows_at(r.grad_out, span))

    @task(COTANGENT_RELAY)
    def _():
        kept.out.relay()

    def out_wait():
        if once(OUT):
            ready(get_og)
            kept.out.wait()

    def cross_rows(c, rows):
        if once(W_SO):
            ready(get_so, get_cq)
        kept.to_self[c].wait_recv()
        after = r.after[rows, :] + mm(r.self_mixed[rows, :], r.all_so[...])
        r.after[rows, :] = after
        normed, rate = normalize(after)
        r.n_cross[rows, :] = normed.astype(BF16)
        r.r_cross[rows, :] = rate
        hidden = (normed * gain_c + shift_c).astype(BF16)
        r.h_cross[rows, :] = hidden
        to_heads(pick(mm(hidden, r.all_cq[:, window])) * HEAD_DIM**-0.5, r.cq, rows)

    def cross_chunk(c, rows):
        heads = attend(
            r.cq, r.mk, r.mv, cross_masked, r.cross_weights, r.cross_mix, rows, src_full
        )
        kept.to_cross[c] = gather_columns(r.cross_parts, c, heads)

    stats = [None] * 6

    def add(name, value):
        value = jnp.sum(value, axis=0, keepdims=True)
        stats[name] = value if stats[name] is None else stats[name] + value

    class Total:
        def __init__(self, c, value):
            self.c = c
            self.keep = part_of(core, half)
            r.sum_send[c] = value.astype(BF16)
            self.step = send(r.sum_send.at[c, part_of(1 - core, half)], r.sum_core.at[c], to_core)

        def second(self):
            self.step.wait_recv()
            r.sum_mid[self.c] = r.sum_send[self.c, self.keep, :] + r.sum_core[self.c]
            self.step = send(r.sum_mid.at[self.c], r.sum_chip.at[self.c], to_chip)

        def third(self):
            self.step.wait_recv()
            r.sum_full[self.c, self.keep, :] = r.sum_mid[self.c] + r.sum_chip[self.c]
            spot = r.sum_full.at[self.c, self.keep]
            self.step = send(spot, spot, to_core)

        def wait(self):
            self.step.wait_recv()
            return r.sum_full[self.c].astype(F32)

    class Scatter:
        def __init__(self, mail, core_in, chip_in):
            self.mail, self.core_in, self.chip_in = mail, core_in, chip_in
            self.steps = [
                send(mail.at[2 * spot + 1 - core], core_in.at[spot], to_core) for spot in range(2)
            ]

        def second(self):
            for step in self.steps:
                step.wait_recv()
            away = 1 - chip
            self.mail[2 * away + core] += self.core_in[away]
            self.step = send(self.mail.at[2 * away + core], self.chip_in, to_chip)

        def wait(self):
            self.step.wait_recv()
            value = self.mail[me].astype(F32) + self.core_in[chip].astype(F32)
            return value + self.chip_in[...].astype(F32)

    lanes = 2 * part

    class Reduce:
        def __init__(self, at, top, length):
            self.group = getattr(r, GROUPS[at // 2])
            self.at = at
            self.rows = pl.ds(top, length)
            self.cols = pl.ds(at % 2 * lanes, lanes)
            self.order = ORDERS[at]
            self.step = 0

        def index(self, last):
            spots = [slice(None)] * 3
            for bit in self.order[: self.step]:
                spots[2 - bit] = bits[bit]
            bit = self.order[self.step]
            spots[2 - bit] = last(bits[bit])
            return tuple(spots) + (self.rows, self.cols)

        def start(self):
            inbox = (r.in_half, r.in_quarter, r.in_eighth)[self.step]
            inbox = inbox.at[(self.at,) + (slice(None),) * (2 - self.step) + (self.rows,)]
            away = self.index(lambda bit: 1 - bit)
            self.copy = send(self.group.at[away], inbox, peers_dp[self.order[self.step]])
            self.inbox = inbox

        def next(self):
            self.copy.wait_recv()
            keep = self.index(lambda bit: bit)
            value = self.group[keep] + self.inbox[...]
            if self.step < 2:
                self.group[keep] = value
                self.step += 1
                self.start()
            else:
                r.b_sums[self.at, me, self.rows, :] = value
                spot = lambda who: r.b_sums.at[self.at, who, self.rows]
                if self.at < STRAIGHT:
                    self.gather = Gather(spot(me), spot)
                else:
                    self.copies = [send(spot(me), spot(me), peer) for peer in peers + [to_far]]

        def relay(self):
            self.gather.relay()

        def wait(self):
            if self.at < STRAIGHT:
                self.gather.wait()
            else:
                for copy in self.copies:
                    copy.wait_recv()
            kept.ended[self.at] = kept.ended.get(self.at, 0) + 1
            if kept.ended[self.at] == CUTS[self.at // 2]:
                store(r.b_sums.at[self.at], r.o_sums.at[self.at])

    def put(group, at, value):
        ref = getattr(r, GROUPS[group])
        value = value.astype(BF16)
        if direct:
            value = value.reshape(2, 2, 2, share, value.shape[-1])
            ref[:, :, :, :, at : at + value.shape[-1]] = value
        else:
            ref[:, at : at + value.shape[-1]] = value

    def feed_up(c, rows):
        if once(W_CO):
            ready(get_co, *([] if direct else get_fi))
        kept.to_cross[c].wait()
        mixed = joined(r.cross_parts, c)
        r.cross_mixed[rows, :] = mixed
        after = r.after[rows, :] + mm(mixed, r.all_co[...])
        r.after[rows, :] = after
        normed, rate = normalize(after)
        r.n_feed[rows, :] = normed.astype(BF16)
        r.r_feed[rows, :] = rate
        hidden = (normed * gain_f + shift_f).astype(BF16)
        r.h_feed[rows, :] = hidden
        upward = mm(hidden, r.own_fi[...])
        bell = 0.5 + 0.5 * lax.erf(upward * 2.0**-0.5)
        r.active[rows, :] = (upward * bell).astype(BF16)
        kept.slope[c] = bell + upward * jnp.exp(-0.5 * upward * upward) * 0.3989422804014327

    def feed_back(c, rows):
        if once(W_FO):
            ready(*get_fo)
        out_wait()
        normed, slope = r.n_feed[rows, :].astype(F32), kept.slope[c]
        grad_up = (mm_t(r.grad_out[rows, :], r.own_fo[...]) * slope).astype(BF16)
        r.grad_up[rows, :] = grad_up
        back = mm_t(grad_up, r.own_fi[...])
        add(4, back * normed)
        add(5, back)
        kept.total[c] = Total(c, back)

    def layer_chunk(c, rows):
        if once(W_FO):
            ready(*get_fo)
        value = mm(r.active[rows, :], r.own_fo[...]).astype(BF16)
        r.layer_mail[2 * c : 2 * c + 2] = value.reshape(2, span, width)

    @task(LAYER_SEND)
    def _():
        kept.layer = Scatter(r.layer_mail, r.layer_core, r.layer_chip)

    @task(LAYER_SECOND)
    def _():
        kept.layer.second()

    @task(LAYER_OUT)
    def _():
        r.b_layer[...] = r.after[own_span, :] + kept.layer.wait()
        store(r.b_layer, r.o_layer)

    @task(GRAD_FO)
    def _():
        out_wait()
        put(0, 0, t_mm(r.active[...], r.grad_out[...]))

    @task(GRAD_FI)
    def _():
        put(1, 0, t_mm(r.h_feed[...], r.grad_up[...]))

    def cross_before(c, rows):
        grad = kept.total[c].wait()
        normed = r.n_feed[rows, :].astype(F32)
        grad = r.grad_out[rows, :].astype(F32) + norm_back(grad, gain_f, normed, r.r_feed[rows, :])
        r.grad_row[rows, :] = grad
        low = grad.astype(BF16)
        r.grad_cross[rows, :] = low
        to_heads(mm_t(low, r.all_co[own_rows, :]).astype(BF16), r.grad_mix, rows)

    def cross_back(c, rows):
        heads = attend_back(
            r.cq, r.mk, r.mv, r.grad_mix, r.cross_weights, r.cross_mix,
            r.grad_mk, r.grad_mv, rows, src_full, c == 0,
        )
        r.grad_cross_rows[rows, :] = jnp.concatenate(heads, axis=1)
        kept.to_rows[c] = gather_columns(r.row_parts, c, heads)

    @task(MEMORY_TERMS)
    def _():
        mk_t = r.grad_mk[...].reshape(part, src_full)
        mv_t = r.grad_mv[...].reshape(part, src_full)
        terms = mm_t(place(mk_t.T.astype(BF16)), r.win_ck[...]) + mm_t(
            place(mv_t.T.astype(BF16)), r.win_cv[...]
        )
        r.mem_mail[...] = terms.astype(BF16).reshape(seq, src_span, width)
        kept.memory = Scatter(r.mem_mail, r.mem_core, r.mem_chip)

    @task(MEMORY_SECOND)
    def _():
        kept.memory.second()

    @task(MEMORY_OUT)
    def _():
        r.b_memory[...] = kept.memory.wait()
        store(r.b_memory, r.o_memory)

    @task(GRAD_CK)
    def _():
        put(2, part, mm(r.grad_mk[...].reshape(part, src_full).astype(BF16), r.mem[...]).T)

    @task(GRAD_CV)
    def _():
        put(2, 2 * part, mm(r.grad_mv[...].reshape(part, src_full).astype(BF16), r.mem[...]).T)

    @task(GRAD_CO)
    def _():
        put(2, 0, pick(t_mm(r.cross_mixed[...], r.grad_cross[:, window])))

    @task(GRAD_CQ)
    def _():
        put(2, 3 * part, t_mm(r.h_cross[...], r.grad_cross_rows[...]))

    def self_before(c, rows):
        kept.to_rows[c].wait()
        grad = mm_t(joined(r.row_parts, c), r.all_cq[...])
        normed = r.n_cross[rows, :].astype(F32)
        add(2, grad * normed)
        add(3, grad)
        grad = r.grad_row[rows, :] + norm_back(grad, gain_c, normed, r.r_cross[rows, :])
        r.grad_row[rows, :] = grad
        to_heads(mm_t(grad.astype(BF16), r.all_so[own_rows, :]).astype(BF16), r.grad_mix, rows)

    def self_back(c, rows):
        heads = attend_back(
            r.q, r.k, r.v, r.grad_mix, r.self_weights, r.self_mix,
            r.grad_k, r.grad_v, rows, rows.stop, c == CHUNKS - 1, own_head,
        )
        r.grad_self_rows[rows, :] = jnp.concatenate(heads, axis=1)

    def put_self(at, value):
        if not direct:
            put(3, at * part, value)
        elif at in (1, 2):
            put(3, (at - 1) * part, value)
        else:
            value = value.astype(BF16).reshape(2, 2, 2, share, part)
            tall = share // 2
            packed = jnp.concatenate([value[:, :, :, :tall], value[:, :, :, tall:]], axis=4)
            top = 0 if at == 0 else tall
            r.g_self[:, :, :, top : top + tall, lanes:] = packed

    @task(GRAD_SO)
    def _():
        put_self(0, pick(t_mm(r.self_mixed[...], r.grad_row[:, window].astype(BF16))))

    @task(GRAD_SQ)
    def _():
        put_self(1, t_mm(r.h_attend[...], r.grad_self_rows[...]))

    @task(GRAD_SK)
    def _():
        put_self(2, mm(r.grad_k[...].reshape(part, full).astype(BF16), r.h_attend[...]).T)

    @task(GRAD_SV)
    def _():
        put_self(3, mm(r.grad_v[...].reshape(part, full).astype(BF16), r.h_attend[...]).T)

    @task(TOKEN_TERMS)
    def _():
        k_t = r.grad_k[...].reshape(part, full)
        v_t = r.grad_v[...].reshape(part, full)
        back = (
            mm_t(place(r.grad_self_rows[...]), r.win_sq[:, own_window])
            + mm_t(place(k_t.T.astype(BF16)), r.win_sk[:, own_window])
            + mm_t(place(v_t.T.astype(BF16)), r.win_sv[:, own_window])
        )
        add(0, back * r.n_attend[...].astype(F32))
        add(1, back)
        r.tok_mail[...] = back.astype(BF16).reshape(seq, span, width)
        kept.tokens = Scatter(r.tok_mail, r.tok_core, r.tok_chip)

    @task(TOKEN_SECOND)
    def _():
        kept.tokens.second()

    @task(TOKEN_OUT)
    def _():
        normed, rate = normalize(r.row[own_span, :].astype(F32))
        grad = kept.tokens.wait()
        r.b_tokens[...] = r.grad_row[own_span, :] + norm_back(grad, gain_a, normed, rate)
        store(r.b_tokens, r.o_tokens)

    class Stats:
        def __init__(self):
            shared = jnp.where(me == 0, 1.0, 0.0)
            rows = stats[:2] + [row * shared for row in stats[2:4]] + stats[4:]
            self.value = jnp.concatenate(rows + [jnp.zeros((2, width), F32)], axis=0)
            self.step = 0
            r.o_stats[...] = self.value

        def start(self):
            r.stat_out[self.step] = self.value
            peer = (peers + peers_dp)[self.step]
            self.copy = send(r.stat_out.at[self.step], r.stat_in.at[self.step], peer)

        def next(self):
            self.copy.wait_recv()
            self.value = self.value + r.stat_in[self.step]
            self.step += 1
            if self.step < 5:
                self.start()
            else:
                r.o_stats[...] = self.value

    @task(NORMS_SEND)
    def _():
        kept.stats = Stats()
        if direct:
            kept.stats.start()

    if direct:
        for level in range(5):
            tasks[NORMS_STEP, level] = lambda: kept.stats.next()

    for c, rows in enumerate(chunks):
        for name, function in (
            (SELF, self_chunk),
            (ROWS, cross_rows),
            (CROSS, cross_chunk),
            (FEED_UP, feed_up),
            (FEED_BACK, feed_back),
            (LAYER, layer_chunk),
            (CROSS_GRAD, cross_before),
            (CROSS_BACK, cross_back),
            (SELF_GRAD, self_before),
            (SELF_BACK, self_back),
        ):
            tasks[name, c] = functools.partial(function, c, rows)
        tasks[CROSS_RELAY, c] = lambda c=c: kept.to_cross[c].relay()
        tasks[ROWS_RELAY, c] = lambda c=c: kept.to_rows[c].relay()
        tasks[TOTAL_SECOND, c] = lambda c=c: kept.total[c].second()
        tasks[TOTAL_THIRD, c] = lambda c=c: kept.total[c].third()

    if direct:
        for at in range(8):
            cuts = CUTS[at // 2]
            for cut in range(cuts):
                one = Reduce(at, cut * (share // cuts), share // cuts)
                for level, function in enumerate(
                    (one.start, one.next, one.next, one.next, one.relay, one.wait)
                ):
                    tasks[at, cut, level] = function

    for name in SCHEDULE:
        if name in tasks:
            tasks[name]()
    finish(list(busy))
    ready(*stores)


def row_call(seq, span, src_span, width, part, units, direct, operands):
    full, src_full = span * seq, src_span * seq
    count, size = part // HEAD_DIM, full // CHUNKS
    half = size // 2
    shapes = dict(
        row=((full, width), BF16),
        mem=((src_full, width), BF16),
        grad_out=((full, width), BF16),
        win_sq=((width, 2 * part), BF16),
        win_sk=((width, 2 * part), BF16),
        win_sv=((width, 2 * part), BF16),
        win_ck=((width, WINDOW), BF16),
        win_cv=((width, WINDOW), BF16),
        all_so=((width, width), BF16),
        all_cq=((width, width), BF16),
        all_co=((width, width), BF16),
        own_fi=((width, units), BF16),
        own_fo=((units, width), BF16),
        self_bias=((full, full), F32),
        target_col=((full, 1), F32),
        cross_code=((1, src_full), F32),
        n_attend=((full, width), BF16),
        n_cross=((full, width), BF16),
        n_feed=((full, width), BF16),
        r_cross=((full, 1), F32),
        r_feed=((full, 1), F32),
        h_attend=((full, width), BF16),
        h_cross=((full, width), BF16),
        h_feed=((full, width), BF16),
        after=((full, width), F32),
        grad_row=((full, width), F32),
        q=((2 * count, full, HEAD_DIM), BF16),
        k=((2 * count, full, HEAD_DIM), BF16),
        v=((2 * count, full, 2 * HEAD_DIM), BF16),
        cq=((count, full, HEAD_DIM), BF16),
        mk=((count, src_full, HEAD_DIM), BF16),
        mv=((count, src_full, 2 * HEAD_DIM), BF16),
        grad_mix=((count, full, HEAD_DIM), BF16),
        self_weights=((count * full, full), BF16),
        cross_weights=((count * full, src_full), BF16),
        self_mix=((count, full, 2 * HEAD_DIM), F32),
        cross_mix=((count, full, 2 * HEAD_DIM), F32),
        grad_k=((count, HEAD_DIM, full), F32),
        grad_v=((count, HEAD_DIM, full), F32),
        grad_mk=((count, HEAD_DIM, src_full), F32),
        grad_mv=((count, HEAD_DIM, src_full), F32),
        cross_parts=((CHUNKS, seq, size + half, 2 * HEAD_DIM), BF16),
        row_parts=((CHUNKS, seq, size + half, 2 * HEAD_DIM), BF16),
        self_mixed=((full, width), BF16),
        cross_mixed=((full, width), BF16),
        active=((full, units), BF16),
        grad_up=((full, units), BF16),
        grad_cross=((full, width), BF16),
        grad_cross_rows=((full, part), BF16),
        grad_self_rows=((full, part), BF16),
        sum_send=((CHUNKS, size, width), BF16),
        sum_core=((CHUNKS, half, width), BF16),
        sum_mid=((CHUNKS, half, width), BF16),
        sum_chip=((CHUNKS, half, width), BF16),
        sum_full=((CHUNKS, size, width), BF16),
        layer_mail=((seq, span, width), BF16),
        layer_core=((2, span, width), BF16),
        layer_chip=((span, width), BF16),
        tok_mail=((seq, span, width), BF16),
        tok_core=((2, span, width), BF16),
        tok_chip=((span, width), BF16),
        b_layer=((span, width), F32),
        b_tokens=((span, width), F32),
        b_memory=((src_span, width), F32),
        mem_mail=((seq, src_span, width), BF16),
        mem_core=((2, src_span, width), BF16),
        mem_chip=((src_span, width), BF16),
    )
    group = (width, 4 * part)
    if direct:
        blocks, share = 8, width // 8
        lanes = 2 * part
        group = (2, 2, 2, share, 4 * part)
        shapes.update({name: (group, BF16) for name in GROUPS})
        shapes.update(
            in_half=((8, 2, 2, share, lanes), BF16),
            in_quarter=((8, 2, share, lanes), BF16),
            in_eighth=((8, share, lanes), BF16),
            b_sums=((8, seq, share, lanes), BF16),
            stat_out=((5, 8, width), F32),
            stat_in=((5, 8, width), F32),
        )
    names = list(shapes) + SEMAPHORES
    scratch = [pltpu.VMEM(shape, dtype) for shape, dtype in shapes.values()]
    scratch += [pltpu.SemaphoreType.DMA((80,)), pltpu.SemaphoreType.DMA((224,)), pltpu.SemaphoreType.DMA((224,))]
    hbm = pl.BlockSpec(memory_space=pl.ANY)
    vmem = pl.BlockSpec(memory_space=pltpu.VMEM)
    smem = pl.BlockSpec(memory_space=pltpu.SMEM)
    outs = [((span, width), F32), ((span, width), F32), ((src_span, width), F32), ((8, width), F32)]
    out_specs = [hbm] * 3 + [vmem]
    if direct:
        outs += [((8, seq, share, lanes), BF16)]
        out_specs += [hbm]
    else:
        outs += [(group, BF16)] * 4
        out_specs += [vmem] * 4
    return pl.pallas_call(
        functools.partial(row_kernel, names, seq, direct),
        out_shape=[jax.ShapeDtypeStruct(s, t) for s, t in outs],
        in_specs=[hbm] * 3 + [vmem] * 2 + [smem] + [hbm] * 10 + [vmem] * 6,
        out_specs=out_specs,
        scratch_shapes=scratch,
        compiler_params=pltpu.CompilerParams(
            collective_id=0, has_side_effects=True, vmem_limit_bytes=64 * 2**20 - 2**17
        ),
    )(*operands)


def final_kernel(seq, dp, layer, tokens, memory, stats, sums, *refs):
    outs, norms, got, passed, built = refs[:13], refs[13:19], refs[19], refs[20:23], refs[23:33]
    in_sems, out_sems = refs[33:]
    sources = [(sums.at[pl.ds(2 * g, 2)], got.at[pl.ds(2 * g, 2)]) for g in range(4)]
    sources += list(zip((memory, layer, tokens), (passed[2], passed[0], passed[1])))
    loads = [pltpu.make_async_copy(*pair, in_sems.at[i]) for i, pair in enumerate(sources)]
    stores = [
        pltpu.make_async_copy(src, dst, out_sems.at[i])
        for i, (src, dst) in enumerate(zip(passed + built, outs))
    ]
    for copy in loads:
        copy.start()
    share, lanes = sums.shape[2:]
    part = lanes // 2
    sq, sk, sv, so, cq, ck, cv, co, fi, fo = built
    width = stats.shape[1]
    back = lax.rem(width - lax.axis_index("dp") * share, width)
    own = pltpu.roll(stats[...], back, 1)[:, :share]
    for i, out in enumerate(norms):
        out[...] = own[i]
    unit = fo.shape[0] // seq
    loads[0].wait()
    for s in range(seq):
        for at in range(2):
            fo[s * unit : (s + 1) * unit, at * lanes : (at + 1) * lanes] = got[at, s].astype(F32)
    stores[12].start()
    loads[1].wait()
    for at in range(2):
        wide = [got[2 + at, s].astype(F32) for s in range(seq)]
        for b in range(dp // 2):
            block = [w[:, b * unit : (b + 1) * unit] for w in wide]
            start = (at * (dp // 2) + b) * seq * unit
            fi[:, start : start + seq * unit] = jnp.concatenate(block, 1)
    stores[11].start()
    loads[2].wait()
    loads[3].wait()
    for i, (out, spot) in enumerate(zip((co, ck, cv, cq, sq, sk), (10, 8, 9, 7, 3, 4))):
        start = i % 2 * part
        block = [got[4 + i // 2, s].astype(F32)[:, start : start + part] for s in (0, 2, 1, 3)]
        out[...] = jnp.concatenate(block, 1)
        stores[spot].start()
    tall = share // 2
    for out, top, spot in ((so, 0, 6), (sv, tall, 5)):
        block = [got[7, s].astype(F32)[top : top + tall] for s in (0, 2, 1, 3)]
        for side in range(2):
            pieces = [piece[:, side * part : (side + 1) * part] for piece in block]
            out[side * tall : (side + 1) * tall, :] = jnp.concatenate(pieces, 1)
        stores[spot].start()
    for copy, place in zip(loads[4:], (2, 0, 1)):
        copy.wait()
        stores[place].start()
    for copy in stores:
        copy.wait()


def final_call(seq, dp, layer, tokens, memory, stats, sums):
    share, width = sums.shape[2], stats.shape[1]
    feed = sums.shape[3] * 2 * seq
    hbm = pl.BlockSpec(memory_space=pl.ANY)
    vmem = pl.BlockSpec(memory_space=pltpu.VMEM)
    shapes = [layer.shape, tokens.shape, memory.shape] + [(share, width)] * 8
    shapes += [(share, feed), (feed // dp, width)] + [(share,)] * 6
    return pl.pallas_call(
        functools.partial(final_kernel, seq, dp),
        out_shape=[jax.ShapeDtypeStruct(shape, F32) for shape in shapes],
        in_specs=[hbm] * 3 + [vmem] + [hbm],
        out_specs=[hbm] * 13 + [vmem] * 6,
        scratch_shapes=[pltpu.VMEM(sums.shape, BF16)]
        + [pltpu.VMEM(shape, F32) for shape in shapes[:13]]
        + [pltpu.SemaphoreType.DMA((7,)), pltpu.SemaphoreType.DMA((13,))],
        compiler_params=pltpu.CompilerParams(vmem_limit_bytes=64 * 2**20 - 2**17),
    )(layer, tokens, memory, stats, sums)


def swap(value, axis, bit):
    size = lax.axis_size(axis)
    return lax.ppermute(value, axis, [(i, i ^ bit) for i in range(size)])


def scatter_sum(value, bits):
    index = lax.axis_index("dp")
    size = lax.axis_size("dp")
    levels = size.bit_length() - 1
    blocks = value.reshape((2,) * levels + value.shape[1:])
    left = list(range(levels))[::-1]
    for bit in bits:
        at = left.index(bit)
        mine = (index >> bit) & 1
        keep = lax.dynamic_index_in_dim(blocks, mine, at, keepdims=False)
        away = lax.dynamic_index_in_dim(blocks, 1 - mine, at, keepdims=False)
        left.pop(at)
        got = swap(away.astype(BF16), "dp", 1 << bit)
        blocks = keep.astype(F32) + got.astype(F32)
    return blocks


def shards(
    tokens,
    memory,
    target_segments,
    memory_segments,
    pad_counts,
    out_grad,
    self_query,
    self_key,
    self_value,
    self_out,
    cross_query,
    cross_key,
    cross_value,
    cross_out,
    feed_in,
    feed_out,
    gain_attend,
    shift_attend,
    gain_cross,
    shift_cross,
    gain_feed,
    shift_feed,
):
    seq, dp = lax.axis_size("seq"), lax.axis_size("dp")
    me = lax.axis_index("seq")
    span, width = tokens.shape[1:]
    part = width // seq
    feed = feed_in.shape[1]
    unit = feed // dp // seq
    direct = dp == 8 and unit == width // dp and unit % 16 == 0
    fi, fo = feed_in, feed_out
    if not direct:
        fi = lax.dynamic_index_in_dim(fi.reshape(width, dp, seq, unit), me, 2, keepdims=False)
        fi = fi.reshape(width, dp * unit)
        fo = lax.dynamic_index_in_dim(fo.reshape(dp, seq, unit, width), me, 1, keepdims=False)
        fo = fo.reshape(dp * unit, width)
    operands = (
        tokens[0], memory[0], out_grad[0], target_segments, memory_segments, pad_counts,
        self_query, self_key, self_value, self_out, cross_query, cross_key, cross_value, cross_out,
        fi, fo, gain_attend, shift_attend, gain_cross, shift_cross, gain_feed, shift_feed,
    )
    results = row_call(seq, span, memory.shape[1], width, part, dp * unit, direct, operands)
    if direct:
        results = final_call(seq, dp, *results)
        return tuple(value[None] for value in results[:3]) + tuple(results[3:])
    layer_out, tokens_grad, memory_grad, stats, g_fo, g_fi, g_cross, g_self = results
    gather = lambda v, axis: lax.all_gather(v, "seq", axis=axis, tiled=True)

    levels = dp.bit_length() - 1
    up = list(range(levels))
    first, second = up, up[1:] + up[:1]
    share = width // dp
    split = lambda v: v.reshape(dp, share, -1)
    groups = ((split(g_fo), first), (split(g_fi), second), (split(g_cross), first), (split(g_self), second))
    summed = [gather(scatter_sum(v, bits).astype(BF16)[None], 0) for v, bits in groups]
    whole_fo = summed[0].reshape(seq * share, width).astype(F32)
    whole_fi = (
        summed[1].reshape(seq, share, dp, unit).transpose(1, 2, 0, 3).reshape(share, feed)
    ).astype(F32)

    def whole(group, at):
        block = group[:, :, at * part : (at + 1) * part]
        block = block.reshape(2, 2, share, part).transpose(2, 1, 0, 3)
        return block.reshape(share, width).astype(F32)

    co, ck, cv, cq = (whole(summed[2], at) for at in range(4))
    so, sq, sk, sv = (whole(summed[3], at) for at in range(4))
    stats = lax.psum(stats, ("seq", "dp"))
    norm_part = lax.dynamic_slice_in_dim(stats, lax.axis_index("dp") * share, share, 1)
    return (
        layer_out[None],
        tokens_grad[None],
        memory_grad[None],
        sq,
        sk,
        sv,
        so,
        cq,
        ck,
        cv,
        co,
        whole_fi,
        whole_fo,
    ) + tuple(norm_part[i] for i in range(6))


def solution(mesh):
    rows = P("dp", "seq", None)
    in_specs = (rows, rows, P("dp", None), P("dp", None), P("dp", None), rows) + (P(),) * 16
    out_specs = (rows,) * 3 + (P("dp", None),) * 10 + (P("dp"),) * 6
    return jax.shard_map(shards, mesh=mesh, in_specs=in_specs, out_specs=out_specs, check_vma=False)
```

```python
import functools

import jax
import jax.numpy as jnp
from jax import lax
from jax.experimental import pallas as pl
from jax.experimental.pallas import tpu as pltpu
from jax.sharding import PartitionSpec as P

HEAD_DIM = 64
EPSILON = 1e-05
NEGATIVE = -1e30
F32 = jnp.float32
BF16 = jnp.bfloat16
MESH = pl.DeviceIdType.MESH
WINDOW = 256
CHUNKS = 2


def mm(left, right):
    return jnp.dot(left, right, preferred_element_type=F32)


def mm_t(left, right):
    return lax.dot_general(left, right, (((1,), (1,)), ((), ())), preferred_element_type=F32)


def t_mm(left, right):
    return lax.dot_general(left, right, (((0,), (0,)), ((), ())), preferred_element_type=F32)


def normalize(values):
    centered = values - jnp.mean(values, axis=-1, keepdims=True)
    rate = lax.rsqrt(jnp.mean(centered * centered, axis=-1, keepdims=True) + EPSILON)
    return centered * rate, rate


def norm_back(grad, gain, normed, rate):
    scaled = grad * gain
    inner = jnp.mean(scaled * normed, axis=-1, keepdims=True)
    return rate * (scaled - jnp.mean(scaled, axis=-1, keepdims=True) - normed * inner)


class Names:
    def __init__(self, names, refs):
        self.__dict__.update(zip(names, refs))


INPUTS = ["tokens", "memory", "out_grad", "target_ids", "memory_ids", "pads"]
INPUTS += ["w_sq", "w_sk", "w_sv", "w_so", "w_cq", "w_ck", "w_cv", "w_co", "w_fi", "w_fo"]
INPUTS += ["gain_a", "shift_a", "gain_c", "shift_c", "gain_f", "shift_f"]
OUTPUTS = ["o_layer", "o_tokens", "o_memory", "o_stats"]
SEMAPHORES = ["load_sem", "send_sem", "recv_sem"]
GROUPS = ["g_fo", "g_fi", "g_cross", "g_self"]
ALONG, ACROSS, MIXED, TURNED = (1, 2, 0), (0, 1, 2), (1, 0, 2), (0, 2, 1)
ORDERS = (ACROSS, ALONG, ALONG, ACROSS, ACROSS, ACROSS, ACROSS, ACROSS)
STRAIGHT = 6
CUTS = (2, 1, 1, 6)
(
    OWN_FI, TOKENS_NEAR, TOKENS_MIDDLE, TOKENS_FAR, MEMORY_NEAR, MEMORY_MIDDLE, MEMORY_FAR, TOKENS_RELAY, MEMORY_RELAY,
    COTANGENT_SEND, COTANGENT_RELAY, LAYER_SEND, LAYER_SECOND, LAYER_OUT, MEMORY_TERMS,
    MEMORY_SECOND, MEMORY_OUT, TOKEN_TERMS, TOKEN_SECOND, TOKEN_OUT, GRAD_FO, GRAD_FI, GRAD_CK,
    GRAD_CV, GRAD_CO, GRAD_CQ, GRAD_SO, GRAD_SQ, GRAD_SK, GRAD_SV, NORMS_SEND,
) = range(31)
(
    SELF, ROWS, CROSS, FEED_UP, FEED_BACK, LAYER, CROSS_GRAD, CROSS_BACK, SELF_GRAD, SELF_BACK,
    CROSS_RELAY, ROWS_RELAY, TOTAL_SECOND, TOTAL_THIRD, NORMS_STEP,
) = range(100, 115)
OUT, W_SO, W_CO, W_FO = range(4)
SCHEDULE = [
    OWN_FI, TOKENS_NEAR, MEMORY_NEAR, TOKENS_RELAY, TOKENS_MIDDLE, TOKENS_FAR, (SELF, 1), (SELF, 0),
    (ROWS, 1), COTANGENT_SEND, (ROWS, 0), MEMORY_RELAY, MEMORY_MIDDLE, MEMORY_FAR, (CROSS, 0),
    (CROSS, 1), COTANGENT_RELAY, (CROSS_RELAY, 0), (FEED_UP, 0), (CROSS_RELAY, 1), (FEED_BACK, 0),
    (FEED_UP, 1), (TOTAL_SECOND, 0), GRAD_FO, (LAYER, 1), (1, 0, 0), (0, 0, 0), (FEED_BACK, 1),
    GRAD_FI, (3, 0, 0), (2, 0, 0), (TOTAL_SECOND, 1), (LAYER, 0), LAYER_SEND, (0, 1, 0), (1, 1, 0),
    (TOTAL_THIRD, 0), LAYER_SECOND, (1, 0, 1), (0, 0, 1), (CROSS_GRAD, 0), (CROSS_BACK, 0),
    (TOTAL_THIRD, 1), (CROSS_GRAD, 1), GRAD_CO, (CROSS_BACK, 1), GRAD_CK, (4, 0, 0), (ROWS_RELAY, 0),
    (1, 1, 1), GRAD_CQ, LAYER_OUT, (1, 0, 2), (3, 0, 1), (0, 1, 1), GRAD_CV, (0, 0, 2), (5, 0, 0),
    MEMORY_TERMS, (ROWS_RELAY, 1), (2, 0, 1), (SELF_GRAD, 0), (1, 1, 2), MEMORY_SECOND, (SELF_GRAD, 1),
    GRAD_SO, (7, 0, 0), (3, 0, 2), (4, 0, 1), (SELF_BACK, 1), (SELF_BACK, 0), GRAD_SK, GRAD_SV,
    (7, 4, 0), (7, 1, 0), (7, 2, 0), TOKEN_TERMS, (7, 3, 0), (0, 1, 2), (5, 0, 1), (1, 0, 3),
    NORMS_SEND, GRAD_SQ, TOKEN_SECOND, (NORMS_STEP, 0), (6, 0, 0), (7, 0, 1), (2, 0, 2), (4, 0, 2),
    MEMORY_OUT, (7, 5, 0), (7, 4, 1), (0, 0, 3), (6, 1, 0), (6, 2, 0), (6, 3, 0), (6, 4, 0), (6, 5, 0),
    (3, 0, 3), (1, 0, 4), (7, 1, 1), (1, 1, 3), (7, 2, 1), (1, 0, 5), (0, 1, 3), (7, 3, 1), (5, 0, 2),
    (7, 0, 2), (6, 0, 1), TOKEN_OUT, (NORMS_STEP, 1), (2, 0, 3), (4, 0, 3), (7, 4, 2), (0, 0, 4),
    (7, 1, 2), (7, 5, 1), (7, 2, 2), (0, 0, 5), (7, 3, 2), (6, 1, 1), (3, 0, 4), (1, 1, 4), (6, 2, 1),
    (3, 0, 5), (0, 1, 4), (5, 0, 3), (6, 0, 2), (6, 3, 1), (1, 1, 5), (7, 0, 3), (0, 1, 5), (7, 4, 3),
    (6, 4, 1), (7, 5, 2), (7, 1, 3), (2, 0, 4), (7, 2, 3), (6, 5, 1), (6, 1, 2), (7, 3, 3),
    (NORMS_STEP, 2), (2, 0, 5), (6, 2, 2), (4, 0, 4), (6, 3, 2), (6, 0, 3), (6, 4, 2), (4, 0, 5),
    (5, 0, 4), (7, 5, 3), (7, 0, 5), (6, 5, 2), (7, 4, 5), (5, 0, 5), (6, 1, 3), (NORMS_STEP, 3),
    (7, 1, 5), (7, 2, 5), (6, 2, 3), (7, 3, 5), (6, 3, 3), (6, 0, 5), (6, 4, 3), (7, 5, 5), (6, 5, 3),
    (6, 1, 5), (6, 2, 5), (NORMS_STEP, 4), (6, 3, 5), (6, 4, 5), (6, 5, 5),
]


def row_kernel(scratch_names, seq, direct, *refs):
    r = Names(INPUTS + OUTPUTS + (["o_sums"] if direct else GROUPS) + scratch_names, refs)
    me = lax.axis_index("seq")
    core = lax.rem(me, 2)
    chip = me // 2
    peer_c = me + 1 - 2 * core
    peer_x = lax.rem(me + 2, 4)
    span = r.tokens.shape[0]
    full, width = r.row.shape
    src_span = r.memory.shape[0]
    src_full = src_span * seq
    part = width // seq
    count = part // HEAD_DIM
    size = full // CHUNKS
    odd = chip
    half_width = 2 * part
    core_window = pl.ds(pl.multiple_of(core * half_width, 128), half_width)
    window = pl.ds(pl.multiple_of(core * half_width + chip * 128, 128), WINDOW)
    own_window = pl.ds(pl.multiple_of(chip * 128, 128), WINDOW)
    own_rows = pl.ds(pl.multiple_of((2 * core + chip) * part, 64), part)
    own_head, other_head = chip * count, (1 - chip) * count
    own_span = pl.ds(pl.multiple_of(me * span, span), span)

    def pick(value):
        return jnp.where(odd == 1, value[:, 64 : 64 + part], value[:, :part])

    def place(value):
        empty = jnp.zeros((value.shape[0], WINDOW - part), value.dtype)
        return jnp.where(
            odd == 1,
            jnp.concatenate([empty, value], 1),
            jnp.concatenate([value, empty], 1),
        )

    loads = []

    def load(src, dst):
        copy = pltpu.make_async_copy(src, dst, r.load_sem.at[len(loads)])
        copy.start()
        loads.append(copy)
        return copy

    stores = []

    def store(src, dst):
        stores.append(load(src, dst))

    def ready(*copies):
        for copy in copies:
            copy.wait()

    place_dp = lax.axis_index("dp")
    peers = [{"seq": peer_c}, {"seq": peer_x}]
    to_core, to_chip = peers
    to_far = {"seq": lax.rem(peer_c + 2, 4)}
    bits, peers_dp = [], []
    if direct:
        for level in range(3):
            bit = lax.rem(place_dp // 2**level, 2)
            bits.append(bit)
            peers_dp.append({"dp": place_dp + 2**level * (1 - 2 * bit)})
    barrier = pltpu.get_barrier_semaphore()
    others = peers + peers_dp + ([to_far] if direct else [])
    for peer in others:
        pl.semaphore_signal(barrier, inc=1, device_id=peer, device_id_type=MESH)

    own_source = pl.ds(pl.multiple_of(me * src_span, src_span), src_span)
    get_tok = load(r.tokens, r.row.at[own_span])
    get_sq = load(r.w_sq.at[:, core_window], r.win_sq)
    get_sk = load(r.w_sk.at[:, core_window], r.win_sk)
    get_sv = load(r.w_sv.at[:, core_window], r.win_sv)
    get_mem = load(r.memory, r.mem.at[own_source])
    get_ck = load(r.w_ck.at[:, window], r.win_ck)
    get_cv = load(r.w_cv.at[:, window], r.win_cv)
    get_fi, get_fo = [], []
    if direct:
        blocks, share = r.g_fo.shape[0] * 4, r.g_fo.shape[3]
        unit = share

        def wide_fi(b):
            spot = pl.ds(pl.multiple_of(b % 4 * WINDOW, WINDOW), WINDOW)
            return r.cross_weights.at[pl.ds(pl.multiple_of(b // 4 * width, width), width), spot]

        for b in range(blocks):
            start = pl.multiple_of(b * (seq * unit) + chip * 128, 128)
            get_fi.append(load(r.w_fi.at[:, pl.ds(start, WINDOW)], wide_fi(b)))
        for b in range(blocks):
            start = pl.multiple_of((b * seq + me) * unit, 16)
            get_fo.append(load(r.w_fo.at[pl.ds(start, unit)], r.own_fo.at[pl.ds(b * unit, unit)]))
    else:
        get_fi = [load(r.w_fi, r.own_fi)]
        get_fo = [load(r.w_fo, r.own_fo)]
    get_so = load(r.w_so, r.all_so)
    get_cq = load(r.w_cq, r.all_cq)
    get_co = load(r.w_co, r.all_co)
    get_og = load(r.out_grad, r.grad_out.at[own_span])

    def column(ids):
        return jnp.broadcast_to(ids.astype(F32), (128, ids.shape[1])).T[:, :1]

    target_ids = r.target_ids[...]
    memory_ids = r.memory_ids[...]
    self_code = jnp.where(
        lax.broadcasted_iota(jnp.int32, (1, full), 1) < full - r.pads[0, 0], target_ids, -1
    ).astype(F32)
    cross_code = jnp.where(
        lax.broadcasted_iota(jnp.int32, (1, src_full), 1) < src_full - r.pads[0, 1], memory_ids, -1
    ).astype(F32)
    target_col = column(target_ids)
    r.target_col[...] = target_col

    def bias_rows(at, carry):
        rows = pl.ds(pl.multiple_of(at * span, span), span)
        i_pos = lax.broadcasted_iota(jnp.int32, (span, full), 0) + at * span
        j_pos = lax.broadcasted_iota(jnp.int32, (span, full), 1)
        same = r.target_col[rows, :] == self_code
        r.self_bias[rows, :] = jnp.where((same & (j_pos <= i_pos)) | (i_pos == j_pos), 0.0, NEGATIVE)
        return carry

    lax.fori_loop(0, seq, bias_rows, 0)
    r.cross_code[...] = cross_code

    def self_masked(scores, rows, reach):
        return scores + r.self_bias[rows, :reach]

    def cross_masked(scores, rows, reach):
        return jnp.where(r.target_col[rows, :] == r.cross_code[:, :reach], scores, NEGATIVE)

    gain_a, shift_a, gain_c, shift_c, gain_f, shift_f = (
        getattr(r, name)[...].astype(F32).reshape(1, width) for name in INPUTS[-6:]
    )
    pl.semaphore_wait(barrier, len(others))

    sent, busy = [], []

    def send(src, dst, peer):
        at = len(sent)
        copy = pltpu.make_async_remote_copy(
            src_ref=src,
            dst_ref=dst,
            send_sem=r.send_sem.at[at],
            recv_sem=r.recv_sem.at[at],
            device_id=peer,
            device_id_type=MESH,
        )
        copy.start()
        sent.append(copy)
        busy.append(copy)
        return copy

    def finish(copies):
        for copy in copies:
            copy.wait_send()
            busy[:] = [other for other in busy if other is not copy]

    class Gather:
        def __init__(self, src, spot):
            self.spot = spot
            self.x = send(src, spot(me), to_chip)
            self.c = send(src, spot(me), to_core)

        def near(self):
            self.c.wait_recv()

        def relay(self):
            self.x.wait_recv()
            self.second = send(self.spot(peer_x), self.spot(peer_x), to_core)

        def far(self):
            self.second.wait_recv()

        def wait(self):
            self.near()
            self.far()

    def rows_at(ref, length):
        return lambda who: ref.at[pl.ds(pl.multiple_of(who * length, length), length)]

    tok = Gather(r.tokens, rows_at(r.row, span))
    mem = Gather(r.memory, rows_at(r.mem, src_span))
    tasks = {}

    class kept:
        to_self, to_cross, to_rows, total, slope, ended = {}, {}, {}, {}, {}, {}
        seen = set()

    def once(what):
        first = what not in kept.seen
        kept.seen.add(what)
        return first

    def task(name):
        def keep(function):
            tasks[name] = function

        return keep

    @task(OWN_FI)
    def _():
        if not direct:
            return
        from_row = lax.broadcasted_iota(jnp.int32, (WINDOW, WINDOW), 0)
        to_col = lax.broadcasted_iota(jnp.int32, (WINDOW, WINDOW), 1)
        skip = me * unit - chip * 128
        ready(*get_fi)
        def tile(t, carry):
            total = None
            for near in range(4):
                b = 2 * t + near
                at = to_col + (t * WINDOW - b * unit)
                chosen = (from_row == at + skip) & (at >= 0) & (at < unit)
                term = mm(wide_fi(b)[...], jnp.where(chosen, 1.0, 0.0).astype(BF16))
                total = term if total is None else total + term
            r.own_fi[:, pl.ds(pl.multiple_of(t * WINDOW, WINDOW), WINDOW)] = total.astype(BF16)
            return carry

        lax.fori_loop(0, blocks * unit // WINDOW, tile, 0)

    def to_heads(value, ref, rows):
        ones = jnp.ones((value.shape[0], HEAD_DIM), ref.dtype)
        for h in range(value.shape[1] // HEAD_DIM):
            head = value[:, h * HEAD_DIM : (h + 1) * HEAD_DIM].astype(ref.dtype)
            ref[h, rows, :] = head if ref.shape[2] == HEAD_DIM else jnp.concatenate([head, ones], 1)

    def part_of(who, length):
        return pl.ds(pl.multiple_of(who * length, length), length)

    def project_tokens(rows):
        row = r.row[rows, :].astype(F32)
        normed, _ = normalize(row)
        r.n_attend[rows, :] = normed.astype(BF16)
        hidden = (normed * gain_a + shift_a).astype(BF16)
        r.h_attend[rows, :] = hidden
        r.after[rows, :] = row
        to_heads(mm(hidden, r.win_sq[...]) * HEAD_DIM**-0.5, r.q, rows)
        to_heads(mm(hidden, r.win_sk[...]), r.k, rows)
        to_heads(mm(hidden, r.win_sv[...]), r.v, rows)

    def project_memory(rows):
        source = r.mem[rows, :]
        to_heads(pick(mm(source, r.win_ck[...])), r.mk, rows)
        to_heads(pick(mm(source, r.win_cv[...])), r.mv, rows)

    @task(TOKENS_NEAR)
    def _():
        ready(get_tok, get_sq, get_sk, get_sv)
        tok.near()
        project_tokens(part_of(chip, full // 2))

    @task(MEMORY_NEAR)
    def _():
        ready(get_mem, get_ck, get_cv)
        mem.near()
        project_memory(part_of(chip, src_full // 2))

    tasks[TOKENS_RELAY] = tok.relay

    @task(TOKENS_MIDDLE)
    def _():
        project_tokens(part_of(peer_x, span))

    @task(TOKENS_FAR)
    def _():
        tok.far()
        project_tokens(part_of(3 - me, span))

    tasks[MEMORY_RELAY] = mem.relay

    @task(MEMORY_MIDDLE)
    def _():
        project_memory(part_of(peer_x, src_span))

    @task(MEMORY_FAR)
    def _():
        mem.far()
        project_memory(part_of(3 - me, src_span))

    def attend(q, k, v, masked, weights, mixed, rows, reach, base=0):
        def one(h):
            scores = masked(mm_t(q[base + h, rows, :], k[base + h, :reach, :]), rows, reach)
            highest = jnp.max(scores, axis=-1, keepdims=True)
            low = jnp.exp(scores - highest).astype(BF16)
            product = mm(low, v[base + h, :reach, :])
            over = 1.0 / product[:, HEAD_DIM : HEAD_DIM + 1]
            head = product[:, :HEAD_DIM] * over
            if weights is not None:
                weights[h * full + rows.start : h * full + rows.stop, :reach] = low
                mixed[h, rows, HEAD_DIM : HEAD_DIM + 1] = over
                mixed[h, rows, :HEAD_DIM] = head
            return head.astype(BF16)

        return [one(h) for h in range(count)]

    def attend_back(q, k, v, grad, weights, mixed, dk, dv, rows, reach, first, base=0):
        def one(h):
            scaled = grad[h, rows, :].astype(F32) * mixed[h, rows, HEAD_DIM : HEAD_DIM + 1]
            inner = jnp.sum(scaled * mixed[h, rows, :HEAD_DIM], axis=-1, keepdims=True)
            low = scaled.astype(BF16)
            exponent = weights[h * full + rows.start : h * full + rows.stop, :reach]
            grad_weights = mm_t(low, v[base + h, :reach, :HEAD_DIM])
            grad_scores = (exponent.astype(F32) * (grad_weights - inner)).astype(BF16)
            grad_q = mm(grad_scores, k[base + h, :reach, :]) * HEAD_DIM**-0.5
            more_k = mm(q[base + h, rows, :].T, grad_scores)
            more_v = mm(low.T, exponent)
            if first:
                dk[h, :, :reach] = more_k
                dv[h, :, :reach] = more_v
            else:
                dk[h, :, :reach] += more_k
                dv[h, :, :reach] += more_v
            return grad_q.astype(BF16)

        return [one(h) for h in range(count)]

    chunks = [slice(c * size, (c + 1) * size) for c in range(CHUNKS)]
    half = size // 2

    def gather_columns(buffer, c, heads):
        buffer[c, me, :size, :] = jnp.concatenate(heads[:2], axis=1)
        buffer[c, me, size:, :] = jnp.concatenate([heads[2][:half], heads[2][half:]], axis=1)
        return Gather(buffer.at[c, me], lambda who: buffer.at[c, who])

    def joined(buffer, c):
        pieces = []
        for s in (0, 2, 1, 3):
            last = buffer[c, s, size:, :]
            pieces.append(buffer[c, s, :size, :])
            pieces.append(jnp.concatenate([last[:, :HEAD_DIM], last[:, HEAD_DIM:]], axis=0))
        return jnp.concatenate(pieces, axis=1)

    def self_chunk(c, rows):
        ours, theirs = (
            jnp.concatenate(attend(r.q, r.k, r.v, self_masked, weights, mix, rows, rows.stop, base), 1)
            for weights, mix, base in (
                (r.self_weights, r.self_mix, own_head),
                (None, None, other_head),
            )
        )
        first, second = jnp.where(chip == 0, ours, theirs), jnp.where(chip == 0, theirs, ours)
        spot = r.self_mixed.at[rows, core_window]
        spot[...] = jnp.concatenate([first, second], axis=1)
        kept.to_self[c] = send(spot, spot, to_core)

    @task(COTANGENT_SEND)
    def _():
        kept.out = Gather(r.out_grad, rows_at(r.grad_out, span))

    @task(COTANGENT_RELAY)
    def _():
        kept.out.relay()

    def out_wait():
        if once(OUT):
            ready(get_og)
            kept.out.wait()

    def cross_rows(c, rows):
        if once(W_SO):
            ready(get_so, get_cq)
        kept.to_self[c].wait_recv()
        after = r.after[rows, :] + mm(r.self_mixed[rows, :], r.all_so[...])
        r.after[rows, :] = after
        normed, rate = normalize(after)
        r.n_cross[rows, :] = normed.astype(BF16)
        r.r_cross[rows, :] = rate
        hidden = (normed * gain_c + shift_c).astype(BF16)
        r.h_cross[rows, :] = hidden
        to_heads(pick(mm(hidden, r.all_cq[:, window])) * HEAD_DIM**-0.5, r.cq, rows)

    def cross_chunk(c, rows):
        heads = attend(
            r.cq, r.mk, r.mv, cross_masked, r.cross_weights, r.cross_mix, rows, src_full
        )
        kept.to_cross[c] = gather_columns(r.cross_parts, c, heads)

    stats = [None] * 6

    def add(name, value):
        value = jnp.sum(value, axis=0, keepdims=True)
        stats[name] = value if stats[name] is None else stats[name] + value

    class Total:
        def __init__(self, c, value):
            self.c = c
            self.keep = part_of(core, half)
            r.sum_send[c] = value.astype(BF16)
            self.step = send(r.sum_send.at[c, part_of(1 - core, half)], r.sum_core.at[c], to_core)

        def second(self):
            self.step.wait_recv()
            r.sum_mid[self.c] = r.sum_send[self.c, self.keep, :] + r.sum_core[self.c]
            self.step = send(r.sum_mid.at[self.c], r.sum_chip.at[self.c], to_chip)

        def third(self):
            self.step.wait_recv()
            r.sum_full[self.c, self.keep, :] = r.sum_mid[self.c] + r.sum_chip[self.c]
            spot = r.sum_full.at[self.c, self.keep]
            self.step = send(spot, spot, to_core)

        def wait(self):
            self.step.wait_recv()
            return r.sum_full[self.c].astype(F32)

    class Scatter:
        def __init__(self, mail, core_in, chip_in):
            self.mail, self.core_in, self.chip_in = mail, core_in, chip_in
            self.steps = [
                send(mail.at[2 * spot + 1 - core], core_in.at[spot], to_core) for spot in range(2)
            ]

        def second(self):
            for step in self.steps:
                step.wait_recv()
            away = 1 - chip
            self.mail[2 * away + core] += self.core_in[away]
            self.step = send(self.mail.at[2 * away + core], self.chip_in, to_chip)

        def wait(self):
            self.step.wait_recv()
            value = self.mail[me].astype(F32) + self.core_in[chip].astype(F32)
            return value + self.chip_in[...].astype(F32)

    lanes = 2 * part

    class Reduce:
        def __init__(self, at, top, length):
            self.group = getattr(r, GROUPS[at // 2])
            self.at = at
            self.rows = pl.ds(top, length)
            self.cols = pl.ds(at % 2 * lanes, lanes)
            self.order = ORDERS[at]
            self.step = 0

        def index(self, last):
            spots = [slice(None)] * 3
            for bit in self.order[: self.step]:
                spots[2 - bit] = bits[bit]
            bit = self.order[self.step]
            spots[2 - bit] = last(bits[bit])
            return tuple(spots) + (self.rows, self.cols)

        def start(self):
            inbox = (r.in_half, r.in_quarter, r.in_eighth)[self.step]
            inbox = inbox.at[(self.at,) + (slice(None),) * (2 - self.step) + (self.rows,)]
            away = self.index(lambda bit: 1 - bit)
            self.copy = send(self.group.at[away], inbox, peers_dp[self.order[self.step]])
            self.inbox = inbox

        def next(self):
            self.copy.wait_recv()
            keep = self.index(lambda bit: bit)
            value = self.group[keep] + self.inbox[...]
            if self.step < 2:
                self.group[keep] = value
                self.step += 1
                self.start()
            else:
                r.b_sums[self.at, me, self.rows, :] = value
                spot = lambda who: r.b_sums.at[self.at, who, self.rows]
                if self.at < STRAIGHT:
                    self.gather = Gather(spot(me), spot)
                else:
                    self.copies = [send(spot(me), spot(me), peer) for peer in peers + [to_far]]

        def relay(self):
            self.gather.relay()

        def wait(self):
            if self.at < STRAIGHT:
                self.gather.wait()
            else:
                for copy in self.copies:
                    copy.wait_recv()
            kept.ended[self.at] = kept.ended.get(self.at, 0) + 1
            if kept.ended[self.at] == CUTS[self.at // 2]:
                store(r.b_sums.at[self.at], r.o_sums.at[self.at])

    def put(group, at, value):
        ref = getattr(r, GROUPS[group])
        value = value.astype(BF16)
        if direct:
            value = value.reshape(2, 2, 2, share, value.shape[-1])
            ref[:, :, :, :, at : at + value.shape[-1]] = value
        else:
            ref[:, at : at + value.shape[-1]] = value

    def feed_up(c, rows):
        if once(W_CO):
            ready(get_co, *([] if direct else get_fi))
        kept.to_cross[c].wait()
        mixed = joined(r.cross_parts, c)
        r.cross_mixed[rows, :] = mixed
        after = r.after[rows, :] + mm(mixed, r.all_co[...])
        r.after[rows, :] = after
        normed, rate = normalize(after)
        r.n_feed[rows, :] = normed.astype(BF16)
        r.r_feed[rows, :] = rate
        hidden = (normed * gain_f + shift_f).astype(BF16)
        r.h_feed[rows, :] = hidden
        upward = mm(hidden, r.own_fi[...])
        bell = 0.5 + 0.5 * lax.erf(upward * 2.0**-0.5)
        r.active[rows, :] = (upward * bell).astype(BF16)
        kept.slope[c] = bell + upward * jnp.exp(-0.5 * upward * upward) * 0.3989422804014327

    def feed_back(c, rows):
        if once(W_FO):
            ready(*get_fo)
        out_wait()
        normed, slope = r.n_feed[rows, :].astype(F32), kept.slope[c]
        grad_up = (mm_t(r.grad_out[rows, :], r.own_fo[...]) * slope).astype(BF16)
        r.grad_up[rows, :] = grad_up
        back = mm_t(grad_up, r.own_fi[...])
        add(4, back * normed)
        add(5, back)
        kept.total[c] = Total(c, back)

    def layer_chunk(c, rows):
        if once(W_FO):
            ready(*get_fo)
        value = mm(r.active[rows, :], r.own_fo[...]).astype(BF16)
        r.layer_mail[2 * c : 2 * c + 2] = value.reshape(2, span, width)

    @task(LAYER_SEND)
    def _():
        kept.layer = Scatter(r.layer_mail, r.layer_core, r.layer_chip)

    @task(LAYER_SECOND)
    def _():
        kept.layer.second()

    @task(LAYER_OUT)
    def _():
        r.b_layer[...] = r.after[own_span, :] + kept.layer.wait()
        store(r.b_layer, r.o_layer)

    @task(GRAD_FO)
    def _():
        out_wait()
        put(0, 0, t_mm(r.active[...], r.grad_out[...]))

    @task(GRAD_FI)
    def _():
        put(1, 0, t_mm(r.h_feed[...], r.grad_up[...]))

    def cross_before(c, rows):
        grad = kept.total[c].wait()
        normed = r.n_feed[rows, :].astype(F32)
        grad = r.grad_out[rows, :].astype(F32) + norm_back(grad, gain_f, normed, r.r_feed[rows, :])
        r.grad_row[rows, :] = grad
        low = grad.astype(BF16)
        r.grad_cross[rows, :] = low
        to_heads(mm_t(low, r.all_co[own_rows, :]).astype(BF16), r.grad_mix, rows)

    def cross_back(c, rows):
        heads = attend_back(
            r.cq, r.mk, r.mv, r.grad_mix, r.cross_weights, r.cross_mix,
            r.grad_mk, r.grad_mv, rows, src_full, c == 0,
        )
        r.grad_cross_rows[rows, :] = jnp.concatenate(heads, axis=1)
        kept.to_rows[c] = gather_columns(r.row_parts, c, heads)

    @task(MEMORY_TERMS)
    def _():
        mk_t = r.grad_mk[...].reshape(part, src_full)
        mv_t = r.grad_mv[...].reshape(part, src_full)
        terms = mm_t(place(mk_t.T.astype(BF16)), r.win_ck[...]) + mm_t(
            place(mv_t.T.astype(BF16)), r.win_cv[...]
        )
        r.mem_mail[...] = terms.astype(BF16).reshape(seq, src_span, width)
        kept.memory = Scatter(r.mem_mail, r.mem_core, r.mem_chip)

    @task(MEMORY_SECOND)
    def _():
        kept.memory.second()

    @task(MEMORY_OUT)
    def _():
        r.b_memory[...] = kept.memory.wait()
        store(r.b_memory, r.o_memory)

    @task(GRAD_CK)
    def _():
        put(2, part, mm(r.grad_mk[...].reshape(part, src_full).astype(BF16), r.mem[...]).T)

    @task(GRAD_CV)
    def _():
        put(2, 2 * part, mm(r.grad_mv[...].reshape(part, src_full).astype(BF16), r.mem[...]).T)

    @task(GRAD_CO)
    def _():
        put(2, 0, pick(t_mm(r.cross_mixed[...], r.grad_cross[:, window])))

    @task(GRAD_CQ)
    def _():
        put(2, 3 * part, t_mm(r.h_cross[...], r.grad_cross_rows[...]))

    def self_before(c, rows):
        kept.to_rows[c].wait()
        grad = mm_t(joined(r.row_parts, c), r.all_cq[...])
        normed = r.n_cross[rows, :].astype(F32)
        add(2, grad * normed)
        add(3, grad)
        grad = r.grad_row[rows, :] + norm_back(grad, gain_c, normed, r.r_cross[rows, :])
        r.grad_row[rows, :] = grad
        to_heads(mm_t(grad.astype(BF16), r.all_so[own_rows, :]).astype(BF16), r.grad_mix, rows)

    def self_back(c, rows):
        heads = attend_back(
            r.q, r.k, r.v, r.grad_mix, r.self_weights, r.self_mix,
            r.grad_k, r.grad_v, rows, rows.stop, c == CHUNKS - 1, own_head,
        )
        r.grad_self_rows[rows, :] = jnp.concatenate(heads, axis=1)

    def put_self(at, value):
        if not direct:
            put(3, at * part, value)
        elif at in (1, 2):
            put(3, (at - 1) * part, value)
        else:
            value = value.astype(BF16).reshape(2, 2, 2, share, part)
            tall = share // 2
            packed = jnp.concatenate([value[:, :, :, :tall], value[:, :, :, tall:]], axis=4)
            top = 0 if at == 0 else tall
            r.g_self[:, :, :, top : top + tall, lanes:] = packed

    @task(GRAD_SO)
    def _():
        put_self(0, pick(t_mm(r.self_mixed[...], r.grad_row[:, window].astype(BF16))))

    @task(GRAD_SQ)
    def _():
        put_self(1, t_mm(r.h_attend[...], r.grad_self_rows[...]))

    @task(GRAD_SK)
    def _():
        put_self(2, mm(r.grad_k[...].reshape(part, full).astype(BF16), r.h_attend[...]).T)

    @task(GRAD_SV)
    def _():
        put_self(3, mm(r.grad_v[...].reshape(part, full).astype(BF16), r.h_attend[...]).T)

    @task(TOKEN_TERMS)
    def _():
        k_t = r.grad_k[...].reshape(part, full)
        v_t = r.grad_v[...].reshape(part, full)
        back = (
            mm_t(place(r.grad_self_rows[...]), r.win_sq[:, own_window])
            + mm_t(place(k_t.T.astype(BF16)), r.win_sk[:, own_window])
            + mm_t(place(v_t.T.astype(BF16)), r.win_sv[:, own_window])
        )
        add(0, back * r.n_attend[...].astype(F32))
        add(1, back)
        r.tok_mail[...] = back.astype(BF16).reshape(seq, span, width)
        kept.tokens = Scatter(r.tok_mail, r.tok_core, r.tok_chip)

    @task(TOKEN_SECOND)
    def _():
        kept.tokens.second()

    @task(TOKEN_OUT)
    def _():
        normed, rate = normalize(r.row[own_span, :].astype(F32))
        grad = kept.tokens.wait()
        r.b_tokens[...] = r.grad_row[own_span, :] + norm_back(grad, gain_a, normed, rate)
        store(r.b_tokens, r.o_tokens)

    class Stats:
        def __init__(self):
            shared = jnp.where(me == 0, 1.0, 0.0)
            rows = stats[:2] + [row * shared for row in stats[2:4]] + stats[4:]
            self.value = jnp.concatenate(rows + [jnp.zeros((2, width), F32)], axis=0)
            self.step = 0
            r.o_stats[...] = self.value

        def start(self):
            r.stat_out[self.step] = self.value
            peer = (peers + peers_dp)[self.step]
            self.copy = send(r.stat_out.at[self.step], r.stat_in.at[self.step], peer)

        def next(self):
            self.copy.wait_recv()
            self.value = self.value + r.stat_in[self.step]
            self.step += 1
            if self.step < 5:
                self.start()
            else:
                r.o_stats[...] = self.value

    @task(NORMS_SEND)
    def _():
        kept.stats = Stats()
        if direct:
            kept.stats.start()

    if direct:
        for level in range(5):
            tasks[NORMS_STEP, level] = lambda: kept.stats.next()

    for c, rows in enumerate(chunks):
        for name, function in (
            (SELF, self_chunk),
            (ROWS, cross_rows),
            (CROSS, cross_chunk),
            (FEED_UP, feed_up),
            (FEED_BACK, feed_back),
            (LAYER, layer_chunk),
            (CROSS_GRAD, cross_before),
            (CROSS_BACK, cross_back),
            (SELF_GRAD, self_before),
            (SELF_BACK, self_back),
        ):
            tasks[name, c] = functools.partial(function, c, rows)
        tasks[CROSS_RELAY, c] = lambda c=c: kept.to_cross[c].relay()
        tasks[ROWS_RELAY, c] = lambda c=c: kept.to_rows[c].relay()
        tasks[TOTAL_SECOND, c] = lambda c=c: kept.total[c].second()
        tasks[TOTAL_THIRD, c] = lambda c=c: kept.total[c].third()

    if direct:
        for at in range(8):
            cuts = CUTS[at // 2]
            for cut in range(cuts):
                one = Reduce(at, cut * (share // cuts), share // cuts)
                for level, function in enumerate(
                    (one.start, one.next, one.next, one.next, one.relay, one.wait)
                ):
                    tasks[at, cut, level] = function

    for name in SCHEDULE:
        if name in tasks:
            tasks[name]()
    finish(list(busy))
    ready(*stores)


def row_call(seq, span, src_span, width, part, units, direct, operands):
    full, src_full = span * seq, src_span * seq
    count, size = part // HEAD_DIM, full // CHUNKS
    half = size // 2
    shapes = dict(
        row=((full, width), BF16),
        mem=((src_full, width), BF16),
        grad_out=((full, width), BF16),
        win_sq=((width, 2 * part), BF16),
        win_sk=((width, 2 * part), BF16),
        win_sv=((width, 2 * part), BF16),
        win_ck=((width, WINDOW), BF16),
        win_cv=((width, WINDOW), BF16),
        all_so=((width, width), BF16),
        all_cq=((width, width), BF16),
        all_co=((width, width), BF16),
        own_fi=((width, units), BF16),
        own_fo=((units, width), BF16),
        self_bias=((full, full), F32),
        target_col=((full, 1), F32),
        cross_code=((1, src_full), F32),
        n_attend=((full, width), BF16),
        n_cross=((full, width), BF16),
        n_feed=((full, width), BF16),
        r_cross=((full, 1), F32),
        r_feed=((full, 1), F32),
        h_attend=((full, width), BF16),
        h_cross=((full, width), BF16),
        h_feed=((full, width), BF16),
        after=((full, width), F32),
        grad_row=((full, width), F32),
        q=((2 * count, full, HEAD_DIM), BF16),
        k=((2 * count, full, HEAD_DIM), BF16),
        v=((2 * count, full, 2 * HEAD_DIM), BF16),
        cq=((count, full, HEAD_DIM), BF16),
        mk=((count, src_full, HEAD_DIM), BF16),
        mv=((count, src_full, 2 * HEAD_DIM), BF16),
        grad_mix=((count, full, HEAD_DIM), BF16),
        self_weights=((count * full, full), BF16),
        cross_weights=((count * full, src_full), BF16),
        self_mix=((count, full, 2 * HEAD_DIM), F32),
        cross_mix=((count, full, 2 * HEAD_DIM), F32),
        grad_k=((count, HEAD_DIM, full), F32),
        grad_v=((count, HEAD_DIM, full), F32),
        grad_mk=((count, HEAD_DIM, src_full), F32),
        grad_mv=((count, HEAD_DIM, src_full), F32),
        cross_parts=((CHUNKS, seq, size + half, 2 * HEAD_DIM), BF16),
        row_parts=((CHUNKS, seq, size + half, 2 * HEAD_DIM), BF16),
        self_mixed=((full, width), BF16),
        cross_mixed=((full, width), BF16),
        active=((full, units), BF16),
        grad_up=((full, units), BF16),
        grad_cross=((full, width), BF16),
        grad_cross_rows=((full, part), BF16),
        grad_self_rows=((full, part), BF16),
        sum_send=((CHUNKS, size, width), BF16),
        sum_core=((CHUNKS, half, width), BF16),
        sum_mid=((CHUNKS, half, width), BF16),
        sum_chip=((CHUNKS, half, width), BF16),
        sum_full=((CHUNKS, size, width), BF16),
        layer_mail=((seq, span, width), BF16),
        layer_core=((2, span, width), BF16),
        layer_chip=((span, width), BF16),
        tok_mail=((seq, span, width), BF16),
        tok_core=((2, span, width), BF16),
        tok_chip=((span, width), BF16),
        b_layer=((span, width), F32),
        b_tokens=((span, width), F32),
        b_memory=((src_span, width), F32),
        mem_mail=((seq, src_span, width), BF16),
        mem_core=((2, src_span, width), BF16),
        mem_chip=((src_span, width), BF16),
    )
    group = (width, 4 * part)
    if direct:
        blocks, share = 8, width // 8
        lanes = 2 * part
        group = (2, 2, 2, share, 4 * part)
        shapes.update({name: (group, BF16) for name in GROUPS})
        shapes.update(
            in_half=((8, 2, 2, share, lanes), BF16),
            in_quarter=((8, 2, share, lanes), BF16),
            in_eighth=((8, share, lanes), BF16),
            b_sums=((8, seq, share, lanes), BF16),
            stat_out=((5, 8, width), F32),
            stat_in=((5, 8, width), F32),
        )
    names = list(shapes) + SEMAPHORES
    scratch = [pltpu.VMEM(shape, dtype) for shape, dtype in shapes.values()]
    scratch += [pltpu.SemaphoreType.DMA((80,)), pltpu.SemaphoreType.DMA((224,)), pltpu.SemaphoreType.DMA((224,))]
    hbm = pl.BlockSpec(memory_space=pl.ANY)
    vmem = pl.BlockSpec(memory_space=pltpu.VMEM)
    smem = pl.BlockSpec(memory_space=pltpu.SMEM)
    outs = [((span, width), F32), ((span, width), F32), ((src_span, width), F32), ((8, width), F32)]
    out_specs = [hbm] * 3 + [vmem]
    if direct:
        outs += [((8, seq, share, lanes), BF16)]
        out_specs += [hbm]
    else:
        outs += [(group, BF16)] * 4
        out_specs += [vmem] * 4
    return pl.pallas_call(
        functools.partial(row_kernel, names, seq, direct),
        out_shape=[jax.ShapeDtypeStruct(s, t) for s, t in outs],
        in_specs=[hbm] * 3 + [vmem] * 2 + [smem] + [hbm] * 10 + [vmem] * 6,
        out_specs=out_specs,
        scratch_shapes=scratch,
        compiler_params=pltpu.CompilerParams(
            collective_id=0, has_side_effects=True, vmem_limit_bytes=64 * 2**20 - 2**17
        ),
    )(*operands)


def final_kernel(seq, dp, layer, tokens, memory, stats, sums, *refs):
    outs, norms, got, passed, built = refs[:13], refs[13:19], refs[19], refs[20:23], refs[23:33]
    in_sems, out_sems = refs[33:]
    sources = [(sums.at[pl.ds(2 * g, 2)], got.at[pl.ds(2 * g, 2)]) for g in range(4)]
    sources += list(zip((memory, layer, tokens), (passed[2], passed[0], passed[1])))
    loads = [pltpu.make_async_copy(*pair, in_sems.at[i]) for i, pair in enumerate(sources)]
    stores = [
        pltpu.make_async_copy(src, dst, out_sems.at[i])
        for i, (src, dst) in enumerate(zip(passed + built, outs))
    ]
    for copy in loads:
        copy.start()
    share, lanes = sums.shape[2:]
    part = lanes // 2
    sq, sk, sv, so, cq, ck, cv, co, fi, fo = built
    width = stats.shape[1]
    back = lax.rem(width - lax.axis_index("dp") * share, width)
    own = pltpu.roll(stats[...], back, 1)[:, :share]
    for i, out in enumerate(norms):
        out[...] = own[i]
    unit = fo.shape[0] // seq
    loads[0].wait()
    for s in range(seq):
        for at in range(2):
            fo[s * unit : (s + 1) * unit, at * lanes : (at + 1) * lanes] = got[at, s].astype(F32)
    stores[12].start()
    loads[1].wait()
    for at in range(2):
        wide = [got[2 + at, s].astype(F32) for s in range(seq)]
        for b in range(dp // 2):
            block = [w[:, b * unit : (b + 1) * unit] for w in wide]
            start = (at * (dp // 2) + b) * seq * unit
            fi[:, start : start + seq * unit] = jnp.concatenate(block, 1)
    stores[11].start()
    loads[2].wait()
    loads[3].wait()
    for i, (out, spot) in enumerate(zip((co, ck, cv, cq, sq, sk), (10, 8, 9, 7, 3, 4))):
        start = i % 2 * part
        block = [got[4 + i // 2, s].astype(F32)[:, start : start + part] for s in (0, 2, 1, 3)]
        out[...] = jnp.concatenate(block, 1)
        stores[spot].start()
    tall = share // 2
    for out, top, spot in ((so, 0, 6), (sv, tall, 5)):
        block = [got[7, s].astype(F32)[top : top + tall] for s in (0, 2, 1, 3)]
        for side in range(2):
            pieces = [piece[:, side * part : (side + 1) * part] for piece in block]
            out[side * tall : (side + 1) * tall, :] = jnp.concatenate(pieces, 1)
        stores[spot].start()
    for copy, place in zip(loads[4:], (2, 0, 1)):
        copy.wait()
        stores[place].start()
    for copy in stores:
        copy.wait()


def final_call(seq, dp, layer, tokens, memory, stats, sums):
    share, width = sums.shape[2], stats.shape[1]
    feed = sums.shape[3] * 2 * seq
    hbm = pl.BlockSpec(memory_space=pl.ANY)
    vmem = pl.BlockSpec(memory_space=pltpu.VMEM)
    shapes = [layer.shape, tokens.shape, memory.shape] + [(share, width)] * 8
    shapes += [(share, feed), (feed // dp, width)] + [(share,)] * 6
    return pl.pallas_call(
        functools.partial(final_kernel, seq, dp),
        out_shape=[jax.ShapeDtypeStruct(shape, F32) for shape in shapes],
        in_specs=[hbm] * 3 + [vmem] + [hbm],
        out_specs=[hbm] * 13 + [vmem] * 6,
        scratch_shapes=[pltpu.VMEM(sums.shape, BF16)]
        + [pltpu.VMEM(shape, F32) for shape in shapes[:13]]
        + [pltpu.SemaphoreType.DMA((7,)), pltpu.SemaphoreType.DMA((13,))],
        compiler_params=pltpu.CompilerParams(vmem_limit_bytes=64 * 2**20 - 2**17),
    )(layer, tokens, memory, stats, sums)


def swap(value, axis, bit):
    size = lax.axis_size(axis)
    return lax.ppermute(value, axis, [(i, i ^ bit) for i in range(size)])


def scatter_sum(value, bits):
    index = lax.axis_index("dp")
    size = lax.axis_size("dp")
    levels = size.bit_length() - 1
    blocks = value.reshape((2,) * levels + value.shape[1:])
    left = list(range(levels))[::-1]
    for bit in bits:
        at = left.index(bit)
        mine = (index >> bit) & 1
        keep = lax.dynamic_index_in_dim(blocks, mine, at, keepdims=False)
        away = lax.dynamic_index_in_dim(blocks, 1 - mine, at, keepdims=False)
        left.pop(at)
        got = swap(away.astype(BF16), "dp", 1 << bit)
        blocks = keep.astype(F32) + got.astype(F32)
    return blocks


def shards(
    tokens,
    memory,
    target_segments,
    memory_segments,
    pad_counts,
    out_grad,
    self_query,
    self_key,
    self_value,
    self_out,
    cross_query,
    cross_key,
    cross_value,
    cross_out,
    feed_in,
    feed_out,
    gain_attend,
    shift_attend,
    gain_cross,
    shift_cross,
    gain_feed,
    shift_feed,
):
    seq, dp = lax.axis_size("seq"), lax.axis_size("dp")
    me = lax.axis_index("seq")
    span, width = tokens.shape[1:]
    part = width // seq
    feed = feed_in.shape[1]
    unit = feed // dp // seq
    direct = dp == 8 and unit == width // dp and unit % 16 == 0
    fi, fo = feed_in, feed_out
    if not direct:
        fi = lax.dynamic_index_in_dim(fi.reshape(width, dp, seq, unit), me, 2, keepdims=False)
        fi = fi.reshape(width, dp * unit)
        fo = lax.dynamic_index_in_dim(fo.reshape(dp, seq, unit, width), me, 1, keepdims=False)
        fo = fo.reshape(dp * unit, width)
    operands = (
        tokens[0], memory[0], out_grad[0], target_segments, memory_segments, pad_counts,
        self_query, self_key, self_value, self_out, cross_query, cross_key, cross_value, cross_out,
        fi, fo, gain_attend, shift_attend, gain_cross, shift_cross, gain_feed, shift_feed,
    )
    results = row_call(seq, span, memory.shape[1], width, part, dp * unit, direct, operands)
    if direct:
        results = final_call(seq, dp, *results)
        return tuple(value[None] for value in results[:3]) + tuple(results[3:])
    layer_out, tokens_grad, memory_grad, stats, g_fo, g_fi, g_cross, g_self = results
    gather = lambda v, axis: lax.all_gather(v, "seq", axis=axis, tiled=True)

    levels = dp.bit_length() - 1
    up = list(range(levels))
    first, second = up, up[1:] + up[:1]
    share = width // dp
    split = lambda v: v.reshape(dp, share, -1)
    groups = ((split(g_fo), first), (split(g_fi), second), (split(g_cross), first), (split(g_self), second))
    summed = [gather(scatter_sum(v, bits).astype(BF16)[None], 0) for v, bits in groups]
    whole_fo = summed[0].reshape(seq * share, width).astype(F32)
    whole_fi = (
        summed[1].reshape(seq, share, dp, unit).transpose(1, 2, 0, 3).reshape(share, feed)
    ).astype(F32)

    def whole(group, at):
        block = group[:, :, at * part : (at + 1) * part]
        block = block.reshape(2, 2, share, part).transpose(2, 1, 0, 3)
        return block.reshape(share, width).astype(F32)

    co, ck, cv, cq = (whole(summed[2], at) for at in range(4))
    so, sq, sk, sv = (whole(summed[3], at) for at in range(4))
    stats = lax.psum(stats, ("seq", "dp"))
    norm_part = lax.dynamic_slice_in_dim(stats, lax.axis_index("dp") * share, share, 1)
    return (
        layer_out[None],
        tokens_grad[None],
        memory_grad[None],
        sq,
        sk,
        sv,
        so,
        cq,
        ck,
        cv,
        co,
        whole_fi,
        whole_fo,
    ) + tuple(norm_part[i] for i in range(6))


def solution(mesh):
    rows = P("dp", "seq", None)
    in_specs = (rows, rows, P("dp", None), P("dp", None), P("dp", None), rows) + (P(),) * 16
    out_specs = (rows,) * 3 + (P("dp", None),) * 10 + (P("dp"),) * 6
    return jax.shard_map(shards, mesh=mesh, in_specs=in_specs, out_specs=out_specs, check_vma=False)
```

```python
import functools

import jax
import jax.numpy as jnp
from jax import lax
from jax.experimental import pallas as pl
from jax.experimental.pallas import tpu as pltpu
from jax.sharding import PartitionSpec as P

HEAD_DIM = 64
EPSILON = 1e-05
NEGATIVE = -1e30
F32 = jnp.float32
BF16 = jnp.bfloat16
MESH = pl.DeviceIdType.MESH
WINDOW = 256
CHUNKS = 2


def mm(left, right):
    return jnp.dot(left, right, preferred_element_type=F32)


def mm_t(left, right):
    return lax.dot_general(left, right, (((1,), (1,)), ((), ())), preferred_element_type=F32)


def t_mm(left, right):
    return lax.dot_general(left, right, (((0,), (0,)), ((), ())), preferred_element_type=F32)


def normalize(values):
    centered = values - jnp.mean(values, axis=-1, keepdims=True)
    rate = lax.rsqrt(jnp.mean(centered * centered, axis=-1, keepdims=True) + EPSILON)
    return centered * rate, rate


def norm_back(grad, gain, normed, rate):
    scaled = grad * gain
    inner = jnp.mean(scaled * normed, axis=-1, keepdims=True)
    return rate * (scaled - jnp.mean(scaled, axis=-1, keepdims=True) - normed * inner)


class Names:
    def __init__(self, names, refs):
        self.__dict__.update(zip(names, refs))


INPUTS = ["tokens", "memory", "out_grad", "target_ids", "memory_ids", "pads"]
INPUTS += ["w_sq", "w_sk", "w_sv", "w_so", "w_cq", "w_ck", "w_cv", "w_co", "w_fi", "w_fo"]
INPUTS += ["gain_a", "shift_a", "gain_c", "shift_c", "gain_f", "shift_f"]
OUTPUTS = ["o_layer", "o_tokens", "o_memory", "o_stats"]
SEMAPHORES = ["load_sem", "send_sem", "recv_sem"]
GROUPS = ["g_fo", "g_fi", "g_cross", "g_self"]
ALONG, ACROSS, MIXED, TURNED = (1, 2, 0), (0, 1, 2), (1, 0, 2), (0, 2, 1)
ORDERS = (MIXED, ACROSS, ACROSS, ALONG, ACROSS, ACROSS, ACROSS, ACROSS)
STRAIGHT = 6
CUTS = (1, 1, 2, 6)
(
    OWN_FI, TOKENS_NEAR, TOKENS_MIDDLE, TOKENS_FAR, MEMORY_NEAR, MEMORY_MIDDLE, MEMORY_FAR, TOKENS_RELAY, MEMORY_RELAY,
    COTANGENT_SEND, COTANGENT_RELAY, LAYER_SEND, LAYER_SECOND, LAYER_OUT, MEMORY_TERMS,
    MEMORY_SECOND, MEMORY_OUT, TOKEN_TERMS, TOKEN_SECOND, TOKEN_OUT, GRAD_FO, GRAD_FI, GRAD_CK,
    GRAD_CV, GRAD_CO, GRAD_CQ, GRAD_SO, GRAD_SQ, GRAD_SK, GRAD_SV, NORMS_SEND,
) = range(31)
(
    SELF, ROWS, CROSS, FEED_UP, FEED_BACK, LAYER, CROSS_GRAD, CROSS_BACK, SELF_GRAD, SELF_BACK,
    CROSS_RELAY, ROWS_RELAY, TOTAL_SECOND, TOTAL_THIRD, NORMS_STEP,
) = range(100, 115)
OUT, W_SO, W_CO, W_FO = range(4)
SCHEDULE = [
    TOKENS_NEAR, OWN_FI, MEMORY_NEAR, TOKENS_RELAY, TOKENS_MIDDLE, TOKENS_FAR, (SELF, 1), (SELF, 0),
    COTANGENT_SEND, (ROWS, 1), MEMORY_RELAY, (ROWS, 0), MEMORY_MIDDLE, MEMORY_FAR, (CROSS, 0),
    COTANGENT_RELAY, (CROSS, 1), (CROSS_RELAY, 0), (FEED_UP, 0), (CROSS_RELAY, 1), (FEED_BACK, 0),
    (FEED_UP, 1), (TOTAL_SECOND, 0), GRAD_FO, (1, 0, 0), (0, 0, 0), (FEED_BACK, 1), GRAD_FI,
    (TOTAL_SECOND, 1), (2, 0, 0), (3, 0, 0), (LAYER, 1), (TOTAL_THIRD, 0), (LAYER, 0), LAYER_SEND,
    (CROSS_GRAD, 0), (CROSS_BACK, 0), (TOTAL_THIRD, 1), (1, 0, 1), (0, 0, 1), LAYER_SECOND,
    (CROSS_GRAD, 1), (CROSS_BACK, 1), GRAD_CV, GRAD_CQ, (5, 0, 0), (3, 0, 1), MEMORY_TERMS, (5, 1, 0),
    GRAD_CO, (ROWS_RELAY, 0), GRAD_CK, (0, 0, 2), (2, 0, 1), (4, 0, 0), MEMORY_SECOND, (ROWS_RELAY, 1),
    (1, 0, 2), (4, 1, 0), (SELF_GRAD, 0), (SELF_GRAD, 1), (5, 0, 1), GRAD_SO, (SELF_BACK, 1),
    (5, 1, 1), (7, 1, 0), (SELF_BACK, 0), (4, 0, 1), (2, 0, 2), GRAD_SK, (0, 0, 3), (7, 0, 0),
    (7, 2, 0), GRAD_SQ, (6, 0, 0), (5, 0, 2), TOKEN_TERMS, (1, 0, 3), (6, 1, 0), (5, 1, 2), (7, 1, 1),
    GRAD_SV, (7, 5, 0), TOKEN_SECOND, (7, 0, 1), (4, 1, 1), NORMS_SEND, (4, 0, 2), (6, 2, 0),
    (7, 2, 1), (7, 3, 0), (6, 3, 0), (7, 1, 2), (7, 0, 2), (NORMS_STEP, 0), (6, 0, 1), (7, 4, 0),
    (7, 5, 1), (2, 0, 3), (6, 4, 0), (5, 0, 3), LAYER_OUT, (3, 0, 2), (6, 2, 1), (4, 1, 2), (6, 3, 1),
    (4, 0, 3), (6, 1, 1), (5, 1, 3), (6, 5, 0), (7, 3, 1), (7, 1, 3), (6, 0, 2), (6, 2, 2), (6, 4, 1),
    (7, 5, 2), (7, 4, 1), (7, 0, 3), (NORMS_STEP, 1), (4, 1, 3), (6, 3, 2), (6, 1, 2), (3, 0, 3),
    (7, 2, 2), (6, 5, 1), (7, 3, 2), (5, 0, 4), (6, 2, 3), (6, 0, 3), (6, 4, 2), (NORMS_STEP, 2),
    (7, 5, 3), (1, 0, 4), (2, 0, 4), (7, 4, 2), (4, 1, 4), (6, 3, 3), (0, 0, 4), (6, 5, 2), (6, 1, 3),
    (7, 2, 3), (4, 1, 5), (5, 1, 4), (7, 3, 3), (3, 0, 4), (6, 4, 3), (NORMS_STEP, 3), TOKEN_OUT,
    (6, 0, 5), (7, 4, 3), MEMORY_OUT, (6, 5, 3), (7, 5, 5), (2, 0, 5), (6, 1, 5), (7, 1, 5), (5, 0, 5),
    (6, 2, 5), (0, 0, 5), (7, 2, 5), (4, 0, 4), (7, 0, 5), (4, 0, 5), (3, 0, 5), (6, 3, 5),
    (NORMS_STEP, 4), (5, 1, 5), (1, 0, 5), (7, 3, 5), (6, 4, 5), (7, 4, 5), (6, 5, 5),
]


def row_kernel(scratch_names, seq, direct, *refs):
    r = Names(INPUTS + OUTPUTS + (["o_sums"] if direct else GROUPS) + scratch_names, refs)
    me = lax.axis_index("seq")
    core = lax.rem(me, 2)
    chip = me // 2
    peer_c = me + 1 - 2 * core
    peer_x = lax.rem(me + 2, 4)
    span = r.tokens.shape[0]
    full, width = r.row.shape
    src_span = r.memory.shape[0]
    src_full = src_span * seq
    part = width // seq
    count = part // HEAD_DIM
    size = full // CHUNKS
    odd = chip
    half_width = 2 * part
    core_window = pl.ds(pl.multiple_of(core * half_width, 128), half_width)
    window = pl.ds(pl.multiple_of(core * half_width + chip * 128, 128), WINDOW)
    own_window = pl.ds(pl.multiple_of(chip * 128, 128), WINDOW)
    own_rows = pl.ds(pl.multiple_of((2 * core + chip) * part, 64), part)
    own_head, other_head = chip * count, (1 - chip) * count
    own_span = pl.ds(pl.multiple_of(me * span, span), span)

    def pick(value):
        return jnp.where(odd == 1, value[:, 64 : 64 + part], value[:, :part])

    def place(value):
        empty = jnp.zeros((value.shape[0], WINDOW - part), value.dtype)
        return jnp.where(
            odd == 1,
            jnp.concatenate([empty, value], 1),
            jnp.concatenate([value, empty], 1),
        )

    loads = []

    def load(src, dst):
        copy = pltpu.make_async_copy(src, dst, r.load_sem.at[len(loads)])
        copy.start()
        loads.append(copy)
        return copy

    stores = []

    def store(src, dst):
        stores.append(load(src, dst))

    def ready(*copies):
        for copy in copies:
            copy.wait()

    place_dp = lax.axis_index("dp")
    peers = [{"seq": peer_c}, {"seq": peer_x}]
    to_core, to_chip = peers
    to_far = {"seq": lax.rem(peer_c + 2, 4)}
    bits, peers_dp = [], []
    if direct:
        for level in range(3):
            bit = lax.rem(place_dp // 2**level, 2)
            bits.append(bit)
            peers_dp.append({"dp": place_dp + 2**level * (1 - 2 * bit)})
    barrier = pltpu.get_barrier_semaphore()
    others = peers + peers_dp + ([to_far] if direct else [])
    for peer in others:
        pl.semaphore_signal(barrier, inc=1, device_id=peer, device_id_type=MESH)

    own_source = pl.ds(pl.multiple_of(me * src_span, src_span), src_span)
    get_tok = load(r.tokens, r.row.at[own_span])
    get_sq = load(r.w_sq.at[:, core_window], r.win_sq)
    get_sk = load(r.w_sk.at[:, core_window], r.win_sk)
    get_sv = load(r.w_sv.at[:, core_window], r.win_sv)
    get_mem = load(r.memory, r.mem.at[own_source])
    get_ck = load(r.w_ck.at[:, window], r.win_ck)
    get_cv = load(r.w_cv.at[:, window], r.win_cv)
    get_fi, get_fo = [], []
    if direct:
        blocks, share = r.g_fo.shape[0] * 4, r.g_fo.shape[3]
        unit = share

        def wide_fi(b):
            spot = pl.ds(pl.multiple_of(b % 4 * WINDOW, WINDOW), WINDOW)
            return r.cross_weights.at[pl.ds(pl.multiple_of(b // 4 * width, width), width), spot]

        for b in range(blocks):
            start = pl.multiple_of(b * (seq * unit) + chip * 128, 128)
            get_fi.append(load(r.w_fi.at[:, pl.ds(start, WINDOW)], wide_fi(b)))
        for b in range(blocks):
            start = pl.multiple_of((b * seq + me) * unit, 16)
            get_fo.append(load(r.w_fo.at[pl.ds(start, unit)], r.own_fo.at[pl.ds(b * unit, unit)]))
    else:
        get_fi = [load(r.w_fi, r.own_fi)]
        get_fo = [load(r.w_fo, r.own_fo)]
    get_so = load(r.w_so, r.all_so)
    get_cq = load(r.w_cq, r.all_cq)
    get_co = load(r.w_co, r.all_co)
    get_og = load(r.out_grad, r.grad_out.at[own_span])

    def column(ids):
        return jnp.broadcast_to(ids.astype(F32), (128, ids.shape[1])).T[:, :1]

    target_ids = r.target_ids[...]
    memory_ids = r.memory_ids[...]
    self_code = jnp.where(
        lax.broadcasted_iota(jnp.int32, (1, full), 1) < full - r.pads[0, 0], target_ids, -1
    ).astype(F32)
    cross_code = jnp.where(
        lax.broadcasted_iota(jnp.int32, (1, src_full), 1) < src_full - r.pads[0, 1], memory_ids, -1
    ).astype(F32)
    target_col = column(target_ids)
    r.target_col[...] = target_col

    def bias_rows(at, carry):
        rows = pl.ds(pl.multiple_of(at * span, span), span)
        i_pos = lax.broadcasted_iota(jnp.int32, (span, full), 0) + at * span
        j_pos = lax.broadcasted_iota(jnp.int32, (span, full), 1)
        same = r.target_col[rows, :] == self_code
        r.self_bias[rows, :] = jnp.where((same & (j_pos <= i_pos)) | (i_pos == j_pos), 0.0, NEGATIVE)
        return carry

    lax.fori_loop(0, seq, bias_rows, 0)
    r.cross_code[...] = cross_code

    def self_masked(scores, rows, reach):
        return scores + r.self_bias[rows, :reach]

    def cross_masked(scores, rows, reach):
        return jnp.where(r.target_col[rows, :] == r.cross_code[:, :reach], scores, NEGATIVE)

    gain_a, shift_a, gain_c, shift_c, gain_f, shift_f = (
        getattr(r, name)[...].astype(F32).reshape(1, width) for name in INPUTS[-6:]
    )
    pl.semaphore_wait(barrier, len(others))

    sent, busy = [], []

    def send(src, dst, peer):
        at = len(sent)
        copy = pltpu.make_async_remote_copy(
            src_ref=src,
            dst_ref=dst,
            send_sem=r.send_sem.at[at],
            recv_sem=r.recv_sem.at[at],
            device_id=peer,
            device_id_type=MESH,
        )
        copy.start()
        sent.append(copy)
        busy.append(copy)
        return copy

    def finish(copies):
        for copy in copies:
            copy.wait_send()
            busy[:] = [other for other in busy if other is not copy]

    class Gather:
        def __init__(self, src, spot):
            self.spot = spot
            self.x = send(src, spot(me), to_chip)
            self.c = send(src, spot(me), to_core)

        def near(self):
            self.c.wait_recv()

        def relay(self):
            self.x.wait_recv()
            self.second = send(self.spot(peer_x), self.spot(peer_x), to_core)

        def far(self):
            self.second.wait_recv()

        def wait(self):
            self.near()
            self.far()

    def rows_at(ref, length):
        return lambda who: ref.at[pl.ds(pl.multiple_of(who * length, length), length)]

    tok = Gather(r.tokens, rows_at(r.row, span))
    mem = Gather(r.memory, rows_at(r.mem, src_span))
    tasks = {}

    class kept:
        to_self, to_cross, to_rows, total, slope, ended = {}, {}, {}, {}, {}, {}
        seen = set()

    def once(what):
        first = what not in kept.seen
        kept.seen.add(what)
        return first

    def task(name):
        def keep(function):
            tasks[name] = function

        return keep

    @task(OWN_FI)
    def _():
        if not direct:
            return
        from_row = lax.broadcasted_iota(jnp.int32, (WINDOW, WINDOW), 0)
        to_col = lax.broadcasted_iota(jnp.int32, (WINDOW, WINDOW), 1)
        skip = me * unit - chip * 128
        ready(*get_fi)
        def tile(t, carry):
            total = None
            for near in range(4):
                b = 2 * t + near
                at = to_col + (t * WINDOW - b * unit)
                chosen = (from_row == at + skip) & (at >= 0) & (at < unit)
                term = mm(wide_fi(b)[...], jnp.where(chosen, 1.0, 0.0).astype(BF16))
                total = term if total is None else total + term
            r.own_fi[:, pl.ds(pl.multiple_of(t * WINDOW, WINDOW), WINDOW)] = total.astype(BF16)
            return carry

        lax.fori_loop(0, blocks * unit // WINDOW, tile, 0)

    def to_heads(value, ref, rows):
        ones = jnp.ones((value.shape[0], HEAD_DIM), ref.dtype)
        for h in range(value.shape[1] // HEAD_DIM):
            head = value[:, h * HEAD_DIM : (h + 1) * HEAD_DIM].astype(ref.dtype)
            ref[h, rows, :] = head if ref.shape[2] == HEAD_DIM else jnp.concatenate([head, ones], 1)

    def part_of(who, length):
        return pl.ds(pl.multiple_of(who * length, length), length)

    def project_tokens(rows):
        row = r.row[rows, :].astype(F32)
        normed, _ = normalize(row)
        r.n_attend[rows, :] = normed.astype(BF16)
        hidden = (normed * gain_a + shift_a).astype(BF16)
        r.h_attend[rows, :] = hidden
        r.after[rows, :] = row
        to_heads(mm(hidden, r.win_sq[...]) * HEAD_DIM**-0.5, r.q, rows)
        to_heads(mm(hidden, r.win_sk[...]), r.k, rows)
        to_heads(mm(hidden, r.win_sv[...]), r.v, rows)

    def project_memory(rows):
        source = r.mem[rows, :]
        to_heads(pick(mm(source, r.win_ck[...])), r.mk, rows)
        to_heads(pick(mm(source, r.win_cv[...])), r.mv, rows)

    @task(TOKENS_NEAR)
    def _():
        ready(get_tok, get_sq, get_sk, get_sv)
        tok.near()
        project_tokens(part_of(chip, full // 2))

    @task(MEMORY_NEAR)
    def _():
        ready(get_mem, get_ck, get_cv)
        mem.near()
        project_memory(part_of(chip, src_full // 2))

    tasks[TOKENS_RELAY] = tok.relay

    @task(TOKENS_MIDDLE)
    def _():
        project_tokens(part_of(peer_x, span))

    @task(TOKENS_FAR)
    def _():
        tok.far()
        project_tokens(part_of(3 - me, span))

    tasks[MEMORY_RELAY] = mem.relay

    @task(MEMORY_MIDDLE)
    def _():
        project_memory(part_of(peer_x, src_span))

    @task(MEMORY_FAR)
    def _():
        mem.far()
        project_memory(part_of(3 - me, src_span))

    def attend(q, k, v, masked, weights, mixed, rows, reach, base=0):
        def one(h):
            scores = masked(mm_t(q[base + h, rows, :], k[base + h, :reach, :]), rows, reach)
            highest = jnp.max(scores, axis=-1, keepdims=True)
            low = jnp.exp(scores - highest).astype(BF16)
            product = mm(low, v[base + h, :reach, :])
            over = 1.0 / product[:, HEAD_DIM : HEAD_DIM + 1]
            head = product[:, :HEAD_DIM] * over
            if weights is not None:
                weights[h * full + rows.start : h * full + rows.stop, :reach] = low
                mixed[h, rows, HEAD_DIM : HEAD_DIM + 1] = over
                mixed[h, rows, :HEAD_DIM] = head
            return head.astype(BF16)

        return [one(h) for h in range(count)]

    def attend_back(q, k, v, grad, weights, mixed, dk, dv, rows, reach, first, base=0):
        def one(h):
            scaled = grad[h, rows, :].astype(F32) * mixed[h, rows, HEAD_DIM : HEAD_DIM + 1]
            inner = jnp.sum(scaled * mixed[h, rows, :HEAD_DIM], axis=-1, keepdims=True)
            low = scaled.astype(BF16)
            exponent = weights[h * full + rows.start : h * full + rows.stop, :reach]
            grad_weights = mm_t(low, v[base + h, :reach, :HEAD_DIM])
            grad_scores = (exponent.astype(F32) * (grad_weights - inner)).astype(BF16)
            grad_q = mm(grad_scores, k[base + h, :reach, :]) * HEAD_DIM**-0.5
            more_k = mm(q[base + h, rows, :].T, grad_scores)
            more_v = mm(low.T, exponent)
            if first:
                dk[h, :, :reach] = more_k
                dv[h, :, :reach] = more_v
            else:
                dk[h, :, :reach] += more_k
                dv[h, :, :reach] += more_v
            return grad_q.astype(BF16)

        return [one(h) for h in range(count)]

    chunks = [slice(c * size, (c + 1) * size) for c in range(CHUNKS)]
    half = size // 2

    def gather_columns(buffer, c, heads):
        buffer[c, me, :size, :] = jnp.concatenate(heads[:2], axis=1)
        buffer[c, me, size:, :] = jnp.concatenate([heads[2][:half], heads[2][half:]], axis=1)
        return Gather(buffer.at[c, me], lambda who: buffer.at[c, who])

    def joined(buffer, c):
        pieces = []
        for s in (0, 2, 1, 3):
            last = buffer[c, s, size:, :]
            pieces.append(buffer[c, s, :size, :])
            pieces.append(jnp.concatenate([last[:, :HEAD_DIM], last[:, HEAD_DIM:]], axis=0))
        return jnp.concatenate(pieces, axis=1)

    def self_chunk(c, rows):
        ours, theirs = (
            jnp.concatenate(attend(r.q, r.k, r.v, self_masked, weights, mix, rows, rows.stop, base), 1)
            for weights, mix, base in (
                (r.self_weights, r.self_mix, own_head),
                (None, None, other_head),
            )
        )
        first, second = jnp.where(chip == 0, ours, theirs), jnp.where(chip == 0, theirs, ours)
        spot = r.self_mixed.at[rows, core_window]
        spot[...] = jnp.concatenate([first, second], axis=1)
        kept.to_self[c] = send(spot, spot, to_core)

    @task(COTANGENT_SEND)
    def _():
        kept.out = Gather(r.out_grad, rows_at(r.grad_out, span))

    @task(COTANGENT_RELAY)
    def _():
        kept.out.relay()

    def out_wait():
        if once(OUT):
            ready(get_og)
            kept.out.wait()

    def cross_rows(c, rows):
        if once(W_SO):
            ready(get_so, get_cq)
        kept.to_self[c].wait_recv()
        after = r.after[rows, :] + mm(r.self_mixed[rows, :], r.all_so[...])
        r.after[rows, :] = after
        normed, rate = normalize(after)
        r.n_cross[rows, :] = normed.astype(BF16)
        r.r_cross[rows, :] = rate
        hidden = (normed * gain_c + shift_c).astype(BF16)
        r.h_cross[rows, :] = hidden
        to_heads(pick(mm(hidden, r.all_cq[:, window])) * HEAD_DIM**-0.5, r.cq, rows)

    def cross_chunk(c, rows):
        heads = attend(
            r.cq, r.mk, r.mv, cross_masked, r.cross_weights, r.cross_mix, rows, src_full
        )
        kept.to_cross[c] = gather_columns(r.cross_parts, c, heads)

    stats = [None] * 6

    def add(name, value):
        value = jnp.sum(value, axis=0, keepdims=True)
        stats[name] = value if stats[name] is None else stats[name] + value

    class Total:
        def __init__(self, c, value):
            self.c = c
            self.keep = part_of(core, half)
            r.sum_send[c] = value.astype(BF16)
            self.step = send(r.sum_send.at[c, part_of(1 - core, half)], r.sum_core.at[c], to_core)

        def second(self):
            self.step.wait_recv()
            r.sum_mid[self.c] = r.sum_send[self.c, self.keep, :] + r.sum_core[self.c]
            self.step = send(r.sum_mid.at[self.c], r.sum_chip.at[self.c], to_chip)

        def third(self):
            self.step.wait_recv()
            r.sum_full[self.c, self.keep, :] = r.sum_mid[self.c] + r.sum_chip[self.c]
            spot = r.sum_full.at[self.c, self.keep]
            self.step = send(spot, spot, to_core)

        def wait(self):
            self.step.wait_recv()
            return r.sum_full[self.c].astype(F32)

    class Scatter:
        def __init__(self, mail, core_in, chip_in):
            self.mail, self.core_in, self.chip_in = mail, core_in, chip_in
            self.steps = [
                send(mail.at[2 * spot + 1 - core], core_in.at[spot], to_core) for spot in range(2)
            ]

        def second(self):
            for step in self.steps:
                step.wait_recv()
            away = 1 - chip
            self.mail[2 * away + core] += self.core_in[away]
            self.step = send(self.mail.at[2 * away + core], self.chip_in, to_chip)

        def wait(self):
            self.step.wait_recv()
            value = self.mail[me].astype(F32) + self.core_in[chip].astype(F32)
            return value + self.chip_in[...].astype(F32)

    lanes = 2 * part

    class Reduce:
        def __init__(self, at, top, length):
            self.group = getattr(r, GROUPS[at // 2])
            self.at = at
            self.rows = pl.ds(top, length)
            self.cols = pl.ds(at % 2 * lanes, lanes)
            self.order = ORDERS[at]
            self.step = 0

        def index(self, last):
            spots = [slice(None)] * 3
            for bit in self.order[: self.step]:
                spots[2 - bit] = bits[bit]
            bit = self.order[self.step]
            spots[2 - bit] = last(bits[bit])
            return tuple(spots) + (self.rows, self.cols)

        def start(self):
            inbox = (r.in_half, r.in_quarter, r.in_eighth)[self.step]
            inbox = inbox.at[(self.at,) + (slice(None),) * (2 - self.step) + (self.rows,)]
            away = self.index(lambda bit: 1 - bit)
            self.copy = send(self.group.at[away], inbox, peers_dp[self.order[self.step]])
            self.inbox = inbox

        def next(self):
            self.copy.wait_recv()
            keep = self.index(lambda bit: bit)
            value = self.group[keep] + self.inbox[...]
            if self.step < 2:
                self.group[keep] = value
                self.step += 1
                self.start()
            else:
                r.b_sums[self.at, me, self.rows, :] = value
                spot = lambda who: r.b_sums.at[self.at, who, self.rows]
                if self.at < STRAIGHT:
                    self.gather = Gather(spot(me), spot)
                else:
                    self.copies = [send(spot(me), spot(me), peer) for peer in peers + [to_far]]

        def relay(self):
            self.gather.relay()

        def wait(self):
            if self.at < STRAIGHT:
                self.gather.wait()
            else:
                for copy in self.copies:
                    copy.wait_recv()
            kept.ended[self.at] = kept.ended.get(self.at, 0) + 1
            if kept.ended[self.at] == CUTS[self.at // 2]:
                store(r.b_sums.at[self.at], r.o_sums.at[self.at])

    def put(group, at, value):
        ref = getattr(r, GROUPS[group])
        value = value.astype(BF16)
        if direct:
            value = value.reshape(2, 2, 2, share, value.shape[-1])
            ref[:, :, :, :, at : at + value.shape[-1]] = value
        else:
            ref[:, at : at + value.shape[-1]] = value

    def feed_up(c, rows):
        if once(W_CO):
            ready(get_co, *([] if direct else get_fi))
        kept.to_cross[c].wait()
        mixed = joined(r.cross_parts, c)
        r.cross_mixed[rows, :] = mixed
        after = r.after[rows, :] + mm(mixed, r.all_co[...])
        r.after[rows, :] = after
        normed, rate = normalize(after)
        r.n_feed[rows, :] = normed.astype(BF16)
        r.r_feed[rows, :] = rate
        hidden = (normed * gain_f + shift_f).astype(BF16)
        r.h_feed[rows, :] = hidden
        upward = mm(hidden, r.own_fi[...])
        bell = 0.5 + 0.5 * lax.erf(upward * 2.0**-0.5)
        r.active[rows, :] = (upward * bell).astype(BF16)
        kept.slope[c] = bell + upward * jnp.exp(-0.5 * upward * upward) * 0.3989422804014327

    def feed_back(c, rows):
        if once(W_FO):
            ready(*get_fo)
        out_wait()
        normed, slope = r.n_feed[rows, :].astype(F32), kept.slope[c]
        grad_up = (mm_t(r.grad_out[rows, :], r.own_fo[...]) * slope).astype(BF16)
        r.grad_up[rows, :] = grad_up
        back = mm_t(grad_up, r.own_fi[...])
        add(4, back * normed)
        add(5, back)
        kept.total[c] = Total(c, back)

    def layer_chunk(c, rows):
        if once(W_FO):
            ready(*get_fo)
        value = mm(r.active[rows, :], r.own_fo[...]).astype(BF16)
        r.layer_mail[2 * c : 2 * c + 2] = value.reshape(2, span, width)

    @task(LAYER_SEND)
    def _():
        kept.layer = Scatter(r.layer_mail, r.layer_core, r.layer_chip)

    @task(LAYER_SECOND)
    def _():
        kept.layer.second()

    @task(LAYER_OUT)
    def _():
        r.b_layer[...] = r.after[own_span, :] + kept.layer.wait()
        store(r.b_layer, r.o_layer)

    @task(GRAD_FO)
    def _():
        out_wait()
        put(0, 0, t_mm(r.active[...], r.grad_out[...]))

    @task(GRAD_FI)
    def _():
        put(1, 0, t_mm(r.h_feed[...], r.grad_up[...]))

    def cross_before(c, rows):
        grad = kept.total[c].wait()
        normed = r.n_feed[rows, :].astype(F32)
        grad = r.grad_out[rows, :].astype(F32) + norm_back(grad, gain_f, normed, r.r_feed[rows, :])
        r.grad_row[rows, :] = grad
        low = grad.astype(BF16)
        r.grad_cross[rows, :] = low
        to_heads(mm_t(low, r.all_co[own_rows, :]).astype(BF16), r.grad_mix, rows)

    def cross_back(c, rows):
        heads = attend_back(
            r.cq, r.mk, r.mv, r.grad_mix, r.cross_weights, r.cross_mix,
            r.grad_mk, r.grad_mv, rows, src_full, c == 0,
        )
        r.grad_cross_rows[rows, :] = jnp.concatenate(heads, axis=1)
        kept.to_rows[c] = gather_columns(r.row_parts, c, heads)

    @task(MEMORY_TERMS)
    def _():
        mk_t = r.grad_mk[...].reshape(part, src_full)
        mv_t = r.grad_mv[...].reshape(part, src_full)
        terms = mm_t(place(mk_t.T.astype(BF16)), r.win_ck[...]) + mm_t(
            place(mv_t.T.astype(BF16)), r.win_cv[...]
        )
        r.mem_mail[...] = terms.astype(BF16).reshape(seq, src_span, width)
        kept.memory = Scatter(r.mem_mail, r.mem_core, r.mem_chip)

    @task(MEMORY_SECOND)
    def _():
        kept.memory.second()

    @task(MEMORY_OUT)
    def _():
        r.b_memory[...] = kept.memory.wait()
        store(r.b_memory, r.o_memory)

    @task(GRAD_CK)
    def _():
        put(2, part, mm(r.grad_mk[...].reshape(part, src_full).astype(BF16), r.mem[...]).T)

    @task(GRAD_CV)
    def _():
        put(2, 2 * part, mm(r.grad_mv[...].reshape(part, src_full).astype(BF16), r.mem[...]).T)

    @task(GRAD_CO)
    def _():
        put(2, 0, pick(t_mm(r.cross_mixed[...], r.grad_cross[:, window])))

    @task(GRAD_CQ)
    def _():
        put(2, 3 * part, t_mm(r.h_cross[...], r.grad_cross_rows[...]))

    def self_before(c, rows):
        kept.to_rows[c].wait()
        grad = mm_t(joined(r.row_parts, c), r.all_cq[...])
        normed = r.n_cross[rows, :].astype(F32)
        add(2, grad * normed)
        add(3, grad)
        grad = r.grad_row[rows, :] + norm_back(grad, gain_c, normed, r.r_cross[rows, :])
        r.grad_row[rows, :] = grad
        to_heads(mm_t(grad.astype(BF16), r.all_so[own_rows, :]).astype(BF16), r.grad_mix, rows)

    def self_back(c, rows):
        heads = attend_back(
            r.q, r.k, r.v, r.grad_mix, r.self_weights, r.self_mix,
            r.grad_k, r.grad_v, rows, rows.stop, c == CHUNKS - 1, own_head,
        )
        r.grad_self_rows[rows, :] = jnp.concatenate(heads, axis=1)

    def put_self(at, value):
        if not direct:
            put(3, at * part, value)
        elif at in (1, 2):
            put(3, (at - 1) * part, value)
        else:
            value = value.astype(BF16).reshape(2, 2, 2, share, part)
            tall = share // 2
            packed = jnp.concatenate([value[:, :, :, :tall], value[:, :, :, tall:]], axis=4)
            top = 0 if at == 0 else tall
            r.g_self[:, :, :, top : top + tall, lanes:] = packed

    @task(GRAD_SO)
    def _():
        put_self(0, pick(t_mm(r.self_mixed[...], r.grad_row[:, window].astype(BF16))))

    @task(GRAD_SQ)
    def _():
        put_self(1, t_mm(r.h_attend[...], r.grad_self_rows[...]))

    @task(GRAD_SK)
    def _():
        put_self(2, mm(r.grad_k[...].reshape(part, full).astype(BF16), r.h_attend[...]).T)

    @task(GRAD_SV)
    def _():
        put_self(3, mm(r.grad_v[...].reshape(part, full).astype(BF16), r.h_attend[...]).T)

    @task(TOKEN_TERMS)
    def _():
        k_t = r.grad_k[...].reshape(part, full)
        v_t = r.grad_v[...].reshape(part, full)
        back = (
            mm_t(place(r.grad_self_rows[...]), r.win_sq[:, own_window])
            + mm_t(place(k_t.T.astype(BF16)), r.win_sk[:, own_window])
            + mm_t(place(v_t.T.astype(BF16)), r.win_sv[:, own_window])
        )
        add(0, back * r.n_attend[...].astype(F32))
        add(1, back)
        r.tok_mail[...] = back.astype(BF16).reshape(seq, span, width)
        kept.tokens = Scatter(r.tok_mail, r.tok_core, r.tok_chip)

    @task(TOKEN_SECOND)
    def _():
        kept.tokens.second()

    @task(TOKEN_OUT)
    def _():
        normed, rate = normalize(r.row[own_span, :].astype(F32))
        grad = kept.tokens.wait()
        r.b_tokens[...] = r.grad_row[own_span, :] + norm_back(grad, gain_a, normed, rate)
        store(r.b_tokens, r.o_tokens)

    class Stats:
        def __init__(self):
            shared = jnp.where(me == 0, 1.0, 0.0)
            rows = stats[:2] + [row * shared for row in stats[2:4]] + stats[4:]
            self.value = jnp.concatenate(rows + [jnp.zeros((2, width), F32)], axis=0)
            self.step = 0
            r.o_stats[...] = self.value

        def start(self):
            r.stat_out[self.step] = self.value
            peer = (peers + peers_dp)[self.step]
            self.copy = send(r.stat_out.at[self.step], r.stat_in.at[self.step], peer)

        def next(self):
            self.copy.wait_recv()
            self.value = self.value + r.stat_in[self.step]
            self.step += 1
            if self.step < 5:
                self.start()
            else:
                r.o_stats[...] = self.value

    @task(NORMS_SEND)
    def _():
        kept.stats = Stats()
        if direct:
            kept.stats.start()

    if direct:
        for level in range(5):
            tasks[NORMS_STEP, level] = lambda: kept.stats.next()

    for c, rows in enumerate(chunks):
        for name, function in (
            (SELF, self_chunk),
            (ROWS, cross_rows),
            (CROSS, cross_chunk),
            (FEED_UP, feed_up),
            (FEED_BACK, feed_back),
            (LAYER, layer_chunk),
            (CROSS_GRAD, cross_before),
            (CROSS_BACK, cross_back),
            (SELF_GRAD, self_before),
            (SELF_BACK, self_back),
        ):
            tasks[name, c] = functools.partial(function, c, rows)
        tasks[CROSS_RELAY, c] = lambda c=c: kept.to_cross[c].relay()
        tasks[ROWS_RELAY, c] = lambda c=c: kept.to_rows[c].relay()
        tasks[TOTAL_SECOND, c] = lambda c=c: kept.total[c].second()
        tasks[TOTAL_THIRD, c] = lambda c=c: kept.total[c].third()

    if direct:
        for at in range(8):
            cuts = CUTS[at // 2]
            for cut in range(cuts):
                one = Reduce(at, cut * (share // cuts), share // cuts)
                for level, function in enumerate(
                    (one.start, one.next, one.next, one.next, one.relay, one.wait)
                ):
                    tasks[at, cut, level] = function

    begun, late = [], False
    for name in SCHEDULE:
        if name in tasks:
            late = late or name == TOKEN_TERMS
            begun.append(list(busy))
            if late:
                finish([copy for copy in busy if any(copy is old for old in begun[-24])][:8])
            tasks[name]()
    finish(list(busy))
    ready(*stores)


def row_call(seq, span, src_span, width, part, units, direct, operands):
    full, src_full = span * seq, src_span * seq
    count, size = part // HEAD_DIM, full // CHUNKS
    half = size // 2
    shapes = dict(
        row=((full, width), BF16),
        mem=((src_full, width), BF16),
        grad_out=((full, width), BF16),
        win_sq=((width, 2 * part), BF16),
        win_sk=((width, 2 * part), BF16),
        win_sv=((width, 2 * part), BF16),
        win_ck=((width, WINDOW), BF16),
        win_cv=((width, WINDOW), BF16),
        all_so=((width, width), BF16),
        all_cq=((width, width), BF16),
        all_co=((width, width), BF16),
        own_fi=((width, units), BF16),
        own_fo=((units, width), BF16),
        self_bias=((full, full), F32),
        target_col=((full, 1), F32),
        cross_code=((1, src_full), F32),
        n_attend=((full, width), BF16),
        n_cross=((full, width), BF16),
        n_feed=((full, width), BF16),
        r_cross=((full, 1), F32),
        r_feed=((full, 1), F32),
        h_attend=((full, width), BF16),
        h_cross=((full, width), BF16),
        h_feed=((full, width), BF16),
        after=((full, width), F32),
        grad_row=((full, width), F32),
        q=((2 * count, full, HEAD_DIM), BF16),
        k=((2 * count, full, HEAD_DIM), BF16),
        v=((2 * count, full, 2 * HEAD_DIM), BF16),
        cq=((count, full, HEAD_DIM), BF16),
        mk=((count, src_full, HEAD_DIM), BF16),
        mv=((count, src_full, 2 * HEAD_DIM), BF16),
        grad_mix=((count, full, HEAD_DIM), BF16),
        self_weights=((count * full, full), BF16),
        cross_weights=((count * full, src_full), BF16),
        self_mix=((count, full, 2 * HEAD_DIM), F32),
        cross_mix=((count, full, 2 * HEAD_DIM), F32),
        grad_k=((count, HEAD_DIM, full), F32),
        grad_v=((count, HEAD_DIM, full), F32),
        grad_mk=((count, HEAD_DIM, src_full), F32),
        grad_mv=((count, HEAD_DIM, src_full), F32),
        cross_parts=((CHUNKS, seq, size + half, 2 * HEAD_DIM), BF16),
        row_parts=((CHUNKS, seq, size + half, 2 * HEAD_DIM), BF16),
        self_mixed=((full, width), BF16),
        cross_mixed=((full, width), BF16),
        active=((full, units), BF16),
        grad_up=((full, units), BF16),
        grad_cross=((full, width), BF16),
        grad_cross_rows=((full, part), BF16),
        grad_self_rows=((full, part), BF16),
        sum_send=((CHUNKS, size, width), BF16),
        sum_core=((CHUNKS, half, width), BF16),
        sum_mid=((CHUNKS, half, width), BF16),
        sum_chip=((CHUNKS, half, width), BF16),
        sum_full=((CHUNKS, size, width), BF16),
        layer_mail=((seq, span, width), BF16),
        layer_core=((2, span, width), BF16),
        layer_chip=((span, width), BF16),
        tok_mail=((seq, span, width), BF16),
        tok_core=((2, span, width), BF16),
        tok_chip=((span, width), BF16),
        b_layer=((span, width), F32),
        b_tokens=((span, width), F32),
        b_memory=((src_span, width), F32),
        mem_mail=((seq, src_span, width), BF16),
        mem_core=((2, src_span, width), BF16),
        mem_chip=((src_span, width), BF16),
    )
    group = (width, 4 * part)
    if direct:
        blocks, share = 8, width // 8
        lanes = 2 * part
        group = (2, 2, 2, share, 4 * part)
        shapes.update({name: (group, BF16) for name in GROUPS})
        shapes.update(
            in_half=((8, 2, 2, share, lanes), BF16),
            in_quarter=((8, 2, share, lanes), BF16),
            in_eighth=((8, share, lanes), BF16),
            b_sums=((8, seq, share, lanes), BF16),
            stat_out=((5, 8, width), F32),
            stat_in=((5, 8, width), F32),
        )
    names = list(shapes) + SEMAPHORES
    scratch = [pltpu.VMEM(shape, dtype) for shape, dtype in shapes.values()]
    scratch += [pltpu.SemaphoreType.DMA((80,)), pltpu.SemaphoreType.DMA((224,)), pltpu.SemaphoreType.DMA((224,))]
    hbm = pl.BlockSpec(memory_space=pl.ANY)
    vmem = pl.BlockSpec(memory_space=pltpu.VMEM)
    smem = pl.BlockSpec(memory_space=pltpu.SMEM)
    outs = [((span, width), F32), ((span, width), F32), ((src_span, width), F32), ((8, width), F32)]
    out_specs = [hbm] * 3 + [vmem]
    if direct:
        outs += [((8, seq, share, lanes), BF16)]
        out_specs += [hbm]
    else:
        outs += [(group, BF16)] * 4
        out_specs += [vmem] * 4
    return pl.pallas_call(
        functools.partial(row_kernel, names, seq, direct),
        out_shape=[jax.ShapeDtypeStruct(s, t) for s, t in outs],
        in_specs=[hbm] * 3 + [vmem] * 2 + [smem] + [hbm] * 10 + [vmem] * 6,
        out_specs=out_specs,
        scratch_shapes=scratch,
        compiler_params=pltpu.CompilerParams(
            collective_id=0, has_side_effects=True, vmem_limit_bytes=64 * 2**20 - 2**17
        ),
    )(*operands)


def final_kernel(seq, dp, layer, tokens, memory, stats, sums, *refs):
    outs, norms, got, passed, built = refs[:13], refs[13:19], refs[19], refs[20:23], refs[23:33]
    in_sems, out_sems = refs[33:]
    sources = [(sums.at[pl.ds(2 * g, 2)], got.at[pl.ds(2 * g, 2)]) for g in range(4)]
    sources += list(zip((memory, layer, tokens), (passed[2], passed[0], passed[1])))
    loads = [pltpu.make_async_copy(*pair, in_sems.at[i]) for i, pair in enumerate(sources)]
    stores = [
        pltpu.make_async_copy(src, dst, out_sems.at[i])
        for i, (src, dst) in enumerate(zip(passed + built, outs))
    ]
    for copy in loads:
        copy.start()
    share, lanes = sums.shape[2:]
    part = lanes // 2
    sq, sk, sv, so, cq, ck, cv, co, fi, fo = built
    width = stats.shape[1]
    back = lax.rem(width - lax.axis_index("dp") * share, width)
    own = pltpu.roll(stats[...], back, 1)[:, :share]
    for i, out in enumerate(norms):
        out[...] = own[i]
    unit = fo.shape[0] // seq
    loads[0].wait()
    for s in range(seq):
        for at in range(2):
            fo[s * unit : (s + 1) * unit, at * lanes : (at + 1) * lanes] = got[at, s].astype(F32)
    stores[12].start()
    loads[1].wait()
    for at in range(2):
        wide = [got[2 + at, s].astype(F32) for s in range(seq)]
        for b in range(dp // 2):
            block = [w[:, b * unit : (b + 1) * unit] for w in wide]
            start = (at * (dp // 2) + b) * seq * unit
            fi[:, start : start + seq * unit] = jnp.concatenate(block, 1)
    stores[11].start()
    loads[2].wait()
    loads[3].wait()
    for i, (out, spot) in enumerate(zip((co, ck, cv, cq, sq, sk), (10, 8, 9, 7, 3, 4))):
        start = i % 2 * part
        block = [got[4 + i // 2, s].astype(F32)[:, start : start + part] for s in (0, 2, 1, 3)]
        out[...] = jnp.concatenate(block, 1)
        stores[spot].start()
    tall = share // 2
    for out, top, spot in ((so, 0, 6), (sv, tall, 5)):
        block = [got[7, s].astype(F32)[top : top + tall] for s in (0, 2, 1, 3)]
        for side in range(2):
            pieces = [piece[:, side * part : (side + 1) * part] for piece in block]
            out[side * tall : (side + 1) * tall, :] = jnp.concatenate(pieces, 1)
        stores[spot].start()
    for copy, place in zip(loads[4:], (2, 0, 1)):
        copy.wait()
        stores[place].start()
    for copy in stores:
        copy.wait()


def final_call(seq, dp, layer, tokens, memory, stats, sums):
    share, width = sums.shape[2], stats.shape[1]
    feed = sums.shape[3] * 2 * seq
    hbm = pl.BlockSpec(memory_space=pl.ANY)
    vmem = pl.BlockSpec(memory_space=pltpu.VMEM)
    shapes = [layer.shape, tokens.shape, memory.shape] + [(share, width)] * 8
    shapes += [(share, feed), (feed // dp, width)] + [(share,)] * 6
    return pl.pallas_call(
        functools.partial(final_kernel, seq, dp),
        out_shape=[jax.ShapeDtypeStruct(shape, F32) for shape in shapes],
        in_specs=[hbm] * 3 + [vmem] + [hbm],
        out_specs=[hbm] * 13 + [vmem] * 6,
        scratch_shapes=[pltpu.VMEM(sums.shape, BF16)]
        + [pltpu.VMEM(shape, F32) for shape in shapes[:13]]
        + [pltpu.SemaphoreType.DMA((7,)), pltpu.SemaphoreType.DMA((13,))],
        compiler_params=pltpu.CompilerParams(vmem_limit_bytes=64 * 2**20 - 2**17),
    )(layer, tokens, memory, stats, sums)


def swap(value, axis, bit):
    size = lax.axis_size(axis)
    return lax.ppermute(value, axis, [(i, i ^ bit) for i in range(size)])


def scatter_sum(value, bits):
    index = lax.axis_index("dp")
    size = lax.axis_size("dp")
    levels = size.bit_length() - 1
    blocks = value.reshape((2,) * levels + value.shape[1:])
    left = list(range(levels))[::-1]
    for bit in bits:
        at = left.index(bit)
        mine = (index >> bit) & 1
        keep = lax.dynamic_index_in_dim(blocks, mine, at, keepdims=False)
        away = lax.dynamic_index_in_dim(blocks, 1 - mine, at, keepdims=False)
        left.pop(at)
        got = swap(away.astype(BF16), "dp", 1 << bit)
        blocks = keep.astype(F32) + got.astype(F32)
    return blocks


def shards(
    tokens,
    memory,
    target_segments,
    memory_segments,
    pad_counts,
    out_grad,
    self_query,
    self_key,
    self_value,
    self_out,
    cross_query,
    cross_key,
    cross_value,
    cross_out,
    feed_in,
    feed_out,
    gain_attend,
    shift_attend,
    gain_cross,
    shift_cross,
    gain_feed,
    shift_feed,
):
    seq, dp = lax.axis_size("seq"), lax.axis_size("dp")
    me = lax.axis_index("seq")
    span, width = tokens.shape[1:]
    part = width // seq
    feed = feed_in.shape[1]
    unit = feed // dp // seq
    direct = dp == 8 and unit == width // dp and unit % 16 == 0
    fi, fo = feed_in, feed_out
    if not direct:
        fi = lax.dynamic_index_in_dim(fi.reshape(width, dp, seq, unit), me, 2, keepdims=False)
        fi = fi.reshape(width, dp * unit)
        fo = lax.dynamic_index_in_dim(fo.reshape(dp, seq, unit, width), me, 1, keepdims=False)
        fo = fo.reshape(dp * unit, width)
    operands = (
        tokens[0], memory[0], out_grad[0], target_segments, memory_segments, pad_counts,
        self_query, self_key, self_value, self_out, cross_query, cross_key, cross_value, cross_out,
        fi, fo, gain_attend, shift_attend, gain_cross, shift_cross, gain_feed, shift_feed,
    )
    results = row_call(seq, span, memory.shape[1], width, part, dp * unit, direct, operands)
    if direct:
        results = final_call(seq, dp, *results)
        return tuple(value[None] for value in results[:3]) + tuple(results[3:])
    layer_out, tokens_grad, memory_grad, stats, g_fo, g_fi, g_cross, g_self = results
    gather = lambda v, axis: lax.all_gather(v, "seq", axis=axis, tiled=True)

    levels = dp.bit_length() - 1
    up = list(range(levels))
    first, second = up, up[1:] + up[:1]
    share = width // dp
    split = lambda v: v.reshape(dp, share, -1)
    groups = ((split(g_fo), first), (split(g_fi), second), (split(g_cross), first), (split(g_self), second))
    summed = [gather(scatter_sum(v, bits).astype(BF16)[None], 0) for v, bits in groups]
    whole_fo = summed[0].reshape(seq * share, width).astype(F32)
    whole_fi = (
        summed[1].reshape(seq, share, dp, unit).transpose(1, 2, 0, 3).reshape(share, feed)
    ).astype(F32)

    def whole(group, at):
        block = group[:, :, at * part : (at + 1) * part]
        block = block.reshape(2, 2, share, part).transpose(2, 1, 0, 3)
        return block.reshape(share, width).astype(F32)

    co, ck, cv, cq = (whole(summed[2], at) for at in range(4))
    so, sq, sk, sv = (whole(summed[3], at) for at in range(4))
    stats = lax.psum(stats, ("seq", "dp"))
    norm_part = lax.dynamic_slice_in_dim(stats, lax.axis_index("dp") * share, share, 1)
    return (
        layer_out[None],
        tokens_grad[None],
        memory_grad[None],
        sq,
        sk,
        sv,
        so,
        cq,
        ck,
        cv,
        co,
        whole_fi,
        whole_fo,
    ) + tuple(norm_part[i] for i in range(6))


def solution(mesh):
    rows = P("dp", "seq", None)
    in_specs = (rows, rows, P("dp", None), P("dp", None), P("dp", None), rows) + (P(),) * 16
    out_specs = (rows,) * 3 + (P("dp", None),) * 10 + (P("dp"),) * 6
    return jax.shard_map(shards, mesh=mesh, in_specs=in_specs, out_specs=out_specs, check_vma=False)
```
